32 devices in a mesh: rep: 2 (over y), fsdp: 16 (over z, x, core).
Axes of the slice: x: 2, y: 2, z: 4, core: 2. Of those that a mesh axis runs over, the one named last changes fastest.
Arguments:
- frames: bfloat16 [23552, 512], P(('rep', 'fsdp')), may hold values from -6 to 6
- memory_bank: bfloat16 [32, 4, 512], P(('rep', 'fsdp')), may hold values from -6 to 6
- cache_keys: bfloat16 [32, 30, 512], P(('rep', 'fsdp')), may hold values from -6 to 6
- cache_values: bfloat16 [32, 30, 512], P(('rep', 'fsdp')), may hold values from -6 to 6
- out_grad: bfloat16 [23552, 512], P(('rep', 'fsdp')), may hold values from -6 to 6
- first_gain: bfloat16 [512], P('fsdp'), may hold values from 0.5 to 1.5
- first_shift: bfloat16 [512], P('fsdp'), may hold values from -1.5 to 1.5
- query_weight: bfloat16 [512, 512], P('fsdp'), may hold values from -0.25 to 0.25
- query_bias: bfloat16 [512], P('fsdp'), may hold values from -1.5 to 1.5
- key_weight: bfloat16 [512, 512], P('fsdp'), may hold values from -0.25 to 0.25
- value_weight: bfloat16 [512, 512], P('fsdp'), may hold values from -0.25 to 0.25
- value_bias: bfloat16 [512], P('fsdp'), may hold values from -1.5 to 1.5
- memory_weight: bfloat16 [512, 1024], P('fsdp'), may hold values from -0.25 to 0.25
- output_weight: bfloat16 [512, 512], P(None, 'fsdp'), may hold values from -0.75 to 0.75
- output_bias: bfloat16 [512], P('fsdp'), may hold values from -1.5 to 1.5
- second_gain: bfloat16 [512], P('fsdp'), may hold values from 0.5 to 1.5
- second_shift: bfloat16 [512], P('fsdp'), may hold values from -1.5 to 1.5
- inner_weight: bfloat16 [512, 2048], P('fsdp'), may hold values from -0.25 to 0.25
- inner_bias: bfloat16 [2048], P('fsdp'), may hold values from -1.5 to 1.5
- outer_weight: bfloat16 [2048, 512], P(None, 'fsdp'), may hold values from -0.25 to 0.25
- outer_bias: bfloat16 [512], P('fsdp'), may hold values from -1.5 to 1.5
Outputs:
- activations: bfloat16 [23552, 512], P(('rep', 'fsdp'))
- frames_grad: float32 [23552, 512], P(('rep', 'fsdp'))
- memory_grad: float32 [32, 4, 512], P(('rep', 'fsdp'))
- cache_keys_grad: float32 [32, 30, 512], P(('rep', 'fsdp'))
- cache_values_grad: float32 [32, 30, 512], P(('rep', 'fsdp'))
- first_gain_grad: float32 [512], P('fsdp')
- first_shift_grad: float32 [512], P('fsdp')
- query_weight_grad: float32 [512, 512], P('fsdp')
- query_bias_grad: float32 [512], P('fsdp')
- key_weight_grad: float32 [512, 512], P('fsdp')
- value_weight_grad: float32 [512, 512], P('fsdp')
- value_bias_grad: float32 [512], P('fsdp')
- memory_weight_grad: float32 [512, 1024], P('fsdp')
- output_weight_grad: float32 [512, 512], P(None, 'fsdp')
- output_bias_grad: float32 [512], P('fsdp')
- second_gain_grad: float32 [512], P('fsdp')
- second_shift_grad: float32 [512], P('fsdp')
- inner_weight_grad: float32 [512, 2048], P('fsdp')
- inner_bias_grad: float32 [2048], P('fsdp')
- outer_weight_grad: float32 [2048, 512], P(None, 'fsdp')
- outer_bias_grad: float32 [512], P('fsdp')
The draws below stay inside these ranges and needn't reach their ends.
All inputs are finite; a program needn't handle non-finite values.
Results may differ from the reference program's by a relative error of at most 0.015.
Values may be sent and summed in bfloat16 or wider, within the bound.
No kernel may reach another device: no remote copies, remote signals or barrier semaphores. Data moves between devices by JAX's collectives and lax.ppermute only.
A program may use at most 128 MiB of HBM per device.

```python
import jax
import jax.numpy as jnp
from jax import lax

D = 512
HEADS = 8
HEAD_DIM = 64
FF = 2048
SEG = 16
RIGHT = 4
LEFT = 30
MEM = 4
BLOCK_LEN = 736
BLOCKS = 32
TOKENS = 23552


def spiked(drawn, key, source, target, parts, factor):
    def block_of(position):
        return (jnp.arange(drawn.shape[position]) // (drawn.shape[position] // parts)).reshape((-1,) + (1,) * (drawn.ndim - 1 - position))

    first = jax.random.permutation(key, parts)[block_of(target)]
    other_side = (block_of(target) + parts // 2) % parts
    return jnp.where((block_of(source) == first) | (block_of(source) == other_side), factor * drawn, drawn)


def shard_levels(stream_key, extent, cuts, least, top_value):
    def one(axis_at, parts):
        draws = jax.random.uniform(jax.random.fold_in(jax.random.fold_in(stream_key, 6), axis_at), (parts,), jnp.float32, least / len(cuts), top_value / len(cuts))
        return jnp.repeat(jnp.exp(draws), extent[axis_at] // parts).reshape((-1,) + (1,) * (len(extent) - axis_at - 1))

    factor_of = one(*cuts[0])
    for cut in cuts[1:]:
        factor_of = factor_of * one(*cut)
    return factor_of


def normal_values(rng, dims, scale, most, split=(), held_as=jnp.bfloat16):
    drawn = jax.random.normal(rng, dims, jnp.float32) * scale
    if len(split) > 0:
        drawn = shard_levels(rng, dims, split, -0.22, 0.18) * drawn
    return jnp.clip(drawn, min=-most, max=most).astype(held_as)


def bell_draw_with(key, extent, scale, most, split, heavy, held_as=jnp.bfloat16):
    values = scale * jax.random.normal(key, extent, jnp.float32)
    if split:
        values = values * shard_levels(key, extent, split, -0.22, 0.18)
    return jnp.clip(spiked(values, jax.random.fold_in(key, 3), *heavy), -most, most).astype(held_as)


def setup_inputs(seed: int = 0) -> dict:
    streams_of = jax.random.split(jax.random.key(seed), 22)
    frames = normal_values(streams_of[0], (TOKENS, D), 1.0, 6.0, ((0, 32),))
    memory_bank = normal_values(streams_of[1], (BLOCKS, MEM, D), 1.0, 6.0, ((0, 32),))
    cache_keys = normal_values(streams_of[2], (BLOCKS, LEFT, D), 1.0, 6.0, ((0, 32),))
    cache_values = normal_values(streams_of[3], (BLOCKS, LEFT, D), 1.0, 6.0, ((0, 32),))
    out_grad = bell_draw_with(streams_of[4], (TOKENS, D), 1.0, 6.0, ((0, 32),), (0, 1, 32, 2.75))
    first_gain = jnp.clip(1.0 + 0.1 * jax.random.normal(streams_of[5], (D,), jnp.float32), 0.5, 1.5).astype(jnp.bfloat16)
    first_shift = normal_values(streams_of[6], (D,), 0.3, 1.5, ((0, 16),))
    query_weight = normal_values(streams_of[7], (D, D), D ** -0.5, 0.25, ((0, 16),))
    query_bias = normal_values(streams_of[8], (D,), 0.3, 1.5, ((0, 16),))
    key_weight = normal_values(streams_of[9], (D, D), D ** -0.5, 0.25, ((0, 16),))
    value_weight = normal_values(streams_of[10], (D, D), D ** -0.5, 0.25, ((0, 16),))
    value_bias = normal_values(streams_of[11], (D,), 0.3, 1.5, ((0, 16),))
    memory_weight = normal_values(streams_of[12], (D, 2 * D), D ** -0.5, 0.25, ((0, 16),))
    output_weight = normal_values(streams_of[13], (D, D), (D // 8) ** -0.5, 0.75, ((1, 16),))
    output_bias = normal_values(streams_of[14], (D,), 0.3, 1.5, ((0, 16),))
    second_gain = jnp.clip(1.0 + 0.1 * jax.random.normal(streams_of[15], (D,), jnp.float32), 0.5, 1.5).astype(jnp.bfloat16)
    second_shift = normal_values(streams_of[16], (D,), 0.3, 1.5, ((0, 16),))
    inner_weight = normal_values(streams_of[17], (D, FF), D ** -0.5, 0.25, ((0, 16),))
    inner_bias = normal_values(streams_of[18], (FF,), 0.3, 1.5, ((0, 16),))
    outer_weight = normal_values(streams_of[19], (FF, D), (FF // 4) ** -0.5, 0.25, ((1, 16),))
    outer_bias = normal_values(streams_of[20], (D,), 0.3, 1.5, ((0, 16),))
    return dict(frames=frames, memory_bank=memory_bank, cache_keys=cache_keys, cache_values=cache_values, out_grad=out_grad, first_gain=first_gain, first_shift=first_shift, query_weight=query_weight, query_bias=query_bias, key_weight=key_weight, value_weight=value_weight, value_bias=value_bias, memory_weight=memory_weight, output_weight=output_weight, output_bias=output_bias, second_gain=second_gain, second_shift=second_shift, inner_weight=inner_weight, inner_bias=inner_bias, outer_weight=outer_weight, outer_bias=outer_bias)


@jax.custom_vjp
def low(v):
    return lax.optimization_barrier(v.astype(jnp.bfloat16)).astype(jnp.float32)

@jax.custom_vjp
def low_back(v):
    return v

def low_keep(v):
    return (low(v), None)

def low_pass(kept, grad):
    return (grad,)

def back_keep(v):
    return (v, None)

def back_low(kept, grad):
    return (low(grad),)
low.defvjp(low_keep, low_pass)
low_back.defvjp(back_keep, back_low)
exact_mode = lax.Precision.HIGHEST
masked_value = -1e+30
epsilon = 1e-05

def norm_rows(entries, gain_vector, shift_vector):
    center = entries - lax.optimization_barrier(jnp.mean(entries, axis=-1, keepdims=True))
    spread = lax.optimization_barrier(jnp.mean(center * center, axis=-1, keepdims=True))
    return center * lax.rsqrt(spread + epsilon) * gain_vector + shift_vector

def visible_keys(length):
    query_place = jnp.arange(length, dtype=jnp.int32)
    segment_start = query_place // SEG * SEG
    key_place = jnp.arange(MEM + LEFT + length, dtype=jnp.int32) - MEM - LEFT
    inside = (key_place[None, :] >= segment_start[:, None] - LEFT) & (key_place[None, :] < segment_start[:, None] + SEG + RIGHT)
    return inside | (key_place[None, :] < -LEFT)

def product(left_matrix, right_matrix):
    return jnp.dot(left_matrix, right_matrix, precision=exact_mode)

def layer(block_rows, bank_input, left_keys, left_values, weights):
    first_gain, first_shift, query_weight, query_bias, key_weight, value_weight, value_bias, memory_weight, output_weight, output_bias, second_gain, second_shift, inner_weight, inner_bias, outer_weight, outer_bias = weights
    scale_factor = HEAD_DIM ** (-0.5)
    normed = low(norm_rows(block_rows, first_gain, first_shift))
    queries = low_back(low(product(normed, query_weight) + query_bias))
    keys_new = low_back(low(product(normed, key_weight)))
    values_new = low_back(low(product(normed, value_weight) + value_bias))
    bank_rows = low_back(low(product(bank_input, memory_weight)))
    all_keys = jnp.concatenate([bank_rows[:, :D], left_keys, keys_new], axis=0)
    all_values = jnp.concatenate([bank_rows[:, D:], left_values, values_new], axis=0)
    query_heads = queries.reshape(BLOCK_LEN, HEADS, HEAD_DIM)
    key_heads = all_keys.reshape(-1, HEADS, HEAD_DIM)
    value_heads = all_values.reshape(-1, HEADS, HEAD_DIM)
    scores = low_back(jnp.einsum('qhd,khd->hqk', query_heads, key_heads, precision=exact_mode) * scale_factor)
    masked = jnp.where(visible_keys(BLOCK_LEN)[None], scores, masked_value)
    highest = lax.optimization_barrier(jnp.max(masked, axis=-1, keepdims=True))
    raised = jnp.exp(masked - highest)
    probabilities = low(raised / lax.optimization_barrier(jnp.sum(raised, axis=-1, keepdims=True)))
    context = jnp.einsum('hqk,khd->qhd', probabilities, value_heads, precision=exact_mode).reshape(BLOCK_LEN, D)
    context = low_back(low(context))
    residual = block_rows + low_back(product(context, output_weight) + output_bias)
    normed_second = low(norm_rows(residual, second_gain, second_shift))
    inner_sum = low_back(product(normed_second, inner_weight) + inner_bias)
    active = low(jax.nn.gelu(inner_sum))
    return residual + low_back(product(active, outer_weight) + outer_bias)

def reference(frames, memory_bank, cache_keys, cache_values, out_grad, first_gain, first_shift, query_weight, query_bias, key_weight, value_weight, value_bias, memory_weight, output_weight, output_bias, second_gain, second_shift, inner_weight, inner_bias, outer_weight, outer_bias):
    weights = tuple((member.astype(jnp.float32) for member in (first_gain, first_shift, query_weight, query_bias, key_weight, value_weight, value_bias, memory_weight, output_weight, output_bias, second_gain, second_shift, inner_weight, inner_bias, outer_weight, outer_bias)))
    block_count = frames.shape[0] // BLOCK_LEN
    inputs = (frames.astype(jnp.float32).reshape(block_count, BLOCK_LEN, D), memory_bank.astype(jnp.float32), cache_keys.astype(jnp.float32), cache_values.astype(jnp.float32), out_grad.astype(jnp.float32).reshape(block_count, BLOCK_LEN, D))

    def advance(totals, member):
        block_rows, bank_input, left_keys, left_values, cotangent = member
        output, pullback = jax.vjp(layer, block_rows, bank_input, left_keys, left_values, weights)
        grad_rows, grad_bank, grad_keys, grad_values, grad_weights = pullback(cotangent)
        totals = jax.tree.map(jnp.add, totals, grad_weights)
        return (totals, (output.astype(jnp.bfloat16), grad_rows, grad_bank, grad_keys, grad_values))
    initial = tuple((jnp.zeros_like(member) for member in weights))
    totals, (outputs, grad_frames, grad_memory, grad_left_keys, grad_left_values) = lax.scan(advance, initial, inputs)
    return (outputs.reshape(-1, D), grad_frames.reshape(-1, D), grad_memory, grad_left_keys, grad_left_values, totals[0], totals[1], totals[2], totals[3], totals[4], totals[5], totals[6], totals[7], totals[8], totals[9], totals[10], totals[11], totals[12], totals[13], totals[14], totals[15])
```

```python
import functools

import jax
import jax.numpy as jnp
from jax import lax
from jax.experimental import pallas as pl
from jax.experimental.pallas import tpu as pltpu
from jax.sharding import PartitionSpec as P

HEADS = 8
SEG = 16
RIGHT = 4
LEFT = 30
MEM = 4

LEAD = 32
GROUP = 64
SPAN = 112
KEYS = 128
QUAD = 4
masked_value = -1e30
epsilon = 1e-05
gelu_a = 0.7978845608028654
gelu_b = gelu_a * 0.044715

bf16 = jnp.bfloat16
f32 = jnp.float32
VMEM = pl.BlockSpec(memory_space=pltpu.VMEM)
ANY = pl.BlockSpec(memory_space=pl.ANY)


def dot(a, b):
    return lax.dot_general(a, b, (((1,), (0,)), ((), ())), preferred_element_type=f32)


def dot_nt(a, b):
    return lax.dot_general(a, b, (((1,), (1,)), ((), ())), preferred_element_type=f32)


def dot_tn(a, b):
    return lax.dot_general(a, b, (((0,), (0,)), ((), ())), preferred_element_type=f32)


def row_tiles(rows):
    return [(start, min(256, rows - start)) for start in range(0, rows, 256)]


def centred(v):
    center = v - jnp.mean(v, axis=-1, keepdims=True)
    spread = jnp.mean(center * center, axis=-1, keepdims=True)
    scale = lax.rsqrt(spread + epsilon)
    return center * scale, scale


def norm_back(e, n, scale, gain):
    eg = e * gain
    return scale * (
        eg - jnp.mean(eg, axis=-1, keepdims=True) - n * jnp.mean(eg * n, axis=-1, keepdims=True)
    )


def colsum(v):
    return jnp.sum(v, axis=0, keepdims=True)


RING = (0, 2, 4, 6, 7, 5, 3, 1)


def ring_pairs(step):
    pairs = []
    for k in range(8):
        for core in range(2):
            pairs.append((2 * RING[k] + core, 2 * RING[(k + step) % 8] + core))
    return pairs


TO_RIGHT, TO_LEFT = ring_pairs(1), ring_pairs(-1)
TO_CORE = [(i, i ^ 1) for i in range(16)]


def ring_ids():
    rank = lax.axis_index("fsdp")
    core, chip = lax.rem(rank, 2), lax.div(rank, 2)
    z, x = lax.div(chip, 2), lax.rem(chip, 2)
    return jnp.where(x == 0, z, 7 - z), core


def ring_rank(position, core):
    position = lax.rem(position, 8)
    return 2 * jnp.where(position < 4, 2 * position, 15 - 2 * position) + core


def halves(width):
    return width // 2 // 128 * 128


def chunk_plan(width):
    half = halves(width)
    plan = [(0, 0, width)]
    for s in (1, 2, 3):
        plan += [(8 - s, 0, width), (s, 0, width)]
    plan += [(4, 0, half), (4, half, width - half)]
    return [(d, 0, c, w) for d, c, w in plan] + [(d, 1, c, w) for d, c, w in plan]


def send(v, pairs):
    return lax.ppermute(v, "fsdp", pairs)


def ring_gather(shard):
    half = halves(shard.shape[1])
    got = [shard]
    a = b = shard
    for _ in range(3):
        a, b = send(a, TO_RIGHT), send(b, TO_LEFT)
        got += [a, b]
    got += [send(a[:, :half], TO_RIGHT), send(b[:, half:], TO_LEFT)]
    return got + [send(v, TO_CORE) for v in got]


def place_start(chunk_refs, plan, whole, sems):
    copies = []
    if plan is None:
        copies.append(pltpu.make_async_copy(chunk_refs[0], whole, sems.at[0]))
    else:
        position, core = ring_ids()
        for i, (distance, flip, column, width) in enumerate(plan):
            owner = ring_rank(position + distance, core if flip == 0 else 1 - core)
            rows = pl.ds(pl.multiple_of(owner * 32, 32), 32)
            copies.append(
                pltpu.make_async_copy(
                    chunk_refs[i], whole.at[rows, pl.ds(column, width)], sems.at[i]
                )
            )
    for copy in copies:
        copy.start()
    return copies


def spread_start(whole, mine, other, sems):
    position, core = ring_ids()
    copies = []
    for distance in range(8):
        for flip, target in ((0, mine), (1, other)):
            owner = ring_rank(position + distance, core if flip == 0 else 1 - core)
            rows = pl.ds(pl.multiple_of(owner * 32, 32), 32)
            copies.append(
                pltpu.make_async_copy(
                    whole.at[rows, :], target.at[distance], sems.at[2 * distance + flip]
                )
            )
    for copy in copies:
        copy.start()
    return copies


def wait_all(copies):
    for copy in copies:
        copy.wait()


def head_masks():
    lane = lax.broadcasted_iota(jnp.int32, (1, 64 * QUAD), 1)
    return [(lane // 64 == h).astype(f32) for h in range(QUAD)]


def stacked(rows, masks):
    return jnp.concatenate([rows * m for m in masks], axis=0)


def unstacked(wide, masks):
    parts = [wide[GROUP * h : GROUP * (h + 1)] * masks[h] for h in range(QUAD)]
    return parts[0] + parts[1] + parts[2] + parts[3]


def added_mask(limit):
    row = lax.broadcasted_iota(jnp.int32, (KEYS, GROUP * QUAD), 0)
    query = lax.rem(lax.broadcasted_iota(jnp.int32, (KEYS, GROUP * QUAD), 1), GROUP)
    first = query // SEG * SEG + (LEAD - LEFT)
    inside = (row >= first) & (row < first + LEFT + SEG + RIGHT) & (row < limit)
    bank = (row >= SPAN) & (row < SPAN + MEM)
    return jnp.where((inside & (row < SPAN)) | bank, 0.0, masked_value)


def attention_forward_kernel(n_chunks, plan, length, *refs):
    frames, bank, cache_k, cache_v, vec = refs[:5]
    chunks = refs[5 : 5 + n_chunks]
    (normed, q, kext, vext, kvmem, pt, ctx, vec_out, w, sems, mask) = refs[5 + n_chunks :]
    width = frames.shape[1]
    groups = q.shape[0] // GROUP
    copies = place_start(chunks, plan, w, sems)
    wait_all(copies)
    if plan is None:
        vectors = vec[...]
    else:
        blocks = w[:, 5 * width :].astype(f32).reshape(16, 32, 256)
        total = jnp.sum(blocks, axis=0)
        vectors = jnp.concatenate([total[:16], total[16:]], axis=1)
    vec_out[...] = vectors

    def left_rows(cache):
        rows = cache[0].astype(f32)
        return jnp.concatenate([jnp.zeros((LEAD - LEFT, width), f32), rows], axis=0).astype(bf16)

    kext[0:LEAD] = left_rows(cache_k)
    vext[0:LEAD] = left_rows(cache_v)
    tail = kext.shape[0] - LEAD - length
    kext[LEAD + length :] = jnp.zeros((tail, width), bf16)
    vext[LEAD + length :] = jnp.zeros((tail, width), bf16)
    q[length:] = jnp.zeros((q.shape[0] - length, width), bf16)
    bank_rows = jnp.concatenate(
        [bank[0].astype(f32), jnp.zeros((16 - MEM, width), f32)], axis=0
    ).astype(bf16)
    kvmem[...] = dot(bank_rows, w[:, 3 * width : 5 * width]).astype(bf16)

    for start, size in row_tiles(length):
        n, _ = centred(frames[start : start + size].astype(f32))
        rows = (n * vectors[0:1] + vectors[1:2]).astype(bf16)
        normed[start : start + size] = rows
        q[start : start + size] = (dot(rows, w[:, :width]) + vectors[2:3]).astype(bf16)
        kext[LEAD + start : LEAD + start + size] = dot(rows, w[:, width : 2 * width]).astype(bf16)
        vext[LEAD + start : LEAD + start + size] = (
            dot(rows, w[:, 2 * width : 3 * width]) + vectors[3:4]
        ).astype(bf16)

    masks = head_masks()
    scale = 64**-0.5
    q_masks = [(m * scale).astype(bf16) for m in masks]
    mask[0] = added_mask(KEYS)
    mask[1] = added_mask(LEAD + length - GROUP * (groups - 1))

    def step(g, carry):
        top = pl.multiple_of(g * GROUP, GROUP)
        hidden = mask[(g == groups - 1).astype(jnp.int32)]
        for j in range(HEADS // QUAD):
            lanes = slice(64 * QUAD * j, 64 * QUAD * (j + 1))
            keys = jnp.concatenate([kext[pl.ds(top, SPAN), lanes], kvmem[:, lanes]], axis=0)
            values = jnp.concatenate(
                [vext[pl.ds(top, SPAN), lanes], kvmem[:, width + lanes.start : width + lanes.stop]],
                axis=0,
            )
            queries = stacked(q[pl.ds(top, GROUP), lanes], q_masks)
            scores = dot_nt(keys, queries) + hidden
            raised = jnp.exp(scores - jnp.max(scores, axis=0, keepdims=True))
            weights = (raised / jnp.sum(raised, axis=0, keepdims=True)).astype(bf16)
            pt[g, j] = weights
            ctx[pl.ds(top, GROUP), lanes] = unstacked(dot_tn(weights, values), masks).astype(bf16)
        return carry

    lax.fori_loop(0, groups, step, 0)


def inner_kernel(n_chunks, plan, length, *refs):
    frames, ctx, vec, out_grad = refs[:4]
    chunks = refs[4 : 4 + n_chunks]
    residual, normed2, active, slope = refs[4 + n_chunks : 8 + n_chunks]
    n_out = 2 if plan is not None else 1
    outer_grads = refs[8 + n_chunks : 8 + n_chunks + n_out]
    w, grads, gt, sems, out_sems = refs[8 + n_chunks + n_out :]
    width = frames.shape[1]
    hidden = active.shape[1]
    wait_all(place_start(chunks, plan, w, sems))
    for start, size in row_tiles(length):
        rows = slice(start, start + size)
        res = frames[rows].astype(f32) + dot_nt(ctx[rows], w[:, :width]) + vec[4:5]
        residual[rows] = res
        n, _ = centred(res)
        normed2[rows] = (n * vec[5:6] + vec[6:7]).astype(bf16)
        gt[:, rows] = out_grad[rows].T

    block = 512

    def step(b, carry):
        at = pl.multiple_of(b * block, block)
        bias = vec[pl.ds(8 + b, 1), :]
        for start, size in row_tiles(length):
            rows = slice(start, start + size)
            u = dot(normed2[rows], w[:, pl.ds(width + at, block)]) + bias
            uu = u * u
            h = 0.5 + 0.5 * jnp.tanh(u * (gelu_a + gelu_b * uu))
            act = u * h
            active[rows, pl.ds(at, block)] = act.astype(bf16)
            slope[rows, pl.ds(at, block)] = (
                h + act * (1.0 - h) * (2 * gelu_a + 6 * gelu_b * uu)
            ).astype(bf16)
        grads[:, pl.ds(at, block)] = dot(gt[...], active[:, pl.ds(at, block)]).astype(bf16)
        return carry

    lax.fori_loop(0, hidden // block, step, 0)
    if plan is not None:
        wait_all(spread_start(grads, *outer_grads, out_sems))
    else:
        outer_grads[0][...] = grads[...]


def upper_kernel(n_chunks, n_inner, plan, inner_plan, length, *refs):
    residual, normed2, active, slope, ctx, out_grad, vec = refs[:7]
    chunks = refs[7 : 7 + n_chunks]
    inner_chunks = refs[7 + n_chunks : 7 + n_chunks + n_inner]
    rest = refs[7 + n_chunks + n_inner :]
    output, grad_res, grad_ctx, vec_grads = rest[:4]
    n_out = 2 if plan is not None else 1
    inner_grads = rest[4 : 4 + n_out]
    w2, w, gi, n2t, gat, grads, acc, sems, inner_sems, out_sems = rest[4 + n_out :]
    width = residual.shape[1]
    hidden = active.shape[1]
    copies = place_start(chunks, plan, w2, sems)
    more = place_start(inner_chunks, inner_plan, w, inner_sems)
    wait_all(copies)
    wait_all(more)
    block = 512

    def step(b, carry):
        at = pl.multiple_of(b * block, block)
        sums = jnp.zeros((1, block), f32)
        for start, size in row_tiles(length):
            rows = slice(start, start + size)
            up = dot(out_grad[rows], w2[:, pl.ds(at, block)])
            part = (up * slope[rows, pl.ds(at, block)].astype(f32)).astype(bf16)
            gi[rows, pl.ds(at, block)] = part
            sums += colsum(part.astype(f32))
        vec_grads[pl.ds(8 + b, 1), :] = sums
        return carry

    lax.fori_loop(0, hidden // block, step, 0)
    vec_grads[0:8] = jnp.zeros((8, width), f32)
    vec_grads[12:16] = jnp.zeros((4, width), f32)
    sums = [jnp.zeros((1, width), f32) for _ in range(4)]
    for start, size in row_tiles(length):
        rows = slice(start, start + size)
        res = residual[rows]
        cot = out_grad[rows].astype(f32)
        output[rows] = (res + dot_nt(active[rows], w2[...]) + vec[7:8]).astype(bf16)
        e = dot_nt(gi[rows], w[:, width:])
        n, scale = centred(res)
        gres = cot + norm_back(e, n, scale, vec[5:6])
        grad_res[rows] = gres
        gat_rows = gres.astype(bf16)
        gat[:, rows] = gat_rows.T
        n2t[:, rows] = normed2[rows].T
        grad_ctx[rows] = dot(gat_rows, w[:, :width]).astype(bf16)
        sums = [
            s + colsum(v)
            for s, v in zip(sums, (gat_rows.astype(f32), e * n, e, cot))
        ]
    grad_ctx[length:] = jnp.zeros((grad_ctx.shape[0] - length, width), bf16)
    for i in range(4):
        vec_grads[4 + i : 5 + i] = sums[i]
    grads[:, :width] = dot(gat[...], ctx[:length]).astype(bf16)

    def weight_step(b, carry):
        at = pl.multiple_of(b * block, block)
        grads[:, pl.ds(width + at, block)] = dot(n2t[...], gi[:, pl.ds(at, block)]).astype(bf16)
        return carry

    lax.fori_loop(0, hidden // block, weight_step, 0)
    if plan is not None:
        wait_all(spread_start(grads, *inner_grads, out_sems))
    else:
        inner_grads[0][...] = grads[...]


def lower_kernel(n_chunks, plan, length, *refs):
    frames, normed, bank, q, kext, vext, kvmem, pt, grad_ctx, grad_res, vec, vec_grads = refs[:12]
    chunks = refs[12 : 12 + n_chunks]
    rest = refs[12 + n_chunks :]
    grad_frames, grad_bank, grad_ck, grad_cv = rest[:4]
    n_out = 2 if plan is not None else 2
    outs = rest[4 : 4 + n_out]
    w, gk, gv, gkm, gq, nt, grads, sems, out_sems = rest[4 + n_out :]
    width = frames.shape[1]
    groups = q.shape[0] // GROUP
    copies = place_start(chunks, plan, w, sems)
    gk[...] = jnp.zeros(gk.shape, f32)
    gv[...] = jnp.zeros(gv.shape, f32)
    gkm[...] = jnp.zeros(gkm.shape, f32)
    masks = head_masks()
    scale = 64**-0.5
    q_masks = [(m * scale).astype(bf16) for m in masks]
    c_masks = [m.astype(bf16) for m in masks]
    out_masks = [m * scale for m in masks]

    def step(g, carry):
        top = pl.multiple_of(g * GROUP, GROUP)
        for j in range(HEADS // QUAD):
            lanes = slice(64 * QUAD * j, 64 * QUAD * (j + 1))
            value_lanes = slice(width + lanes.start, width + lanes.stop)
            keys = jnp.concatenate([kext[pl.ds(top, SPAN), lanes], kvmem[:, lanes]], axis=0)
            values = jnp.concatenate([vext[pl.ds(top, SPAN), lanes], kvmem[:, value_lanes]], axis=0)
            queries = stacked(q[pl.ds(top, GROUP), lanes], q_masks)
            upstream = stacked(grad_ctx[pl.ds(top, GROUP), lanes], c_masks)
            weights = pt[g, j]
            wide = weights.astype(f32)
            gp = dot_nt(values, upstream)
            gs = (wide * (gp - colsum(gp * wide))).astype(bf16)
            gkeys = dot(gs, queries)
            gvalues = dot(weights, upstream)
            gk[pl.ds(top, SPAN), lanes] += gkeys[:SPAN]
            gv[pl.ds(top, SPAN), lanes] += gvalues[:SPAN]
            gkm[:, lanes] += gkeys[SPAN:]
            gkm[:, value_lanes] += gvalues[SPAN:]
            gq[pl.ds(top, GROUP), lanes] = unstacked(dot_tn(gs, keys), out_masks).astype(bf16)
        return carry

    lax.fori_loop(0, groups, step, 0)
    grad_ck[0] = gk[LEAD - LEFT : LEAD]
    grad_cv[0] = gv[LEAD - LEFT : LEAD]
    wait_all(copies)
    bank_grads = gkm[...].astype(bf16)
    grad_bank[0] = dot_nt(bank_grads, w[:, 3 * width : 5 * width])[:MEM]
    bank_rows = jnp.concatenate(
        [bank[0].astype(f32), jnp.zeros((16 - MEM, width), f32)], axis=0
    ).astype(bf16)
    grads[:, 3 * width : 5 * width] = dot_tn(bank_rows, bank_grads).astype(bf16)
    sums = [jnp.zeros((1, width), f32) for _ in range(4)]
    gains = vec[0:1]
    for start, size in row_tiles(length):
        rows = slice(start, start + size)
        nt[:, rows] = normed[rows].T
        gq_rows = gq[rows]
        gk_rows = gk[LEAD + start : LEAD + start + size].astype(bf16)
        gv_rows = gv[LEAD + start : LEAD + start + size].astype(bf16)
        e = (
            dot_nt(gq_rows, w[:, :width])
            + dot_nt(gk_rows, w[:, width : 2 * width])
            + dot_nt(gv_rows, w[:, 2 * width : 3 * width])
        )
        n, s = centred(frames[rows].astype(f32))
        grad_frames[rows] = grad_res[rows] + norm_back(e, n, s, gains)
        sums = [
            t + colsum(v)
            for t, v in zip(sums, (e * n, e, gq_rows.astype(f32), gv_rows.astype(f32)))
        ]
    turned = nt[...]
    grads[:, :width] = dot(turned, gq[:length]).astype(bf16)
    grads[:, width : 2 * width] = dot(turned, gk[LEAD : LEAD + length].astype(bf16)).astype(bf16)
    grads[:, 2 * width : 3 * width] = dot(turned, gv[LEAD : LEAD + length].astype(bf16)).astype(
        bf16
    )
    vectors = jnp.concatenate(sums + [vec_grads[4:16]], axis=0)
    if plan is not None:
        block = jnp.concatenate([vectors[:, :256], vectors[:, 256:]], axis=0).astype(bf16)
        grads[:, 5 * width :] = jnp.concatenate([block] * 16, axis=0)
        wait_all(spread_start(grads, *outs, out_sems))
    else:
        outs[0][...] = grads[...]
        outs[1][...] = vectors


def call(kernel, out_shapes, out_specs, scratch, args, specs, flops, moved, limit=50):
    return pl.pallas_call(
        kernel,
        out_shape=out_shapes,
        in_specs=specs,
        out_specs=out_specs,
        scratch_shapes=scratch,
        compiler_params=pltpu.CompilerParams(vmem_limit_bytes=limit * 1024 * 1024),
        cost_estimate=pl.CostEstimate(flops=flops, bytes_accessed=moved, transcendentals=0),
    )(*args)


def shape(dims, dtype):
    return jax.ShapeDtypeStruct(dims, dtype)


def pack_vectors(vectors, inner_bias, width, ranks):
    rank = lax.axis_index("fsdp")
    owner = jnp.arange(width) // (width // ranks)
    rows = jnp.where(owner == rank, jnp.tile(jnp.stack(vectors), (1, ranks)), 0)
    hidden = inner_bias.shape[0] * ranks
    owner = jnp.arange(hidden) // inner_bias.shape[0]
    inner = jnp.where(owner == rank, jnp.tile(inner_bias, ranks), 0).reshape(-1, width)
    return jnp.concatenate([rows, inner, jnp.zeros((4, width), bf16)], axis=0)


def ring_reduce(mine, other):
    summed = (mine.astype(f32) + send(other, TO_CORE).astype(f32)).astype(bf16)
    width = summed.shape[2]
    half = halves(width)
    a, b = send(summed[4][:, :half], TO_RIGHT), send(summed[4][:, half:], TO_LEFT)
    zeros_a = jnp.zeros((32, width - half), bf16)
    zeros_b = jnp.zeros((32, half), bf16)
    a, b = jnp.concatenate([a, zeros_a], 1), jnp.concatenate([zeros_b, b], 1)
    for s in (3, 2, 1):
        right = (summed[s].astype(f32) + a.astype(f32)).astype(bf16)
        left = (summed[8 - s].astype(f32) + b.astype(f32)).astype(bf16)
        a, b = send(right, TO_RIGHT), send(left, TO_LEFT)
    total = (summed[0].astype(f32) + a.astype(f32) + b.astype(f32)).astype(bf16)
    return total.astype(f32) + lax.ppermute(total, "rep", [(0, 1), (1, 0)]).astype(f32)


def per_device(ring, *args):
    (
        frames,
        memory_bank,
        cache_keys,
        cache_values,
        out_grad,
        first_gain,
        first_shift,
        query_weight,
        query_bias,
        key_weight,
        value_weight,
        value_bias,
        memory_weight,
        output_weight,
        output_bias,
        second_gain,
        second_shift,
        inner_weight,
        inner_bias,
        outer_weight,
        outer_bias,
    ) = args
    length, width = frames.shape
    ranks = width // first_gain.shape[0]
    hidden = inner_bias.shape[0] * ranks
    groups = -(-length // GROUP)
    padded = groups * GROUP
    extended = (groups - 1) * GROUP + SPAN
    packed = pack_vectors(
        [
            first_gain,
            first_shift,
            query_bias,
            value_bias,
            output_bias,
            second_gain,
            second_shift,
            outer_bias,
        ],
        inner_bias,
        width,
        ranks,
    )
    first = [query_weight, key_weight, value_weight, memory_weight]
    second = [output_weight.T, inner_weight]
    third = outer_weight.T
    if ring:
        block = jnp.concatenate([packed[:, : width // 2], packed[:, width // 2 :]], axis=0)
        first = jnp.concatenate(first + [block], axis=1)
        second = jnp.concatenate(second, axis=1)
        plans = [chunk_plan(v.shape[1]) for v in (first, second, third)]
        gathered = [ring_gather(v) for v in (first, second, third)]
        vec = jnp.zeros((16, width), f32)
    else:
        first = jnp.concatenate(first, axis=1)
        second = jnp.concatenate(second, axis=1)
        plans = [None] * 3
        gathered = [
            [lax.all_gather(v, "fsdp", axis=0, tiled=True)] for v in (first, second, third)
        ]
        vec = lax.psum(packed.astype(f32), "fsdp")
    widths = [first.shape[1], second.shape[1], third.shape[1]]
    counts = [len(v) for v in gathered]

    dma = pltpu.SemaphoreType.DMA
    normed, q, kext, vext, kvmem, pt, ctx, vec = call(
        functools.partial(attention_forward_kernel, counts[0], plans[0], length),
        (
            shape((length, width), bf16),
            shape((padded, width), bf16),
            shape((extended, width), bf16),
            shape((extended, width), bf16),
            shape((16, 2 * width), bf16),
            shape((groups, HEADS // QUAD, KEYS, GROUP * QUAD), bf16),
            shape((padded, width), bf16),
            shape((16, width), f32),
        ),
        [VMEM] * 8,
        [
            pltpu.VMEM((width, widths[0]), bf16),
            dma((counts[0],)),
            pltpu.VMEM((2, KEYS, GROUP * QUAD), f32),
        ],
        [frames, memory_bank, cache_keys, cache_values, vec, *gathered[0]],
        [VMEM] * 5 + [ANY] * counts[0],
        6 * length * width * width,
        8 * 2**20,
    )
    grad_shapes = (
        lambda w: (shape((8, 32, w), bf16), shape((8, 32, w), bf16))
        if ring
        else (shape((width, w), bf16),)
    )
    grad_specs = [ANY] * 2 if ring else [VMEM]
    residual, normed2, active, slope, *outer_grads = call(
        functools.partial(inner_kernel, counts[1], plans[1], length),
        (
            shape((length, width), f32),
            shape((length, width), bf16),
            shape((length, hidden), bf16),
            shape((length, hidden), bf16),
            *grad_shapes(widths[2]),
        ),
        [VMEM] * 4 + grad_specs,
        [
            pltpu.VMEM((width, widths[1]), bf16),
            pltpu.VMEM((width, hidden), bf16),
            pltpu.VMEM((width, length), bf16),
            dma((counts[1],)),
            dma((16,)),
        ],
        [frames, ctx, vec, out_grad, *gathered[1]],
        [VMEM] * 4 + [ANY] * counts[1],
        4 * length * width * hidden,
        12 * 2**20,
    )
    output, grad_res, grad_ctx, vec_grads, *inner_grads = call(
        functools.partial(upper_kernel, counts[2], counts[1], plans[2], plans[1], length),
        (
            shape((length, width), bf16),
            shape((length, width), f32),
            shape((padded, width), bf16),
            shape((16, width), f32),
            *grad_shapes(widths[1]),
        ),
        [VMEM] * 4 + grad_specs,
        [
            pltpu.VMEM((width, widths[2]), bf16),
            pltpu.VMEM((width, widths[1]), bf16),
            pltpu.VMEM((length, hidden), bf16),
            pltpu.VMEM((width, length), bf16),
            pltpu.VMEM((width, length), bf16),
            pltpu.VMEM((width, widths[1]), bf16),
            pltpu.VMEM((8, 128), f32),
            dma((counts[2],)),
            dma((counts[1],)),
            dma((16,)),
        ],
        [residual, normed2, active, slope, ctx, out_grad, vec, *gathered[2], *gathered[1]],
        [VMEM] * 7 + [ANY] * (counts[2] + counts[1]),
        8 * length * width * hidden,
        20 * 2**20,
    )
    lower_outs = (
        grad_shapes(widths[0])
        if ring
        else (shape((width, widths[0]), bf16), shape((16, width), f32))
    )
    grad_frames, grad_bank, grad_ck, grad_cv, *lower_grads = call(
        functools.partial(lower_kernel, counts[0], plans[0], length),
        (
            shape((length, width), f32),
            shape((1, MEM, width), f32),
            shape((1, LEFT, width), f32),
            shape((1, LEFT, width), f32),
            *lower_outs,
        ),
        [VMEM] * 4 + ([ANY] * 2 if ring else [VMEM] * 2),
        [
            pltpu.VMEM((width, widths[0]), bf16),
            pltpu.VMEM((extended, width), f32),
            pltpu.VMEM((extended, width), f32),
            pltpu.VMEM((16, 2 * width), f32),
            pltpu.VMEM((padded, width), bf16),
            pltpu.VMEM((width, length), bf16),
            pltpu.VMEM((width, widths[0]), bf16),
            dma((counts[0],)),
            dma((16,)),
        ],
        [
            frames,
            normed,
            memory_bank,
            q,
            kext,
            vext,
            kvmem,
            pt,
            grad_ctx,
            grad_res,
            vec,
            vec_grads,
            *gathered[0],
        ],
        [VMEM] * 12 + [ANY] * counts[0],
        12 * length * width * width,
        20 * 2**20,
    )
    if ring:
        outer_sum = ring_reduce(*outer_grads)
        inner_sum = ring_reduce(*inner_grads)
        lower_sum = ring_reduce(*lower_grads)
        tail = lower_sum[:, 5 * width :]
        vec_sum = jnp.concatenate([tail[:16], tail[16:]], axis=1)
    else:

        def reduce(v):
            part = lax.psum_scatter(v, "fsdp", scatter_dimension=0, tiled=True)
            return lax.psum(part, "rep").astype(f32)

        outer_sum = reduce(outer_grads[0])
        inner_sum = reduce(inner_grads[0])
        lower_sum = reduce(lower_grads[0])
        vec_sum = lax.psum(lower_grads[1], ("rep", "fsdp"))
    rank = lax.axis_index("fsdp")
    part = width // ranks
    own = lax.dynamic_slice(vec_sum[:8], (0, rank * part), (8, part))
    inner_part = inner_bias.shape[0]
    own_inner = lax.dynamic_slice(vec_sum[8:12].reshape(-1), (rank * inner_part,), (inner_part,))
    return (
        output,
        grad_frames,
        grad_bank,
        grad_ck,
        grad_cv,
        own[0],
        own[1],
        lower_sum[:, :width],
        own[2],
        lower_sum[:, width : 2 * width],
        lower_sum[:, 2 * width : 3 * width],
        own[3],
        lower_sum[:, 3 * width : 5 * width],
        inner_sum[:, :width].T,
        own[4],
        own[5],
        own[6],
        inner_sum[:, width:],
        own_inner,
        outer_sum.T,
        own[7],
    )


def solution(mesh):
    both = ("rep", "fsdp")
    rows, vector = P("fsdp", None), P("fsdp")
    columns = P(None, "fsdp")
    weights = (
        vector,
        vector,
        rows,
        vector,
        rows,
        rows,
        vector,
        rows,
        columns,
        vector,
        vector,
        vector,
        rows,
        vector,
        columns,
        vector,
    )
    blocks = P(both, None, None)
    in_specs = (P(both, None), blocks, blocks, blocks, P(both, None), *weights)
    out_specs = (P(both, None), P(both, None), blocks, blocks, blocks, *weights)
    ring = mesh.shape["fsdp"] == 16 and mesh.shape["rep"] == 2
    return jax.shard_map(
        functools.partial(per_device, ring),
        mesh=mesh,
        in_specs=in_specs,
        out_specs=out_specs,
        check_vma=False,
    )
```

```python
import functools

import jax
import jax.numpy as jnp
from jax import lax
from jax.experimental import pallas as pl
from jax.experimental.pallas import tpu as pltpu
from jax.sharding import PartitionSpec as P

HEADS = 8
SEG = 16
RIGHT = 4
LEFT = 30
MEM = 4

LEAD = 32
GROUP = 64
SPAN = 112
KEYS = 128
QUAD = 4
masked_value = -1e30
epsilon = 1e-05
gelu_a = 0.7978845608028654
gelu_b = gelu_a * 0.044715

bf16 = jnp.bfloat16
f32 = jnp.float32
VMEM = pl.BlockSpec(memory_space=pltpu.VMEM)
ANY = pl.BlockSpec(memory_space=pl.ANY)
HBM = pl.BlockSpec(memory_space=pltpu.HBM)


def dot(a, b):
    return lax.dot_general(a, b, (((1,), (0,)), ((), ())), preferred_element_type=f32)


def dot_nt(a, b):
    return lax.dot_general(a, b, (((1,), (1,)), ((), ())), preferred_element_type=f32)


def dot_tn(a, b):
    return lax.dot_general(a, b, (((0,), (0,)), ((), ())), preferred_element_type=f32)


def row_tiles(rows):
    return [(start, min(256, rows - start)) for start in range(0, rows, 256)]


def centred(v):
    center = v - jnp.mean(v, axis=-1, keepdims=True)
    spread = jnp.mean(center * center, axis=-1, keepdims=True)
    scale = lax.rsqrt(spread + epsilon)
    return center * scale, scale


def norm_back(e, n, scale, gain):
    eg = e * gain
    return scale * (
        eg - jnp.mean(eg, axis=-1, keepdims=True) - n * jnp.mean(eg * n, axis=-1, keepdims=True)
    )


def colsum(v):
    return jnp.sum(v, axis=0, keepdims=True)


RING = (0, 2, 4, 6, 7, 5, 3, 1)


def ring_pairs(step):
    pairs = []
    for k in range(8):
        for core in range(2):
            pairs.append((2 * RING[k] + core, 2 * RING[(k + step) % 8] + core))
    return pairs


TO_RIGHT, TO_LEFT = ring_pairs(1), ring_pairs(-1)
TO_CORE = [(i, i ^ 1) for i in range(16)]


def ring_ids():
    rank = lax.axis_index("fsdp")
    core, chip = lax.rem(rank, 2), lax.div(rank, 2)
    z, x = lax.div(chip, 2), lax.rem(chip, 2)
    return jnp.where(x == 0, z, 7 - z), core


def ring_rank(position, core):
    position = lax.rem(position, 8)
    return 2 * jnp.where(position < 4, 2 * position, 15 - 2 * position) + core


def halves(width):
    return width // 2 // 128 * 128


def chunk_plan(width):
    half = halves(width)
    plan = [(0, 0, width)]
    for s in (1, 2, 3):
        plan += [(8 - s, 0, width), (s, 0, width)]
    plan += [(4, 0, half), (4, half, width - half)]
    return [(d, 0, c, w) for d, c, w in plan] + [(d, 1, c, w) for d, c, w in plan]


def send(v, pairs):
    return lax.ppermute(v, "fsdp", pairs)


def ring_gather(shard):
    half = halves(shard.shape[1])
    got = [shard]
    a = b = shard
    for _ in range(3):
        a, b = send(a, TO_RIGHT), send(b, TO_LEFT)
        got += [a, b]
    got += [send(a[:, :half], TO_RIGHT), send(b[:, half:], TO_LEFT)]
    return got + [send(v, TO_CORE) for v in got]


def place(chunks, plan, whole, first=0):
    last = first + whole.shape[1]
    if plan is None:
        whole[...] = chunks[0][:, first:last]
        return
    position, core = ring_ids()
    for ref, (distance, flip, column, width) in zip(chunks, plan):
        owner = ring_rank(position + distance, core if flip == 0 else 1 - core)
        rows = pl.ds(pl.multiple_of(owner * 32, 32), 32)
        start, stop = max(first, column), min(last, column + width)
        if start < stop:
            whole[rows, start - first : stop - first] = ref[:, start - column : stop - column]


def spread(plan, grads, outs):
    if plan is None:
        outs[0][...] = grads[...]
        return
    position, core = ring_ids()
    for distance in range(8):
        for flip, out in enumerate(outs):
            owner = ring_rank(position + distance, core if flip == 0 else 1 - core)
            out[distance] = grads[pl.ds(pl.multiple_of(owner * 32, 32), 32), :]


def start_all(pairs, sems, first=0):
    copies = [pltpu.make_async_copy(a, b, sems.at[first + i]) for i, (a, b) in enumerate(pairs)]
    for copy in copies:
        copy.start()
    return copies


def wait_all(copies):
    for copy in copies:
        copy.wait()


def head_masks():
    lane = lax.broadcasted_iota(jnp.int32, (1, 64 * QUAD), 1)
    return [(lane // 64 == h).astype(f32) for h in range(QUAD)]


def stacked(rows, masks):
    return jnp.concatenate([rows * m for m in masks], axis=0)


def unstacked(wide, masks):
    parts = [wide[GROUP * h : GROUP * (h + 1)] * masks[h] for h in range(QUAD)]
    return parts[0] + parts[1] + parts[2] + parts[3]


def added_mask(limit):
    row = lax.broadcasted_iota(jnp.int32, (KEYS, GROUP * QUAD), 0)
    query = lax.rem(lax.broadcasted_iota(jnp.int32, (KEYS, GROUP * QUAD), 1), GROUP)
    first = query // SEG * SEG + (LEAD - LEFT)
    inside = (row >= first) & (row < first + LEFT + SEG + RIGHT) & (row < limit)
    bank = (row >= SPAN) & (row < SPAN + MEM)
    return jnp.where((inside & (row < SPAN)) | bank, 0.0, masked_value)


def attention_forward_kernel(n_chunks, plan, length, *refs):
    frames, bank, cache_k, cache_v, vec = refs[:5]
    chunks = refs[5 : 5 + n_chunks]
    stored, (ctx, vec_out) = refs[5 + n_chunks : 11 + n_chunks], refs[11 + n_chunks : 13 + n_chunks]
    normed, q, kext, vext, kvmem, pt, w, mask, sems = refs[13 + n_chunks :]
    width = frames.shape[1]
    groups = q.shape[0] // GROUP
    place(chunks, plan, w)
    if plan is None:
        vectors = vec[...]
    else:
        blocks = w[:, 5 * width :].astype(f32).reshape(16, 32, 256)
        total = jnp.sum(blocks, axis=0)
        vectors = jnp.concatenate([total[:16], total[16:]], axis=1)
    vec_out[...] = vectors

    def left_rows(cache):
        rows = cache[0].astype(f32)
        return jnp.concatenate([jnp.zeros((LEAD - LEFT, width), f32), rows], axis=0).astype(bf16)

    kext[0:LEAD] = left_rows(cache_k)
    vext[0:LEAD] = left_rows(cache_v)
    tail = kext.shape[0] - LEAD - length
    kext[LEAD + length :] = jnp.zeros((tail, width), bf16)
    vext[LEAD + length :] = jnp.zeros((tail, width), bf16)
    q[length:] = jnp.zeros((q.shape[0] - length, width), bf16)
    bank_rows = jnp.concatenate(
        [bank[0].astype(f32), jnp.zeros((16 - MEM, width), f32)], axis=0
    ).astype(bf16)
    kvmem[...] = dot(bank_rows, w[:, 3 * width : 5 * width]).astype(bf16)

    for start, size in row_tiles(length):
        n, _ = centred(frames[start : start + size].astype(f32))
        rows = (n * vectors[0:1] + vectors[1:2]).astype(bf16)
        normed[start : start + size] = rows
        q[start : start + size] = (dot(rows, w[:, :width]) + vectors[2:3]).astype(bf16)
        kext[LEAD + start : LEAD + start + size] = dot(rows, w[:, width : 2 * width]).astype(bf16)
        vext[LEAD + start : LEAD + start + size] = (
            dot(rows, w[:, 2 * width : 3 * width]) + vectors[3:4]
        ).astype(bf16)

    copies = start_all(zip((normed, q, kext, vext, kvmem), stored), sems)
    masks = head_masks()
    scale = 64**-0.5
    q_masks = [(m * scale).astype(bf16) for m in masks]
    mask[0] = added_mask(KEYS)
    mask[1] = added_mask(LEAD + length - GROUP * (groups - 1))

    def step(g, carry):
        top = pl.multiple_of(g * GROUP, GROUP)
        hidden = mask[(g == groups - 1).astype(jnp.int32)]
        for j in range(HEADS // QUAD):
            lanes = slice(64 * QUAD * j, 64 * QUAD * (j + 1))
            keys = jnp.concatenate([kext[pl.ds(top, SPAN), lanes], kvmem[:, lanes]], axis=0)
            values = jnp.concatenate(
                [vext[pl.ds(top, SPAN), lanes], kvmem[:, width + lanes.start : width + lanes.stop]],
                axis=0,
            )
            queries = stacked(q[pl.ds(top, GROUP), lanes], q_masks)
            scores = dot_nt(keys, queries) + hidden
            raised = jnp.exp(scores - jnp.max(scores, axis=0, keepdims=True))
            weights = (raised / jnp.sum(raised, axis=0, keepdims=True)).astype(bf16)
            pt[g, j] = weights
            ctx[pl.ds(top, GROUP), lanes] = unstacked(dot_tn(weights, values), masks).astype(bf16)
        return carry

    lax.fori_loop(0, groups, step, 0, unroll=6)
    wait_all(copies + start_all([(pt, stored[5])], sems, 5))


def inner_kernel(n_chunks, plan, length, *refs):
    frames, ctx, vec = refs[:3]
    chunks = refs[3 : 3 + n_chunks]
    residual, normed2, active_out, slope, w, active, sems = refs[3 + n_chunks :]
    width = frames.shape[1]
    hidden = active.shape[1]
    place(chunks, plan, w, second_column(width, plan))
    for start, size in row_tiles(length):
        rows = slice(start, start + size)
        res = frames[rows].astype(f32) + dot_nt(ctx[rows], w[:, :width]) + vec[4:5]
        residual[rows] = res
        n, _ = centred(res)
        normed2[rows] = (n * vec[5:6] + vec[6:7]).astype(bf16)

    block = 512
    copies = []
    for b in range(hidden // block):
        cols = slice(b * block, (b + 1) * block)
        for start, size in row_tiles(length):
            rows = slice(start, start + size)
            u = dot(normed2[rows], w[:, width + cols.start : width + cols.stop]) + vec[8 + b : 9 + b]
            uu = u * u
            h = 0.5 + 0.5 * jnp.tanh(u * (gelu_a + gelu_b * uu))
            act = u * h
            active[rows, cols] = act.astype(bf16)
            slope[rows, cols] = (
                h + act * (1.0 - h) * (2 * gelu_a + 6 * gelu_b * uu)
            ).astype(bf16)
        part = pl.ds(b * block, block)
        copies += start_all([(active.at[:, part], active_out.at[:, part])], sems, b)
    wait_all(copies)


def second_column(width, plan):
    return 5 * width + (0 if plan is None else 256)


def third_column(width, hidden, plan):
    return second_column(width, plan) + width + hidden


def grad_inner_kernel(n_chunks, plan, length, *refs):
    out_grad, slope = refs[:2]
    chunks = refs[2 : 2 + n_chunks]
    gi, vec_grads, w = refs[2 + n_chunks :]
    width, hidden = out_grad.shape[1], slope.shape[1]
    place(chunks, plan, w, third_column(width, hidden, plan))
    block = 512
    vec_grads[...] = jnp.zeros(vec_grads.shape, f32)
    for b in range(hidden // block):
        cols = slice(b * block, (b + 1) * block)
        sums = jnp.zeros((1, block), f32)
        for start, size in row_tiles(length):
            rows = slice(start, start + size)
            up = dot(out_grad[rows], w[:, cols])
            part = (up * slope[rows, cols].astype(f32)).astype(bf16)
            gi[rows, cols] = part
            sums += colsum(part.astype(f32))
        vec_grads[8 + b : 9 + b] = sums
    vec_grads[7:8] = colsum(out_grad[...].astype(f32))


def output_kernel(n_chunks, plan, length, *refs):
    active_in, residual, vec = refs[:3]
    chunks = refs[3 : 3 + n_chunks]
    output, w, active, sems = refs[3 + n_chunks :]
    copies = start_all([(active_in, active)], sems)
    place(chunks, plan, w, third_column(residual.shape[1], active.shape[1], plan))
    wait_all(copies)
    for start, size in row_tiles(length):
        rows = slice(start, start + size)
        output[rows] = (residual[rows] + dot_nt(active[rows], w[...]) + vec[7:8]).astype(bf16)


def hidden_weight_kernel(plan, length, *refs):
    normed2, gi, out_grad, active_in = refs[:4]
    outs, (n2t, gt, active, grads, sems) = refs[4:-5], refs[-5:]
    hidden = gi.shape[1]
    copies = start_all([(active_in, active)], sems)
    for start, size in row_tiles(length):
        rows = slice(start, start + size)
        n2t[:, rows] = normed2[rows].T
        gt[:, rows] = out_grad[rows].T
    for at in range(0, hidden, 512):
        grads[:, at : at + 512] = dot(n2t[...], gi[:, at : at + 512]).astype(bf16)
    wait_all(copies)
    for at in range(0, hidden, 512):
        cols = slice(hidden + at, hidden + at + 512)
        grads[:, cols] = dot(gt[...], active[:, at : at + 512]).astype(bf16)
    spread(plan, grads, outs)


def grad_residual_kernel(n_chunks, plan, length, *refs):
    gi, residual, out_grad, vec, vec_before = refs[:5]
    chunks = refs[5 : 5 + n_chunks]
    grad_res, grad_att, grad_ctx, vec_grads, w = refs[5 + n_chunks :]
    width = residual.shape[1]
    place(chunks, plan, w, second_column(width, plan))
    sums = [jnp.zeros((1, width), f32) for _ in range(3)]
    for start, size in row_tiles(length):
        rows = slice(start, start + size)
        e = dot_nt(gi[rows], w[:, width:])
        n, scale = centred(residual[rows])
        gres = out_grad[rows].astype(f32) + norm_back(e, n, scale, vec[5:6])
        grad_res[rows] = gres
        gat_rows = gres.astype(bf16)
        grad_att[rows] = gat_rows
        grad_ctx[rows] = dot(gat_rows, w[:, :width]).astype(bf16)
        sums = [s + colsum(v) for s, v in zip(sums, (gat_rows.astype(f32), e * n, e))]
    grad_ctx[length:] = jnp.zeros((grad_ctx.shape[0] - length, width), bf16)
    vec_grads[...] = vec_before[...]
    for i in range(3):
        vec_grads[4 + i : 5 + i] = sums[i]


def attention_backward(j, refs, gk, gv, gkm, gq):
    q, kext, vext, kvmem, pt, grad_ctx = refs
    width = q.shape[1]
    groups = q.shape[0] // GROUP
    lanes = slice(64 * QUAD * j, 64 * QUAD * (j + 1))
    value_lanes = slice(width + lanes.start, width + lanes.stop)
    gk[...] = jnp.zeros(gk.shape, f32)
    gv[...] = jnp.zeros(gv.shape, f32)
    gkm[...] = jnp.zeros(gkm.shape, f32)
    masks = head_masks()
    scale = 64**-0.5
    q_masks = [(m * scale).astype(bf16) for m in masks]
    c_masks = [m.astype(bf16) for m in masks]
    out_masks = [m * scale for m in masks]
    half = 64 * QUAD

    def step(g, carry):
        top = pl.multiple_of(g * GROUP, GROUP)
        keys = jnp.concatenate([kext[pl.ds(top, SPAN), lanes], kvmem[:, lanes]], axis=0)
        values = jnp.concatenate([vext[pl.ds(top, SPAN), lanes], kvmem[:, value_lanes]], axis=0)
        queries = stacked(q[pl.ds(top, GROUP), lanes], q_masks)
        upstream = stacked(grad_ctx[pl.ds(top, GROUP), lanes], c_masks)
        weights = pt[g, j]
        wide = weights.astype(f32)
        gp = dot_nt(values, upstream)
        gs = (wide * (gp - colsum(gp * wide))).astype(bf16)
        gkeys = dot(gs, queries)
        gvalues = dot(weights, upstream)
        gk[pl.ds(top, SPAN)] += gkeys[:SPAN]
        gv[pl.ds(top, SPAN)] += gvalues[:SPAN]
        gkm[:, :half] += gkeys[SPAN:]
        gkm[:, half:] += gvalues[SPAN:]
        gq[pl.ds(top, GROUP)] = unstacked(dot_tn(gs, keys), out_masks).astype(bf16)
        return carry

    lax.fori_loop(0, groups, step, 0, unroll=6)


def bank_block(bank, width):
    return jnp.concatenate(
        [bank[0].astype(f32), jnp.zeros((16 - MEM, width), f32)], axis=0
    ).astype(bf16)


def projection_grads(turned, bank, gq, gk, gv, gkm, grads, length, first):
    part = gq.shape[1]
    grads[:, first : first + part] = dot(turned, gq[:length]).astype(bf16)
    grads[:, first + part : first + 2 * part] = dot(turned, gk[...]).astype(bf16)
    grads[:, first + 2 * part : first + 3 * part] = dot(turned, gv[...]).astype(bf16)
    grads[:, first + 3 * part : first + 5 * part] = dot_tn(
        bank_block(bank, turned.shape[0]), gkm
    ).astype(bf16)


def first_quad_kernel(plan, length, *refs):
    grad_att, ctx, bank, grad_ctx = refs[:4]
    stored = refs[4:10]
    gq, gk_rows, gv_rows, gk_left, gv_left, gbank, nt = refs[10:17]
    n_out = 2 if plan is not None else 1
    outs = refs[17 : 17 + n_out]
    gk, gv, gkm, gat, grads, *held, sems = refs[17 + n_out :]
    normed, q, kext, vext, kvmem, pt = held
    copies = start_all(zip(stored, held), sems)
    width = ctx.shape[1]
    for start, size in row_tiles(length):
        rows = slice(start, start + size)
        gat[:, rows] = grad_att[rows].T
    grads[:, :width] = dot(gat[...], ctx[:length]).astype(bf16)
    wait_all(copies)
    for start, size in row_tiles(length):
        rows = slice(start, start + size)
        nt[:, rows] = normed[rows].T
    attention_backward(0, (q, kext, vext, kvmem, pt, grad_ctx), gk, gv, gkm, gq)
    gk_left[...] = gk[0:LEAD]
    gv_left[...] = gv[0:LEAD]
    gk_rows[...] = gk[LEAD : LEAD + length].astype(bf16)
    gv_rows[...] = gv[LEAD : LEAD + length].astype(bf16)
    gbank[...] = gkm[...].astype(bf16)
    projection_grads(nt[...], bank, gq, gk_rows, gv_rows, gbank[...], grads, length, width)
    spread(plan, grads, outs)


def second_quad_kernel(length, *refs):
    grad_ctx, *stored = refs[:6]
    gq, gk_rows, gv_rows, gk_left, gv_left, gbank, gk, gv, gkm, *held, sems = refs[6:]
    q, kext, vext, kvmem, pt = held
    wait_all(start_all(zip(stored, held), sems))
    attention_backward(1, (q, kext, vext, kvmem, pt, grad_ctx), gk, gv, gkm, gq)
    gk_left[...] = gk[0:LEAD]
    gv_left[...] = gv[0:LEAD]
    gk_rows[...] = gk[LEAD : LEAD + length].astype(bf16)
    gv_rows[...] = gv[LEAD : LEAD + length].astype(bf16)
    gbank[...] = gkm[...].astype(bf16)


def lower_kernel(n_chunks, plan, length, *refs):
    frames, bank, grad_res, vec, vec_grads, nt = refs[:6]
    gq, gk, gv, gk_left, gv_left, gbank = ([refs[6 + i], refs[12 + i]] for i in range(6))
    chunks = refs[18 : 18 + n_chunks]
    rest = refs[18 + n_chunks :]
    grad_frames, grad_bank, grad_ck, grad_cv = rest[:4]
    outs = rest[4:6]
    w, grads = rest[6:]
    width = frames.shape[1]
    part = gq[0].shape[1]
    place(chunks, plan, w)
    grad_ck[0] = jnp.concatenate([v[...] for v in gk_left], axis=1)[LEAD - LEFT :]
    grad_cv[0] = jnp.concatenate([v[...] for v in gv_left], axis=1)[LEAD - LEFT :]
    projection_grads(nt[...], bank, gq[1], gk[1], gv[1], gbank[1][...], grads, length, 0)
    bank_grads = jnp.concatenate(
        [v[:, at : at + part] for at in (0, part) for v in gbank], axis=1
    )
    grad_bank[0] = dot_nt(bank_grads, w[:, 3 * width : 5 * width])[:MEM]
    sums = [jnp.zeros((1, width), f32) for _ in range(4)]
    gains = vec[0:1]
    for start, size in row_tiles(length):
        rows = slice(start, start + size)
        parts = [jnp.concatenate([v[rows] for v in pair], axis=1) for pair in (gq, gk, gv)]
        e = (
            dot_nt(parts[0], w[:, :width])
            + dot_nt(parts[1], w[:, width : 2 * width])
            + dot_nt(parts[2], w[:, 2 * width : 3 * width])
        )
        n, s = centred(frames[rows].astype(f32))
        grad_frames[rows] = grad_res[rows] + norm_back(e, n, s, gains)
        sums = [
            t + colsum(v)
            for t, v in zip(sums, (e * n, e, parts[0].astype(f32), parts[2].astype(f32)))
        ]
    vectors = jnp.concatenate(sums + [vec_grads[4:16]], axis=0)
    if plan is not None:
        block = jnp.concatenate([vectors[:, :256], vectors[:, 256:]], axis=0).astype(bf16)
        grads[:, 5 * part :] = jnp.concatenate([block] * 16, axis=0)
        spread(plan, grads, outs)
    else:
        outs[0][...] = grads[...]
        outs[1][...] = vectors


def pack_first_kernel(*refs):
    weights, vectors, inner_bias, out = refs[:7], refs[7:15], refs[15], refs[16]
    held, bias_held, sems = refs[17:25], refs[25], refs[26]
    width = weights[0].shape[1]
    column = 0
    copies = []
    for i, ref in enumerate(weights):
        if i == 4:
            column += 256
        copies.append((ref, out.at[:, pl.ds(column, ref.shape[1])]))
        column += ref.shape[1]
    copies += list(zip((*vectors, inner_bias), (*held, bias_held)))
    copies = [pltpu.make_async_copy(a, b, sems.at[i]) for i, (a, b) in enumerate(copies)]
    for copy in copies:
        copy.start()
    wait_all(copies)
    rank = lax.axis_index("fsdp")
    own = jnp.concatenate([ref[...].astype(f32) for ref in held], axis=0)
    part = own.shape[1]
    placed = jnp.where(
        lax.broadcasted_iota(jnp.int32, (8, width), 1) // part == rank,
        jnp.concatenate([own] * (width // part), axis=1),
        0.0,
    )
    bias = bias_held[...].astype(f32)
    count = bias.shape[1]
    row = lax.broadcasted_iota(jnp.int32, (4, width), 0)
    lane = lax.broadcasted_iota(jnp.int32, (4, width), 1)
    inner = jnp.where(
        (row * width + lane) // count == rank,
        jnp.concatenate([jnp.concatenate([bias] * (width // count), axis=1)] * 4, axis=0),
        0.0,
    )
    block = jnp.concatenate([placed, inner, jnp.zeros((4, width), f32)], axis=0)
    block = jnp.concatenate([block[:, : width // 2], block[:, width // 2 :]], axis=0)
    out[:, 5 * width : 5 * width + 256] = block.astype(bf16)


def first_sum_kernel(mine, other, *refs):
    right, left = refs[-2:]
    total = (mine[0].astype(f32) + other[0].astype(f32)).astype(bf16)
    half = right.shape[1]
    right[...] = total[:, :half]
    left[...] = total[:, half:]


def step_sum_kernel(mine_r, other_r, mine_l, other_l, a, b, *refs):
    right, left = refs[-2:]
    width = right.shape[1]
    wide_a, wide_b = a.shape[1], b.shape[1]
    to_right = mine_r[0].astype(f32) + other_r[0].astype(f32)
    to_left = mine_l[0].astype(f32) + other_l[0].astype(f32)
    right[:, :wide_a] = (to_right[:, :wide_a] + a[...].astype(f32)).astype(bf16)
    left[:, width - wide_b :] = (to_left[:, width - wide_b :] + b[...].astype(f32)).astype(bf16)
    if wide_a < width:
        right[:, wide_a:] = to_right[:, wide_a:].astype(bf16)
        left[:, : width - wide_b] = to_left[:, : width - wide_b].astype(bf16)


def last_sum_kernel(mine, other, a, b, *refs):
    refs[-1][...] = (
        mine[0].astype(f32) + other[0].astype(f32) + a[...].astype(f32) + b[...].astype(f32)
    ).astype(bf16)


def chunk_spec(width, index):
    return pl.BlockSpec((1, 32, width), lambda i: (index, 0, 0))


class Reduction:
    def __init__(self, mine, other):
        self.mine, self.other = mine, send(other, TO_CORE)
        self.width = mine.shape[2]
        self.distance = 4

    def sums(self, kernel, shapes, places, partial, after):
        args, specs = [], []
        for place in places:
            args += [self.mine, self.other]
            specs += [chunk_spec(self.width, place)] * 2
        return call(
            kernel,
            shapes,
            [VMEM] * len(shapes),
            [],
            [*args, *partial, *after],
            [*specs, *[VMEM] * len(partial), *[ANY] * len(after)],
            0.5,
            limit=8,
            grid=(1,),
        )

    def advance(self, after=()):
        width, s = self.width, self.distance
        full = shape((32, width), bf16)
        self.distance -= 1
        if s == 0:
            made = self.sums(last_sum_kernel, [full], [0], [self.a, self.b], after)
            self.total = made[0]
            self.far = lax.ppermute(self.total, "rep", [(0, 1), (1, 0)])
            return made
        if s == 4:
            half = halves(width)
            shapes = [shape((32, half), bf16), shape((32, width - half), bf16)]
            made = self.sums(first_sum_kernel, shapes, [4], [], after)
        else:
            made = self.sums(
                step_sum_kernel, [full, full], [s, 8 - s], [self.a, self.b], after
            )
        self.a, self.b = send(made[0], TO_RIGHT), send(made[1], TO_LEFT)
        return made

    def finish(self):
        while self.distance >= 0:
            self.advance()
        return self


def upper_result_kernel(both, both_far, inner_out, outer_out):
    total = both[...].astype(f32) + both_far[...].astype(f32)
    hidden = inner_out.shape[1]
    inner_out[...] = total[:, :hidden]
    outer_out[...] = total[:, hidden:]


def lower_result_kernel(one, one_far, two, two_far, *refs):
    q_out, k_out, v_out, m_out, output_out = refs[:5]
    vector_outs, inner_out = refs[5:13], refs[13]
    width = output_out.shape[1]
    part = (one.shape[1] - width) // 5
    total = one[...].astype(f32) + one_far[...].astype(f32)
    output_out[...] = total[:, :width]
    pair = [total[:, width:]]
    pair.append(two[...].astype(f32) + two_far[...].astype(f32))
    for i, out in enumerate((q_out, k_out, v_out)):
        for j in range(2):
            out[:, j * part : (j + 1) * part] = pair[j][:, i * part : (i + 1) * part]
    for i in range(2):
        for j in range(2):
            at = (2 * i + j) * part
            m_out[:, at : at + part] = pair[j][:, (3 + i) * part : (4 + i) * part]
    block = pair[1][:, 5 * part :]
    vectors = jnp.concatenate([block[:16], block[16:]], axis=1)
    rank = lax.axis_index("fsdp")
    quarter = lax.rem(rank, 4)

    def pick(v, index, size):
        found = jnp.zeros((v.shape[0], size), f32)
        for k in range(v.shape[1] // size):
            found += jnp.where(index == k, v[:, k * size : (k + 1) * size], 0.0)
        return found

    own = pick(pick(vectors[:8], lax.div(rank, 4), 128), quarter, 32)
    for i, out in enumerate(vector_outs):
        out[...] = own[i : i + 1]
    inner = pick(vectors[8:12], quarter, 128)
    found = jnp.zeros((1, 128), f32)
    for k in range(4):
        found += jnp.where(lax.div(rank, 4) == k, inner[k : k + 1], 0.0)
    inner_out[...] = found


def call(kernel, out_shapes, out_specs, scratch, args, specs, micros, limit=20, grid=()):
    specs = list(specs)
    args = [
        pltpu.with_memory_space_constraint(v, pltpu.HBM) if spec is HBM else v
        for v, spec in zip(args, specs)
    ]
    single = not isinstance(out_specs, (list, tuple))
    shapes = [out_shapes] if single else list(out_shapes)
    spaces = [out_specs] if single else list(out_specs)
    shapes = [
        pltpu.HBM(v.shape, v.dtype) if spec is HBM else v for v, spec in zip(shapes, spaces)
    ]
    return pl.pallas_call(
        kernel,
        grid=grid,
        out_shape=shapes[0] if single else tuple(shapes),
        in_specs=specs,
        out_specs=spaces[0] if single else tuple(spaces),
        scratch_shapes=scratch,
        compiler_params=pltpu.CompilerParams(vmem_limit_bytes=limit * 1024 * 1024),
        cost_estimate=pl.CostEstimate(
            flops=int(micros * 1.15e9), bytes_accessed=int(micros * 3.6e6), transcendentals=0
        ),
    )(*args)


def shape(dims, dtype):
    return jax.ShapeDtypeStruct(dims, dtype)


def per_device(ring, *args):
    (
        frames,
        memory_bank,
        cache_keys,
        cache_values,
        out_grad,
        first_gain,
        first_shift,
        query_weight,
        query_bias,
        key_weight,
        value_weight,
        value_bias,
        memory_weight,
        output_weight,
        output_bias,
        second_gain,
        second_shift,
        inner_weight,
        inner_bias,
        outer_weight,
        outer_bias,
    ) = args
    length, width = frames.shape
    ranks = width // first_gain.shape[0]
    part = width // ranks
    inner_part = inner_bias.shape[0]
    hidden = inner_part * ranks
    groups = -(-length // GROUP)
    padded = groups * GROUP
    extended = (groups - 1) * GROUP + SPAN
    quad = 64 * QUAD
    vectors = [
        first_gain,
        first_shift,
        query_bias,
        value_bias,
        output_bias,
        second_gain,
        second_shift,
        outer_bias,
    ]
    first = [query_weight, key_weight, value_weight, memory_weight]
    second = [output_weight.T, inner_weight, outer_weight.T]
    if ring:
        weights = call(
            pack_first_kernel,
            shape((part, 6 * width + 2 * hidden + 256), bf16),
            VMEM,
            [
                *([pltpu.VMEM((1, part), bf16)] * 8),
                pltpu.VMEM((1, inner_part), bf16),
                pltpu.SemaphoreType.DMA((16,)),
            ],
            [
                *first,
                *second,
                *(v.reshape(1, part) for v in vectors),
                inner_bias.reshape(1, inner_part),
            ],
            [HBM] * 16,
            1,
            limit=8,
        )
        gathered = ring_gather(weights)
        plan = chunk_plan(weights.shape[1])
        vec = jnp.zeros((16, width), f32)
    else:
        weights = jnp.concatenate(first + second, axis=1)
        plan = None
        gathered = [lax.all_gather(weights, "fsdp", axis=0, tiled=True)]
        vec = jnp.concatenate(
            [
                jnp.stack([lax.all_gather(v, "fsdp", axis=0, tiled=True) for v in vectors]),
                lax.all_gather(inner_bias, "fsdp", axis=0, tiled=True).reshape(-1, width),
                jnp.zeros((4, width), bf16),
            ],
            axis=0,
        ).astype(f32)
    count = len(gathered)
    first_width, second_width = 5 * width + (256 if ring else 0), width + hidden

    dma = pltpu.SemaphoreType.DMA
    attended_shapes = (
        shape((length, width), bf16),
        shape((padded, width), bf16),
        shape((extended, width), bf16),
        shape((extended, width), bf16),
        shape((16, 2 * width), bf16),
        shape((groups, HEADS // QUAD, KEYS, GROUP * QUAD), bf16),
    )
    held = [pltpu.VMEM(v.shape, v.dtype) for v in attended_shapes]
    *attended, ctx, vec = call(
        functools.partial(attention_forward_kernel, count, plan, length),
        (
            *attended_shapes,
            shape((padded, width), bf16),
            shape((16, width), f32),
        ),
        [HBM] * 6 + [VMEM] * 2,
        [
            *held,
            pltpu.VMEM((width, first_width), bf16),
            pltpu.VMEM((2, KEYS, GROUP * QUAD), f32),
            dma((6,)),
        ],
        [frames, memory_bank, cache_keys, cache_values, vec, *gathered],
        [VMEM] * (5 + count),
        9,
    )

    def grad_shapes(w):
        if ring:
            return (shape((8, 32, w), bf16), shape((8, 32, w), bf16))
        return (shape((width, w), bf16),)

    grad_specs = [VMEM] * (2 if ring else 1)
    row, wide_row = shape((length, width), bf16), shape((length, hidden), bf16)
    row_wide, vec_shape = shape((length, width), f32), shape((16, width), f32)
    residual, normed2, active, slope = call(
        functools.partial(inner_kernel, count, plan, length),
        (row_wide, row, wide_row, wide_row),
        [VMEM, VMEM, HBM, VMEM],
        [
            pltpu.VMEM((width, second_width), bf16),
            pltpu.VMEM((length, hidden), bf16),
            dma((hidden // 512,)),
        ],
        [frames, ctx, vec, *gathered],
        [VMEM] * (3 + count),
        7,
    )

    gi, vec_grads = call(
        functools.partial(grad_inner_kernel, count, plan, length),
        (wide_row, vec_shape),
        [VMEM] * 2,
        [pltpu.VMEM((width, hidden), bf16)],
        [out_grad, slope, *gathered],
        [VMEM] * (2 + count),
        3,
    )
    both_grads = call(
        functools.partial(hidden_weight_kernel, plan, length),
        grad_shapes(2 * hidden),
        grad_specs,
        [
            pltpu.VMEM((width, length), bf16),
            pltpu.VMEM((width, length), bf16),
            pltpu.VMEM((length, hidden), bf16),
            pltpu.VMEM((width, 2 * hidden), bf16),
            dma((1,)),
        ],
        [normed2, gi, out_grad, active],
        [VMEM] * 3 + [HBM],
        4,
    )
    both = Reduction(*both_grads) if ring else None

    def steps(after, *reductions):
        made = []
        if ring:
            for reduction in reductions:
                made += reduction.advance([after])
        return made

    grad_res, grad_att, grad_ctx, vec_grads = gated(
        functools.partial(grad_residual_kernel, count, plan, length),
        (row_wide, row, shape((padded, width), bf16), vec_shape),
        [VMEM] * 4,
        [pltpu.VMEM((width, second_width), bf16)],
        [gi, residual, out_grad, vec, vec_grads, *gathered],
        [VMEM] * (5 + count),
        5,
        both_grads[:1],
    )
    made = steps(vec_grads, both)
    part_row = shape((length, quad), bf16)
    left_row = shape((LEAD, quad), f32)
    quad_shapes = (
        shape((padded, quad), bf16),
        part_row,
        part_row,
        left_row,
        left_row,
        shape((16, 2 * quad), bf16),
    )
    quad_scratch = [
        pltpu.VMEM((extended, quad), f32),
        pltpu.VMEM((extended, quad), f32),
        pltpu.VMEM((16, 2 * quad), f32),
    ]
    *quad_one, nt, one_a, one_b = gated(
        functools.partial(first_quad_kernel, plan, length),
        (*quad_shapes, shape((width, length), bf16), *grad_shapes(width + 5 * quad)),
        [VMEM] * 7 + grad_specs,
        [
            *quad_scratch,
            pltpu.VMEM((width, length), bf16),
            pltpu.VMEM((width, width + 5 * quad), bf16),
            *held,
            dma((6,)),
        ],
        [grad_att, ctx, memory_bank, grad_ctx, *attended],
        [VMEM] * 4 + [HBM] * 6,
        7,
        made,
    ) + (() if ring else (None,))
    one = Reduction(one_a, one_b) if ring else None
    made = steps(nt, both)
    quad_two = gated(
        functools.partial(second_quad_kernel, length),
        quad_shapes,
        [VMEM] * 6,
        [*quad_scratch, *held[1:], dma((5,))],
        [grad_ctx, *attended[1:]],
        [VMEM] + [HBM] * 5,
        4,
        made,
    )
    made = steps(quad_two[5], both, one)
    lower_outs = (
        grad_shapes(5 * quad + 256) if ring else (shape((width, 5 * quad), bf16), vec_shape)
    )
    grad_frames, grad_bank, grad_ck, grad_cv, two_a, two_b = gated(
        functools.partial(lower_kernel, count, plan, length),
        (
            row_wide,
            shape((1, MEM, width), f32),
            shape((1, LEFT, width), f32),
            shape((1, LEFT, width), f32),
            *lower_outs,
        ),
        [VMEM] * 6,
        [
            pltpu.VMEM((width, first_width), bf16),
            pltpu.VMEM((width, 5 * quad + (256 if ring else 0)), bf16),
        ],
        [frames, memory_bank, grad_res, vec, vec_grads, nt, *quad_one, *quad_two, *gathered],
        [VMEM] * (18 + count),
        11,
        made,
    )
    two = Reduction(two_a, two_b) if ring else None
    made = steps(grad_bank, both, one)
    output = gated(
        functools.partial(output_kernel, count, plan, length),
        row,
        VMEM,
        [
            pltpu.VMEM((width, hidden), bf16),
            pltpu.VMEM((length, hidden), bf16),
            dma((1,)),
        ],
        [active, residual, vec, *gathered],
        [HBM] + [VMEM] * (2 + count),
        3,
        made,
    )
    if ring:
        for reduction in (both, one, two):
            reduction.finish()
        inner_sum, outer_sum = call(
            upper_result_kernel,
            (shape((part, hidden), f32), shape((part, hidden), f32)),
            [VMEM] * 2,
            [],
            [both.total, both.far],
            [VMEM] * 2,
            1,
            limit=8,
        )
        square = shape((part, width), f32)
        q_sum, k_sum, v_sum, m_sum, output_sum, *own = call(
            lower_result_kernel,
            (
                square,
                square,
                square,
                shape((part, 2 * width), f32),
                square,
                *([shape((1, part), f32)] * 8),
                shape((1, inner_part), f32),
            ),
            [VMEM] * 14,
            [],
            [one.total, one.far, two.total, two.far],
            [VMEM] * 4,
            1,
            limit=8,
        )
        own_inner = own[8].reshape(inner_part)
        own = [v.reshape(part) for v in own[:8]]
    else:

        def reduce(v):
            total = lax.psum_scatter(v, "fsdp", scatter_dimension=0, tiled=True)
            return lax.psum(total, "rep").astype(f32)

        total = reduce(both_grads[0])
        inner_sum, outer_sum = total[:, :hidden], total[:, hidden:]
        low, high = reduce(one_a), reduce(two_a)
        output_sum = low[:, :width]
        sums = [v.reshape(part, 5, quad) for v in (low[:, width:], high)]
        q_sum, k_sum, v_sum, m_low, m_high = (
            jnp.concatenate([v[:, i] for v in sums], axis=1) for i in range(5)
        )
        m_sum = jnp.concatenate([m_low, m_high], axis=1)
        vec_sum = lax.psum(two_b, ("rep", "fsdp"))
        rank = lax.axis_index("fsdp")
        own = lax.dynamic_slice(vec_sum[:8], (0, rank * part), (8, part))
        own_inner = lax.dynamic_slice(
            vec_sum[8:12].reshape(-1), (rank * inner_part,), (inner_part,)
        )
    return (
        output,
        grad_frames,
        grad_bank,
        grad_ck,
        grad_cv,
        own[0],
        own[1],
        q_sum,
        own[2],
        k_sum,
        v_sum,
        own[3],
        m_sum,
        output_sum.T,
        own[4],
        own[5],
        own[6],
        inner_sum,
        own_inner,
        outer_sum.T,
        own[7],
    )


def without_gates(kernel, n_args, n_gates, *refs):
    kernel(*refs[:n_args], *refs[n_args + n_gates :])


def gated(kernel, out_shapes, out_specs, scratch, args, specs, micros, made):
    return call(
        functools.partial(without_gates, kernel, len(args), len(made)),
        out_shapes,
        out_specs,
        scratch,
        [*args, *made],
        [*specs, *[ANY] * len(made)],
        micros,
    )


def solution(mesh):
    both = ("rep", "fsdp")
    rows, vector = P("fsdp", None), P("fsdp")
    columns = P(None, "fsdp")
    weights = (
        vector,
        vector,
        rows,
        vector,
        rows,
        rows,
        vector,
        rows,
        columns,
        vector,
        vector,
        vector,
        rows,
        vector,
        columns,
        vector,
    )
    blocks = P(both, None, None)
    in_specs = (P(both, None), blocks, blocks, blocks, P(both, None), *weights)
    out_specs = (P(both, None), P(both, None), blocks, blocks, blocks, *weights)
    ring = mesh.shape["fsdp"] == 16 and mesh.shape["rep"] == 2
    return jax.shard_map(
        functools.partial(per_device, ring),
        mesh=mesh,
        in_specs=in_specs,
        out_specs=out_specs,
        check_vma=False,
    )
```

```python
import functools

import jax
import jax.numpy as jnp
from jax import lax
from jax.experimental import pallas as pl
from jax.experimental.pallas import tpu as pltpu
from jax.sharding import PartitionSpec as P

HEADS = 8
SEG = 16
RIGHT = 4
LEFT = 30
MEM = 4

LEAD = 32
GROUP = 64
SPAN = 112
KEYS = 128
QUAD = 4
masked_value = -1e30
epsilon = 1e-05
gelu_a = 0.7978845608028654
gelu_b = gelu_a * 0.044715

bf16 = jnp.bfloat16
f32 = jnp.float32
VMEM = pl.BlockSpec(memory_space=pltpu.VMEM)
ANY = pl.BlockSpec(memory_space=pl.ANY)
HBM = pl.BlockSpec(memory_space=pltpu.HBM)


def dot(a, b):
    return lax.dot_general(a, b, (((1,), (0,)), ((), ())), preferred_element_type=f32)


def dot_nt(a, b):
    return lax.dot_general(a, b, (((1,), (1,)), ((), ())), preferred_element_type=f32)


def dot_tn(a, b):
    return lax.dot_general(a, b, (((0,), (0,)), ((), ())), preferred_element_type=f32)


def row_tiles(rows):
    return [(start, min(256, rows - start)) for start in range(0, rows, 256)]


def centred(v):
    center = v - jnp.mean(v, axis=-1, keepdims=True)
    spread = jnp.mean(center * center, axis=-1, keepdims=True)
    scale = lax.rsqrt(spread + epsilon)
    return center * scale, scale


def norm_back(e, n, scale, gain):
    eg = e * gain
    return scale * (
        eg - jnp.mean(eg, axis=-1, keepdims=True) - n * jnp.mean(eg * n, axis=-1, keepdims=True)
    )


def colsum(v):
    return jnp.sum(v, axis=0, keepdims=True)


RING = (0, 2, 4, 6, 7, 5, 3, 1)


def ring_pairs(step):
    pairs = []
    for k in range(8):
        for core in range(2):
            pairs.append((2 * RING[k] + core, 2 * RING[(k + step) % 8] + core))
    return pairs


TO_RIGHT, TO_LEFT = ring_pairs(1), ring_pairs(-1)
TO_CORE = [(i, i ^ 1) for i in range(16)]


def ring_ids():
    rank = lax.axis_index("fsdp")
    core, chip = lax.rem(rank, 2), lax.div(rank, 2)
    z, x = lax.div(chip, 2), lax.rem(chip, 2)
    return jnp.where(x == 0, z, 7 - z), core


def ring_rank(position, core):
    position = lax.rem(position, 8)
    return 2 * jnp.where(position < 4, 2 * position, 15 - 2 * position) + core


def halves(width):
    return width // 2 // 128 * 128


def send(v, pairs):
    return lax.ppermute(v, "fsdp", pairs)


def across(v):
    return lax.ppermute(v, "rep", [(0, 1), (1, 0)])


def shares(width):
    third = width // 3 // 128 * 128
    return width - 2 * third, third


def ring_gather(shard, main, after):
    common, third = shares(shard.shape[1])
    got = [(shard, 0, "all")]
    a = b = main
    for step in (1, 2, 3):
        a, b = send(a, TO_RIGHT), send(b, TO_LEFT)
        pair = call(
            tails_kernel,
            shape((shard.shape[0], 2 * third), bf16),
            VMEM,
            [],
            [a, b],
            [VMEM] * 2,
            0.3,
            limit=4,
        )
        pair = across(pair)
        if step == 1:
            pair = hold(pair, after)
        got += [(a, 8 - step, "main"), (b, step, "main"), (pair, step, "pair")]
    a, b = send(a[:, :common], TO_RIGHT), send(b[:, common:], TO_LEFT)
    got += [(a, 4, "common"), (b, 4, "own"), (across(b), 4, "other")]
    return [(v, d, 0, k) for v, d, k in got] + [(send(v, TO_CORE), d, 1, k) for v, d, k in got]


def tails_kernel(a, b, *refs):
    out = refs[-1]
    third = out.shape[1] // 2
    out[:, :third] = a[:, a.shape[1] - third :]
    out[:, third:] = b[:, b.shape[1] - third :]


def lay_rows(places, has_before, *refs):
    refs, whole = refs[: len(places)], refs[-1]
    common, third = shares(whole.shape[1])
    position, core = ring_ids()
    replica = lax.axis_index("rep")
    own = pl.ds(pl.multiple_of(common + replica * third, 128), third)
    other = pl.ds(pl.multiple_of(common + (1 - replica) * third, 128), third)

    def rows(distance, flip):
        owner = ring_rank(position + distance, core if flip == 0 else 1 - core)
        return pl.ds(pl.multiple_of(owner * 32, 32), 32)

    for ref, (distance, flip, kind) in zip(refs, places):
        at = rows(distance, flip)
        if kind == "all":
            whole[at, :] = ref[...]
        elif kind == "main":
            whole[at, :common] = ref[:, :common]
            whole[at, own] = ref[:, common:]
        elif kind == "pair":
            whole[rows(8 - distance, flip), other] = ref[:, :third]
            whole[at, other] = ref[:, third:]
        elif kind == "common":
            whole[at, :common] = ref[...]
        else:
            whole[at, own if kind == "own" else other] = ref[...]


def whole_weights(items, width, before=None):
    places = tuple(item[1:] for item in items)
    arrays = [item[0] for item in items]
    kept = [] if before is None else [before]
    result = shape((width, arrays[0].shape[1] if before is None else before.shape[1]), bf16)
    return pl.pallas_call(
        functools.partial(lay_rows, places, bool(kept)),
        out_shape=result,
        in_specs=[VMEM] * len(arrays) + [VMEM] * len(kept),
        out_specs=VMEM,
        input_output_aliases={len(arrays): 0} if kept else {},
        compiler_params=pltpu.CompilerParams(vmem_limit_bytes=24 * 2**20),
        cost_estimate=pl.CostEstimate(flops=10**9, bytes_accessed=4 * 10**6, transcendentals=0),
    )(*arrays, *kept)


def spread(ring, grads, outs):
    if not ring:
        outs[0][...] = grads[...]
        return
    position, core = ring_ids()
    for distance in range(8):
        for flip, out in enumerate(outs):
            owner = ring_rank(position + distance, core if flip == 0 else 1 - core)
            out[distance] = grads[pl.ds(pl.multiple_of(owner * 32, 32), 32), :]


def start_all(pairs, sems, first=0):
    copies = [pltpu.make_async_copy(a, b, sems.at[first + i]) for i, (a, b) in enumerate(pairs)]
    for copy in copies:
        copy.start()
    return copies


def wait_all(copies):
    for copy in copies:
        copy.wait()


def columns(width, hidden):
    return 5 * width, 6 * width, 6 * width + hidden, 6 * width + 2 * hidden


def head_masks():
    lane = lax.broadcasted_iota(jnp.int32, (1, 64 * QUAD), 1)
    return [(lane // 64 == h).astype(f32) for h in range(QUAD)]


def stacked(rows, masks):
    return jnp.concatenate([rows * m for m in masks], axis=0)


def unstacked(wide, masks):
    parts = [wide[GROUP * h : GROUP * (h + 1)] * masks[h] for h in range(QUAD)]
    return parts[0] + parts[1] + parts[2] + parts[3]


def added_mask(limit):
    row = lax.broadcasted_iota(jnp.int32, (KEYS, GROUP * QUAD), 0)
    query = lax.rem(lax.broadcasted_iota(jnp.int32, (KEYS, GROUP * QUAD), 1), GROUP)
    first = query // SEG * SEG + (LEAD - LEFT)
    inside = (row >= first) & (row < first + LEFT + SEG + RIGHT) & (row < limit)
    bank = (row >= SPAN) & (row < SPAN + MEM)
    return jnp.where((inside & (row < SPAN)) | bank, 0.0, masked_value)


def prepare_kernel(length, frames, out_grad, n_out, bias_out, nt_out, gt_out, nt, gt, sems):
    for start, size in row_tiles(length):
        rows = slice(start, start + size)
        n, _ = centred(frames[rows].astype(f32))
        n_out[rows] = n
        nt[:, rows] = n.astype(bf16).T
        gt[:, rows] = out_grad[rows].T
    copies = start_all([(nt, nt_out), (gt, gt_out)], sems)
    bias_out[...] = jnp.zeros(bias_out.shape, f32)
    bias_out[7:8] = colsum(out_grad[...].astype(f32))
    wait_all(copies)


def attention_forward_kernel(ring, length, *refs):
    normal, bank, cache_k, cache_v, vec, w = refs[:6]
    stored, (ctx, vec_out, cols_out) = refs[6:11], refs[11:14]
    q, kext, vext, kvmem, pt, mask, sems = refs[14:]
    width = normal.shape[1]
    groups = q.shape[0] // GROUP
    if not ring:
        vectors = vec[...]
    else:
        blocks = w[:, w.shape[1] - 256 :].astype(f32).reshape(16, 32, 256)
        total = jnp.sum(blocks, axis=0)
        vectors = jnp.concatenate([total[:16], total[16:]], axis=1)
    vec_out[...] = vectors
    cols_out[...] = vectors.T

    def left_rows(cache):
        rows = cache[0].astype(f32)
        return jnp.concatenate([jnp.zeros((LEAD - LEFT, width), f32), rows], axis=0).astype(bf16)

    kext[0:LEAD] = left_rows(cache_k)
    vext[0:LEAD] = left_rows(cache_v)
    tail = kext.shape[0] - LEAD - length
    kext[LEAD + length :] = jnp.zeros((tail, width), bf16)
    vext[LEAD + length :] = jnp.zeros((tail, width), bf16)
    q[length:] = jnp.zeros((q.shape[0] - length, width), bf16)
    bank_rows = jnp.concatenate(
        [bank[0].astype(f32), jnp.zeros((16 - MEM, width), f32)], axis=0
    ).astype(bf16)
    kvmem[...] = dot(bank_rows, w[:, 3 * width : 5 * width]).astype(bf16)

    for start, size in row_tiles(length):
        rows = (normal[start : start + size] * vectors[0:1] + vectors[1:2]).astype(bf16)
        q[start : start + size] = (dot(rows, w[:, :width]) + vectors[2:3]).astype(bf16)
        kext[LEAD + start : LEAD + start + size] = dot(rows, w[:, width : 2 * width]).astype(bf16)
        vext[LEAD + start : LEAD + start + size] = (
            dot(rows, w[:, 2 * width : 3 * width]) + vectors[3:4]
        ).astype(bf16)

    copies = start_all(zip((q, kext, vext, kvmem), stored), sems)
    masks = head_masks()
    scale = 64**-0.5
    q_masks = [(m * scale).astype(bf16) for m in masks]
    mask[0] = added_mask(KEYS)
    mask[1] = added_mask(LEAD + length - GROUP * (groups - 1))

    def step(g, carry):
        top = pl.multiple_of(g * GROUP, GROUP)
        hidden = mask[(g == groups - 1).astype(jnp.int32)]
        for j in range(HEADS // QUAD):
            lanes = slice(64 * QUAD * j, 64 * QUAD * (j + 1))
            keys = jnp.concatenate([kext[pl.ds(top, SPAN), lanes], kvmem[:, lanes]], axis=0)
            values = jnp.concatenate(
                [vext[pl.ds(top, SPAN), lanes], kvmem[:, width + lanes.start : width + lanes.stop]],
                axis=0,
            )
            queries = stacked(q[pl.ds(top, GROUP), lanes], q_masks)
            scores = dot_nt(keys, queries) + hidden
            raised = jnp.exp(scores - jnp.max(scores, axis=0, keepdims=True))
            weights = (raised / jnp.sum(raised, axis=0, keepdims=True)).astype(bf16)
            pt[j, g] = weights
            ctx[pl.ds(top, GROUP), lanes] = unstacked(dot_tn(weights, values), masks).astype(bf16)
        return carry

    lax.fori_loop(0, groups, step, 0, unroll=6)
    wait_all(copies + start_all([(pt, stored[4])], sems, 4))


def inner_kernel(length, *refs):
    frames, ctx, vec, w, residual, normed2, active, slope, residual_out, active_out, sems = refs
    width = frames.shape[1]
    hidden = active.shape[1]
    first, second, _, _ = columns(width, hidden)
    for start, size in row_tiles(length):
        rows = slice(start, start + size)
        res = frames[rows].astype(f32) + dot_nt(ctx[rows], w[:, first:second]) + vec[4:5]
        residual[rows] = res
        n, _ = centred(res)
        normed2[rows] = (n * vec[5:6] + vec[6:7]).astype(bf16)

    block = 512
    copies = start_all([(residual, residual_out)], sems, hidden // block)
    for b in range(hidden // block):
        cols = slice(b * block, (b + 1) * block)
        for start, size in row_tiles(length):
            rows = slice(start, start + size)
            u = dot(normed2[rows], w[:, second + cols.start : second + cols.stop]) + vec[8 + b : 9 + b]
            uu = u * u
            h = 0.5 + 0.5 * jnp.tanh(u * (gelu_a + gelu_b * uu))
            act = u * h
            active[rows, cols] = act.astype(bf16)
            slope[rows, cols] = (
                h + act * (1.0 - h) * (2 * gelu_a + 6 * gelu_b * uu)
            ).astype(bf16)
        part = pl.ds(b * block, block)
        copies += start_all([(active.at[:, part], active_out.at[:, part])], sems, b)
    wait_all(copies)


def grad_inner_kernel(length, out_grad, slope, vec_before, w, gi, vec_grads):
    width, hidden = out_grad.shape[1], slope.shape[1]
    third = columns(width, hidden)[2]
    block = 512
    vec_grads[...] = vec_before[...]
    for b in range(hidden // block):
        cols = slice(b * block, (b + 1) * block)
        sums = jnp.zeros((1, block), f32)
        for start, size in row_tiles(length):
            rows = slice(start, start + size)
            up = dot(out_grad[rows], w[:, third + cols.start : third + cols.stop])
            part = (up * slope[rows, cols].astype(f32)).astype(bf16)
            gi[rows, cols] = part
            sums += colsum(part.astype(f32))
        vec_grads[8 + b : 9 + b] = sums


def output_kernel(length, active_in, residual_in, vec, w, output, active, residual, sems):
    copies = start_all([(active_in, active), (residual_in, residual)], sems)
    _, _, third, last = columns(residual.shape[1], active.shape[1])
    wait_all(copies)
    for start, size in row_tiles(length):
        rows = slice(start, start + size)
        output[rows] = (residual[rows] + dot_nt(active[rows], w[:, third:last]) + vec[7:8]).astype(bf16)


def hidden_weight_kernel(ring, length, *refs):
    normed2, gi, active, gt_in = refs[:4]
    outs, (n2t, gt, grads, sems) = refs[4:-4], refs[-4:]
    hidden = gi.shape[1]
    copies = start_all([(gt_in, gt)], sems)
    for start, size in row_tiles(length):
        rows = slice(start, start + size)
        n2t[:, rows] = normed2[rows].T
    for at in range(0, hidden, 512):
        grads[:, at : at + 512] = dot(n2t[...], gi[:, at : at + 512]).astype(bf16)
    wait_all(copies)
    for at in range(0, hidden, 512):
        cols = slice(hidden + at, hidden + at + 512)
        grads[:, cols] = dot(gt[...], active[:, at : at + 512]).astype(bf16)
    spread(ring, grads, outs)


def grad_residual_kernel(length, *refs):
    gi, residual, out_grad, vec, vec_before, w, nt_in, *stored = refs[:12]
    grad_att, grad_ctx, vec_grads, nt, *held = refs[12:21]
    grad_res_out, grad_res, sems = refs[21:]
    width = residual.shape[1]
    copies = start_all([(nt_in, nt), *quad_pairs(0, stored, held)], sems)
    first, second, third, _ = columns(width, gi.shape[1])
    sums = [jnp.zeros((1, width), f32) for _ in range(3)]
    for start, size in row_tiles(length):
        rows = slice(start, start + size)
        e = dot_nt(gi[rows], w[:, second:third])
        n, scale = centred(residual[rows])
        gres = out_grad[rows].astype(f32) + norm_back(e, n, scale, vec[5:6])
        grad_res[rows] = gres
        gat_rows = gres.astype(bf16)
        grad_att[rows] = gat_rows
        grad_ctx[rows] = dot(gat_rows, w[:, first:second]).astype(bf16)
        sums = [s + colsum(v) for s, v in zip(sums, (gat_rows.astype(f32), e * n, e))]
    grad_ctx[length:] = jnp.zeros((grad_ctx.shape[0] - length, width), bf16)
    copies += start_all([(grad_res, grad_res_out)], sems, 7)
    vec_grads[...] = vec_before[...]
    for i in range(3):
        vec_grads[4 + i : 5 + i] = sums[i]
    wait_all(copies)


def quad_pairs(j, stored, held):
    q, kext, vext, kvmem, pt = stored
    held_q, held_k, held_v, held_mem, held_pt = held
    size = 64 * QUAD
    width = q.shape[1]
    lanes, values = pl.ds(j * size, size), pl.ds(width + j * size, size)
    return [
        (q.at[:, lanes], held_q),
        (kext.at[:, lanes], held_k),
        (vext.at[:, lanes], held_v),
        (kvmem.at[:, lanes], held_mem.at[:, pl.ds(0, size)]),
        (kvmem.at[:, values], held_mem.at[:, pl.ds(size, size)]),
        (pt.at[j], held_pt),
    ]


def attention_backward(j, held, grad_ctx, gk, gv, gkm, gq):
    q, kext, vext, kvmem, pt = held
    groups = q.shape[0] // GROUP
    size = 64 * QUAD
    lanes = slice(size * j, size * (j + 1))
    gk[...] = jnp.zeros(gk.shape, f32)
    gv[...] = jnp.zeros(gv.shape, f32)
    gkm[...] = jnp.zeros(gkm.shape, f32)
    masks = head_masks()
    scale = 64**-0.5
    q_masks = [(m * scale).astype(bf16) for m in masks]
    c_masks = [m.astype(bf16) for m in masks]
    out_masks = [m * scale for m in masks]

    def step(g, carry):
        top = pl.multiple_of(g * GROUP, GROUP)
        keys = jnp.concatenate([kext[pl.ds(top, SPAN)], kvmem[:, :size]], axis=0)
        values = jnp.concatenate([vext[pl.ds(top, SPAN)], kvmem[:, size:]], axis=0)
        queries = stacked(q[pl.ds(top, GROUP)], q_masks)
        upstream = stacked(grad_ctx[pl.ds(top, GROUP), lanes], c_masks)
        weights = pt[g]
        wide = weights.astype(f32)
        gp = dot_nt(values, upstream)
        gs = (wide * (gp - colsum(gp * wide))).astype(bf16)
        gkeys = dot(gs, queries)
        gvalues = dot(weights, upstream)
        gk[pl.ds(top, SPAN)] += gkeys[:SPAN]
        gv[pl.ds(top, SPAN)] += gvalues[:SPAN]
        gkm[:, :size] += gkeys[SPAN:]
        gkm[:, size:] += gvalues[SPAN:]
        gq[pl.ds(top, GROUP)] = unstacked(dot_tn(gs, keys), out_masks).astype(bf16)
        return carry

    lax.fori_loop(0, groups, step, 0, unroll=6)


def bank_block(bank, width):
    return jnp.concatenate(
        [bank[0].astype(f32), jnp.zeros((16 - MEM, width), f32)], axis=0
    ).astype(bf16)


def pair_of(row):
    high = row.astype(bf16).astype(f32)
    zeros = jnp.zeros((14, row.shape[1]), f32)
    return jnp.concatenate([high, row - high, zeros], axis=0).astype(bf16)


def quad_kernel(j, ring, length, *refs):
    bank, grad_ctx, cols, vec_before, nt, w = refs[:6]
    held, refs = refs[6:11], refs[11:]
    width = nt.shape[0]
    size = 64 * QUAD
    first = width + 5 * size * j
    if j == 0:
        grad_att, ctx, *stored = refs[:7]
        refs = refs[7:]
    else:
        grads_before, refs = refs[0], refs[1:]
    gq, gk_rows, gv_rows, gk_left, gv_left, gbank, vec_grads = refs[:7]
    refs = refs[7:]
    if j == 0:
        more, grads, gk, gv, gkm, *rest = refs[:5], *refs[5:]
    else:
        n_out = 2 if ring else 1
        outs = refs[:n_out]
        gk, gv, gkm, grads = refs[n_out:]
    copies = []
    if j == 0:
        gat, sems = rest
        copies = start_all(quad_pairs(1, stored, more), sems)
        for start, count in row_tiles(length):
            rows = slice(start, start + count)
            gat[:, rows] = grad_att[rows].T
        grads[:, :width] = dot(gat[...], ctx[:length]).astype(bf16)
    attention_backward(j, held, grad_ctx, gk, gv, gkm, gq)
    gk_left[...] = gk[0:LEAD]
    gv_left[...] = gv[0:LEAD]
    gk_rows[...] = gk[LEAD : LEAD + length].astype(bf16)
    gv_rows[...] = gv[LEAD : LEAD + length].astype(bf16)
    gbank[...] = gkm[...].astype(bf16)

    gain, shift = cols[:, 0:1], cols[:, 1:2]
    gains, shifts = jnp.zeros((width, 1), f32), jnp.zeros((16, width), f32)
    sums = []
    for i, g in enumerate((gq[:length], gk_rows[...], gv_rows[...])):
        m = dot(nt[...], g)
        sums.append(colsum(g.astype(f32)))
        at = first + i * size
        grads[:, at : at + size] = (gain * m + shift * sums[i]).astype(bf16)
        own = slice(i * width + j * size, i * width + (j + 1) * size)
        gains += jnp.sum(w[:, own].astype(f32) * m, axis=1, keepdims=True)
        shifts += dot_nt(pair_of(sums[i]), w[:, own])
    at = first + 3 * size
    grads[:, at : at + 2 * size] = dot_tn(bank_block(bank, width), gbank[...]).astype(bf16)
    vec_grads[...] = vec_before[...]
    vec_grads[0:1] += jnp.transpose(jnp.broadcast_to(gains, (width, 128)))[0:1]
    vec_grads[1:2] += colsum(shifts)
    vec_grads[2:3, size * j : size * (j + 1)] = sums[0]
    vec_grads[3:4, size * j : size * (j + 1)] = sums[2]
    if j == 1:
        grads[:, :first] = grads_before[...]
        if ring:
            vectors = vec_grads[...]
            block = jnp.concatenate([vectors[:, :256], vectors[:, 256:]], axis=0).astype(bf16)
            grads[:, at + 2 * size :] = jnp.concatenate([block] * 16, axis=0)
        spread(ring, grads, outs)
    wait_all(copies)


def lower_kernel(length, *refs):
    frames, grad_res_in, vec, w = refs[:4]
    gq, gk, gv, gk_left, gv_left, gbank = ([refs[4 + i], refs[10 + i]] for i in range(6))
    grad_frames, grad_bank, grad_ck, grad_cv, grad_res, sems = refs[16:]
    width = frames.shape[1]
    part = gq[0].shape[1]
    copies = start_all([(grad_res_in, grad_res)], sems)
    grad_ck[0] = jnp.concatenate([v[...] for v in gk_left], axis=1)[LEAD - LEFT :]
    grad_cv[0] = jnp.concatenate([v[...] for v in gv_left], axis=1)[LEAD - LEFT :]
    bank_grads = jnp.concatenate(
        [v[:, at : at + part] for at in (0, part) for v in gbank], axis=1
    )
    grad_bank[0] = dot_nt(bank_grads, w[:, 3 * width : 5 * width])[:MEM]
    wait_all(copies)
    for start, size in row_tiles(length):
        rows = slice(start, start + size)
        parts = [jnp.concatenate([v[rows] for v in pair], axis=1) for pair in (gq, gk, gv)]
        e = (
            dot_nt(parts[0], w[:, :width])
            + dot_nt(parts[1], w[:, width : 2 * width])
            + dot_nt(parts[2], w[:, 2 * width : 3 * width])
        )
        n, s = centred(frames[rows].astype(f32))
        grad_frames[rows] = grad_res[rows] + norm_back(e, n, s, vec[0:1])


def pack_first_kernel(*refs):
    weights, vectors, inner_bias, out, main = refs[:7], refs[7:15], refs[15], refs[16], refs[17]
    held, bias_held, sems = refs[18:26], refs[26], refs[27]
    width = weights[0].shape[1]
    column = 0
    copies = []
    for ref in weights:
        copies.append((ref, out.at[:, pl.ds(column, ref.shape[1])]))
        column += ref.shape[1]
    copies += list(zip((*vectors, inner_bias), (*held, bias_held)))
    copies = [pltpu.make_async_copy(a, b, sems.at[i]) for i, (a, b) in enumerate(copies)]
    for copy in copies:
        copy.start()
    wait_all(copies)
    rank = lax.axis_index("fsdp")
    own = jnp.concatenate([ref[...].astype(f32) for ref in held], axis=0)
    part = own.shape[1]
    placed = jnp.where(
        lax.broadcasted_iota(jnp.int32, (8, width), 1) // part == rank,
        jnp.concatenate([own] * (width // part), axis=1),
        0.0,
    )
    bias = bias_held[...].astype(f32)
    count = bias.shape[1]
    row = lax.broadcasted_iota(jnp.int32, (4, width), 0)
    lane = lax.broadcasted_iota(jnp.int32, (4, width), 1)
    inner = jnp.where(
        (row * width + lane) // count == rank,
        jnp.concatenate([jnp.concatenate([bias] * (width // count), axis=1)] * 4, axis=0),
        0.0,
    )
    block = jnp.concatenate([placed, inner, jnp.zeros((4, width), f32)], axis=0)
    block = jnp.concatenate([block[:, : width // 2], block[:, width // 2 :]], axis=0)
    out[:, column:] = block.astype(bf16)
    common, third = shares(out.shape[1])
    main[:, :common] = out[:, :common]
    main[:, common:] = jnp.where(
        lax.axis_index("rep") == 0,
        out[:, common : common + third].astype(f32),
        out[:, common + third :].astype(f32),
    ).astype(bf16)


def first_sum_kernel(mine, other, *refs):
    right, left = refs[-2:]
    total = (mine[0].astype(f32) + other[0].astype(f32)).astype(bf16)
    half = right.shape[1]
    right[...] = total[:, :half]
    left[...] = total[:, half:]


def step_sum_kernel(mine_r, other_r, mine_l, other_l, a, b, *refs):
    right, left = refs[-2:]
    width = right.shape[1]
    wide_a, wide_b = a.shape[1], b.shape[1]
    to_right = mine_r[0].astype(f32) + other_r[0].astype(f32)
    to_left = mine_l[0].astype(f32) + other_l[0].astype(f32)
    right[:, :wide_a] = (to_right[:, :wide_a] + a[...].astype(f32)).astype(bf16)
    left[:, width - wide_b :] = (to_left[:, width - wide_b :] + b[...].astype(f32)).astype(bf16)
    if wide_a < width:
        right[:, wide_a:] = to_right[:, wide_a:].astype(bf16)
        left[:, : width - wide_b] = to_left[:, : width - wide_b].astype(bf16)


def last_sum_kernel(mine, other, a, b, *refs):
    refs[-1][...] = (
        mine[0].astype(f32) + other[0].astype(f32) + a[...].astype(f32) + b[...].astype(f32)
    ).astype(bf16)


def hold_kernel(*refs):
    pass


def hold(v, after):
    return pl.pallas_call(
        hold_kernel,
        out_shape=shape(v.shape, v.dtype),
        in_specs=[ANY] * (1 + len(after)),
        out_specs=ANY,
        input_output_aliases={0: 0},
        compiler_params=pltpu.CompilerParams(vmem_limit_bytes=2**20),
        cost_estimate=pl.CostEstimate(flops=0, bytes_accessed=0, transcendentals=0),
    )(v, *after)


def chunk_spec(width, index):
    return pl.BlockSpec((1, 32, width), lambda i: (index, 0, 0))


class Reduction:
    def __init__(self, mine, other, after=()):
        if after:
            other = hold(other, after)
        self.mine, self.other = mine, send(other, TO_CORE)
        self.width = mine.shape[2]
        self.distance = 4

    def sums(self, kernel, shapes, places, partial, after):
        args, specs = [], []
        for place in places:
            args += [self.mine, self.other]
            specs += [chunk_spec(self.width, place)] * 2
        return call(
            kernel,
            shapes,
            [VMEM] * len(shapes),
            [],
            [*args, *partial, *after],
            [*specs, *[VMEM] * len(partial), *[ANY] * len(after)],
            0.5,
            limit=8,
            grid=(1,),
        )

    def advance(self, after=()):
        width, s = self.width, self.distance
        full = shape((32, width), bf16)
        self.distance -= 1
        if s == 0:
            made = self.sums(last_sum_kernel, [full], [0], [self.a, self.b], after)
            self.total = made[0]
            self.far = lax.ppermute(self.total, "rep", [(0, 1), (1, 0)])
            return made
        if s == 4:
            half = halves(width)
            shapes = [shape((32, half), bf16), shape((32, width - half), bf16)]
            made = self.sums(first_sum_kernel, shapes, [4], [], after)
        else:
            made = self.sums(
                step_sum_kernel, [full, full], [s, 8 - s], [self.a, self.b], after
            )
        self.a, self.b = send(made[0], TO_RIGHT), send(made[1], TO_LEFT)
        return made

    def finish(self):
        while self.distance >= 0:
            self.advance()
        return self


def upper_result_kernel(both, both_far, inner_out, outer_out):
    total = both[...].astype(f32) + both_far[...].astype(f32)
    hidden = inner_out.shape[1]
    inner_out[...] = total[:, :hidden]
    outer_out[...] = total[:, hidden:]


def lower_result_kernel(near, far, *refs):
    q_out, k_out, v_out, m_out, output_out = refs[:5]
    vector_outs, inner_out = refs[5:13], refs[13]
    width = output_out.shape[1]
    part = 64 * QUAD
    total = near[...].astype(f32) + far[...].astype(f32)
    output_out[...] = total[:, :width]

    def group(j, i):
        at = width + (5 * j + i) * part
        return total[:, at : at + part]

    for i, out in enumerate((q_out, k_out, v_out)):
        for j in range(2):
            out[:, j * part : (j + 1) * part] = group(j, i)
    for i in range(2):
        for j in range(2):
            at = (2 * i + j) * part
            m_out[:, at : at + part] = group(j, 3 + i)
    block = total[:, width + 10 * part :]
    vectors = jnp.concatenate([block[:16], block[16:]], axis=1)
    rank = lax.axis_index("fsdp")
    quarter = lax.rem(rank, 4)

    def pick(v, index, size):
        found = jnp.zeros((v.shape[0], size), f32)
        for k in range(v.shape[1] // size):
            found += jnp.where(index == k, v[:, k * size : (k + 1) * size], 0.0)
        return found

    own = pick(pick(vectors[:8], lax.div(rank, 4), 128), quarter, 32)
    for i, out in enumerate(vector_outs):
        out[...] = own[i : i + 1]
    inner = pick(vectors[8:12], quarter, 128)
    found = jnp.zeros((1, 128), f32)
    for k in range(4):
        found += jnp.where(lax.div(rank, 4) == k, inner[k : k + 1], 0.0)
    inner_out[...] = found


def call(kernel, out_shapes, out_specs, scratch, args, specs, micros, limit=20, grid=()):
    specs = list(specs)
    args = [
        pltpu.with_memory_space_constraint(v, pltpu.HBM) if spec is HBM else v
        for v, spec in zip(args, specs)
    ]
    single = not isinstance(out_specs, (list, tuple))
    shapes = [out_shapes] if single else list(out_shapes)
    spaces = [out_specs] if single else list(out_specs)
    shapes = [
        pltpu.HBM(v.shape, v.dtype) if spec is HBM else v for v, spec in zip(shapes, spaces)
    ]
    return pl.pallas_call(
        kernel,
        grid=grid,
        out_shape=shapes[0] if single else tuple(shapes),
        in_specs=specs,
        out_specs=spaces[0] if single else tuple(spaces),
        scratch_shapes=scratch,
        compiler_params=pltpu.CompilerParams(vmem_limit_bytes=limit * 1024 * 1024),
        cost_estimate=pl.CostEstimate(
            flops=int(micros * 1.15e9), bytes_accessed=int(micros * 3.6e6), transcendentals=0
        ),
    )(*args)


def shape(dims, dtype):
    return jax.ShapeDtypeStruct(dims, dtype)


def per_device(ring, *args):
    (
        frames,
        memory_bank,
        cache_keys,
        cache_values,
        out_grad,
        first_gain,
        first_shift,
        query_weight,
        query_bias,
        key_weight,
        value_weight,
        value_bias,
        memory_weight,
        output_weight,
        output_bias,
        second_gain,
        second_shift,
        inner_weight,
        inner_bias,
        outer_weight,
        outer_bias,
    ) = args
    length, width = frames.shape
    ranks = width // first_gain.shape[0]
    part = width // ranks
    inner_part = inner_bias.shape[0]
    hidden = inner_part * ranks
    groups = -(-length // GROUP)
    padded = groups * GROUP
    extended = (groups - 1) * GROUP + SPAN
    quad = 64 * QUAD
    vectors = [
        first_gain,
        first_shift,
        query_bias,
        value_bias,
        output_bias,
        second_gain,
        second_shift,
        outer_bias,
    ]
    first = [query_weight, key_weight, value_weight, memory_weight]
    second = [output_weight.T, inner_weight, outer_weight.T]
    dma = pltpu.SemaphoreType.DMA
    row, wide_row = shape((length, width), bf16), shape((length, hidden), bf16)
    row_wide, vec_shape = shape((length, width), f32), shape((16, width), f32)
    turned = shape((width, length), bf16)

    def scratch_of(*shapes):
        return [pltpu.VMEM(v.shape, v.dtype) for v in shapes]

    if ring:
        total = 6 * width + 2 * hidden + 256
        weights, main = call(
            pack_first_kernel,
            (shape((part, total), bf16), shape((part, sum(shares(total))), bf16)),
            [VMEM] * 2,
            [
                *([pltpu.VMEM((1, part), bf16)] * 8),
                pltpu.VMEM((1, inner_part), bf16),
                pltpu.SemaphoreType.DMA((16,)),
            ],
            [
                *first,
                *second,
                *(v.reshape(1, part) for v in vectors),
                inner_bias.reshape(1, inner_part),
            ],
            [HBM] * 16,
            1,
            limit=8,
        )
        vec = jnp.zeros((16, width), f32)
    else:
        weights = jnp.concatenate(first + second, axis=1)
        vec = jnp.concatenate(
            [
                jnp.stack([lax.all_gather(v, "fsdp", axis=0, tiled=True) for v in vectors]),
                lax.all_gather(inner_bias, "fsdp", axis=0, tiled=True).reshape(-1, width),
                jnp.zeros((4, width), bf16),
            ],
            axis=0,
        ).astype(f32)
    normal, bias_grad, nt, gt = gated(
        functools.partial(prepare_kernel, length),
        (row_wide, vec_shape, turned, turned),
        [VMEM, VMEM, HBM, HBM],
        [*scratch_of(turned, turned), dma((2,))],
        [frames, out_grad],
        [VMEM] * 2,
        3,
        [weights],
    )
    if ring:
        items = ring_gather(weights, main, [bias_grad])
        early = [v for v in items if v[1] in (0, 1, 7)]
        late = [v for v in items if v[1] not in (0, 1, 7)]
        weights = whole_weights(late, width, whole_weights(early, width))
    else:
        weights = lax.all_gather(weights, "fsdp", axis=0, tiled=True)

    attended_shapes = (
        shape((padded, width), bf16),
        shape((extended, width), bf16),
        shape((extended, width), bf16),
        shape((16, 2 * width), bf16),
        shape((HEADS // QUAD, groups, KEYS, GROUP * QUAD), bf16),
    )
    held_shapes = (
        shape((padded, quad), bf16),
        shape((extended, quad), bf16),
        shape((extended, quad), bf16),
        shape((16, 2 * quad), bf16),
        shape((groups, KEYS, GROUP * QUAD), bf16),
    )
    *attended, ctx, vec, cols = call(
        functools.partial(attention_forward_kernel, ring, length),
        (
            *attended_shapes,
            shape((padded, width), bf16),
            vec_shape,
            shape((width, 16), f32),
        ),
        [HBM] * 5 + [VMEM] * 3,
        [
            *scratch_of(*attended_shapes),
            pltpu.VMEM((2, KEYS, GROUP * QUAD), f32),
            dma((5,)),
        ],
        [normal, memory_bank, cache_keys, cache_values, vec, weights],
        [VMEM] * 6,
        6,
    )

    def grad_shapes(w):
        if ring:
            return (shape((8, 32, w), bf16), shape((8, 32, w), bf16))
        return (shape((width, w), bf16),)

    grad_specs = [VMEM] * (2 if ring else 1)
    residual, normed2, active, slope, residual_far, active_far = call(
        functools.partial(inner_kernel, length),
        (row_wide, row, wide_row, wide_row, row_wide, wide_row),
        [VMEM] * 4 + [HBM] * 2,
        [dma((hidden // 512 + 1,))],
        [frames, ctx, vec, weights],
        [VMEM] * 4,
        7,
    )

    gi, vec_grads = call(
        functools.partial(grad_inner_kernel, length),
        (wide_row, vec_shape),
        [VMEM] * 2,
        [],
        [out_grad, slope, bias_grad, weights],
        [VMEM] * 4,
        3,
    )
    both_grads = call(
        functools.partial(hidden_weight_kernel, ring, length),
        grad_shapes(2 * hidden),
        grad_specs,
        [
            *scratch_of(turned, turned),
            pltpu.VMEM((width, 2 * hidden), bf16),
            dma((1,)),
        ],
        [normed2, gi, active, gt],
        [VMEM] * 3 + [HBM],
        4,
    )
    both = Reduction(*both_grads) if ring else None

    def steps(after, *reductions):
        made = []
        if ring:
            for reduction in reductions:
                made += reduction.advance([after])
        return made

    grad_att, grad_ctx, vec_grads, nt, *held, grad_res = gated(
        functools.partial(grad_residual_kernel, length),
        (row, shape((padded, width), bf16), vec_shape, turned, *held_shapes, row_wide),
        [VMEM] * 9 + [HBM],
        [*scratch_of(row_wide), dma((8,))],
        [gi, residual, out_grad, vec, vec_grads, weights, nt, *attended],
        [VMEM] * 6 + [HBM] * 6,
        4,
        both_grads[:1],
    )
    made = steps(vec_grads, both)
    part_row = shape((length, quad), bf16)
    left_row = shape((LEAD, quad), f32)
    quad_shapes = (
        shape((padded, quad), bf16),
        part_row,
        part_row,
        left_row,
        left_row,
        shape((16, 2 * quad), bf16),
    )
    quad_scratch = [
        pltpu.VMEM((extended, quad), f32),
        pltpu.VMEM((extended, quad), f32),
        pltpu.VMEM((16, 2 * quad), f32),
    ]
    results = gated(
        functools.partial(quad_kernel, 0, ring, length),
        (*quad_shapes, vec_shape, *held_shapes, shape((width, width + 5 * quad), bf16)),
        [VMEM] * 13,
        [
            *quad_scratch,
            *scratch_of(turned),
            dma((6,)),
        ],
        [memory_bank, grad_ctx, cols, vec_grads, nt, weights, *held, grad_att, ctx, *attended],
        [VMEM] * 13 + [HBM] * 5,
        6,
        made,
    )
    quad_one, vec_grads, held, one_grads = results[:6], results[6], results[7:12], results[12]
    made = steps(vec_grads, both)
    low_width = width + 10 * quad + (256 if ring else 0)
    results = gated(
        functools.partial(quad_kernel, 1, ring, length),
        (*quad_shapes, vec_shape, *grad_shapes(low_width)),
        [VMEM] * 7 + grad_specs,
        [*quad_scratch, pltpu.VMEM((width, low_width), bf16)],
        [memory_bank, grad_ctx, cols, vec_grads, nt, weights, *held, one_grads],
        [VMEM] * 12,
        6,
        made,
    )
    quad_two, vec_grads, low_grads = results[:6], results[6], results[7:]
    made = steps(vec_grads, both)
    low = Reduction(*low_grads, made) if ring else None
    output = gated(
        functools.partial(output_kernel, length),
        row,
        VMEM,
        [*scratch_of(wide_row, row_wide), dma((2,))],
        [active_far, residual_far, vec, weights],
        [HBM] * 2 + [VMEM] * 2,
        4,
        made,
    )
    made = steps(output, low)
    made += steps(made[0] if ring else output, both)
    made += steps(made[0] if ring else output, low)
    grad_frames, grad_bank, grad_ck, grad_cv = gated(
        functools.partial(lower_kernel, length),
        (
            row_wide,
            shape((1, MEM, width), f32),
            shape((1, LEFT, width), f32),
            shape((1, LEFT, width), f32),
        ),
        [VMEM] * 4,
        [*scratch_of(row_wide), dma((1,))],
        [frames, grad_res, vec, weights, *quad_one, *quad_two],
        [VMEM, HBM] + [VMEM] * 14,
        5,
        made,
    )
    made = steps(grad_bank, both)
    steps(made[0] if ring else grad_bank, low)
    if ring:
        for reduction in (both, low):
            reduction.finish()
        inner_sum, outer_sum = call(
            upper_result_kernel,
            (shape((part, hidden), f32), shape((part, hidden), f32)),
            [VMEM] * 2,
            [],
            [both.total, both.far],
            [VMEM] * 2,
            1,
            limit=8,
        )
        square = shape((part, width), f32)
        q_sum, k_sum, v_sum, m_sum, output_sum, *own = call(
            lower_result_kernel,
            (
                square,
                square,
                square,
                shape((part, 2 * width), f32),
                square,
                *([shape((1, part), f32)] * 8),
                shape((1, inner_part), f32),
            ),
            [VMEM] * 14,
            [],
            [low.total, low.far],
            [VMEM] * 2,
            1,
            limit=8,
        )
        own_inner = own[8].reshape(inner_part)
        own = [v.reshape(part) for v in own[:8]]
    else:

        def reduce(v):
            total = lax.psum_scatter(v, "fsdp", scatter_dimension=0, tiled=True)
            return lax.psum(total, "rep").astype(f32)

        total = reduce(both_grads[0])
        inner_sum, outer_sum = total[:, :hidden], total[:, hidden:]
        total = reduce(low_grads[0])
        output_sum = total[:, :width]
        sums = total[:, width:].reshape(part, 2, 5, quad)
        q_sum, k_sum, v_sum, m_low, m_high = (
            sums[:, :, i].reshape(part, 2 * quad) for i in range(5)
        )
        m_sum = jnp.concatenate([m_low, m_high], axis=1)
        vec_sum = lax.psum(vec_grads, ("rep", "fsdp"))
        rank = lax.axis_index("fsdp")
        own = lax.dynamic_slice(vec_sum[:8], (0, rank * part), (8, part))
        own_inner = lax.dynamic_slice(
            vec_sum[8:12].reshape(-1), (rank * inner_part,), (inner_part,)
        )
    return (
        output,
        grad_frames,
        grad_bank,
        grad_ck,
        grad_cv,
        own[0],
        own[1],
        q_sum,
        own[2],
        k_sum,
        v_sum,
        own[3],
        m_sum,
        output_sum.T,
        own[4],
        own[5],
        own[6],
        inner_sum,
        own_inner,
        outer_sum.T,
        own[7],
    )


def without_gates(kernel, n_args, n_gates, *refs):
    kernel(*refs[:n_args], *refs[n_args + n_gates :])


def gated(kernel, out_shapes, out_specs, scratch, args, specs, micros, made):
    return call(
        functools.partial(without_gates, kernel, len(args), len(made)),
        out_shapes,
        out_specs,
        scratch,
        [*args, *made],
        [*specs, *[ANY] * len(made)],
        micros,
    )


def solution(mesh):
    both = ("rep", "fsdp")
    rows, vector = P("fsdp", None), P("fsdp")
    columns = P(None, "fsdp")
    weights = (
        vector,
        vector,
        rows,
        vector,
        rows,
        rows,
        vector,
        rows,
        columns,
        vector,
        vector,
        vector,
        rows,
        vector,
        columns,
        vector,
    )
    blocks = P(both, None, None)
    in_specs = (P(both, None), blocks, blocks, blocks, P(both, None), *weights)
    out_specs = (P(both, None), P(both, None), blocks, blocks, blocks, *weights)
    ring = mesh.shape["fsdp"] == 16 and mesh.shape["rep"] == 2
    return jax.shard_map(
        functools.partial(per_device, ring),
        mesh=mesh,
        in_specs=in_specs,
        out_specs=out_specs,
        check_vma=False,
    )
```

```python
import functools

import jax
import jax.numpy as jnp
from jax import lax
from jax.experimental import pallas as pl
from jax.experimental.pallas import tpu as pltpu
from jax.sharding import PartitionSpec as P

HEADS = 8
SEG = 16
RIGHT = 4
LEFT = 30
MEM = 4

LEAD = 32
GROUP = 64
SPAN = 112
KEYS = 128
QUAD = 4
masked_value = -1e30
epsilon = 1e-05
gelu_a = 0.7978845608028654
gelu_b = gelu_a * 0.044715

bf16 = jnp.bfloat16
f32 = jnp.float32
VMEM = pl.BlockSpec(memory_space=pltpu.VMEM)
ANY = pl.BlockSpec(memory_space=pl.ANY)
HBM = pl.BlockSpec(memory_space=pltpu.HBM)


def dot(a, b):
    return lax.dot_general(a, b, (((1,), (0,)), ((), ())), preferred_element_type=f32)


def dot_nt(a, b):
    return lax.dot_general(a, b, (((1,), (1,)), ((), ())), preferred_element_type=f32)


def dot_tn(a, b):
    return lax.dot_general(a, b, (((0,), (0,)), ((), ())), preferred_element_type=f32)


def row_tiles(rows):
    return [(start, min(256, rows - start)) for start in range(0, rows, 256)]


def centred(v):
    center = v - jnp.mean(v, axis=-1, keepdims=True)
    spread = jnp.mean(center * center, axis=-1, keepdims=True)
    scale = lax.rsqrt(spread + epsilon)
    return center * scale, scale


def norm_back(e, n, scale, gain):
    eg = e * gain
    return scale * (
        eg - jnp.mean(eg, axis=-1, keepdims=True) - n * jnp.mean(eg * n, axis=-1, keepdims=True)
    )


def colsum(v):
    return jnp.sum(v, axis=0, keepdims=True)


RING = (0, 2, 4, 6, 7, 5, 3, 1)


def ring_pairs(step):
    pairs = []
    for k in range(8):
        for core in range(2):
            pairs.append((2 * RING[k] + core, 2 * RING[(k + step) % 8] + core))
    return pairs


TO_RIGHT, TO_LEFT = ring_pairs(1), ring_pairs(-1)
TO_CORE = [(i, i ^ 1) for i in range(16)]


def two_way(cross):
    pairs = []
    for k in range(8):
        pairs.append((2 * RING[k], 2 * RING[(k + 1) % 8] + cross))
        pairs.append((2 * RING[k] + 1, 2 * RING[(k - 1) % 8] + 1 - cross))
    return pairs


ALONG, ACROSS = two_way(0), two_way(1)


def ring_ids():
    rank = lax.axis_index("fsdp")
    core, chip = lax.rem(rank, 2), lax.div(rank, 2)
    z, x = lax.div(chip, 2), lax.rem(chip, 2)
    return jnp.where(x == 0, z, 7 - z), core


def ring_rank(position, core):
    position = lax.rem(position, 8)
    return 2 * jnp.where(position < 4, 2 * position, 15 - 2 * position) + core


def halves(width):
    return width // 2 // 128 * 128


def send(v, pairs):
    return lax.ppermute(v, "fsdp", pairs)


def across(v):
    return lax.ppermute(v, "rep", [(0, 1), (1, 0)])


def shares(width):
    third = width // 3 // 128 * 128
    return width - 2 * third, third


def ring_gather(shard, main, after):
    common, third = shares(shard.shape[1])
    got = [(shard, 0, "all")]
    a = b = main
    for step in (1, 2, 3):
        a, b = send(a, TO_RIGHT), send(b, TO_LEFT)
        pair = call(
            tails_kernel,
            shape((shard.shape[0], 2 * third), bf16),
            VMEM,
            [],
            [a, b],
            [VMEM] * 2,
            0.3,
            limit=4,
        )
        pair = across(pair)
        if step == 1:
            pair = hold(pair, after)
        got += [(a, 8 - step, "main"), (b, step, "main"), (pair, step, "pair")]
    a, b = send(a[:, :common], TO_RIGHT), send(b[:, common:], TO_LEFT)
    got += [(a, 4, "common"), (b, 4, "own"), (across(b), 4, "other")]
    return [(v, d, 0, k) for v, d, k in got] + [(send(v, TO_CORE), d, 1, k) for v, d, k in got]


def tails_kernel(a, b, *refs):
    out = refs[-1]
    third = out.shape[1] // 2
    out[:, :third] = a[:, a.shape[1] - third :]
    out[:, third:] = b[:, b.shape[1] - third :]


def lay_rows(places, has_before, *refs):
    refs, whole = refs[: len(places)], refs[-1]
    common, third = shares(whole.shape[1])
    position, core = ring_ids()
    replica = lax.axis_index("rep")
    own = pl.ds(pl.multiple_of(common + replica * third, 128), third)
    other = pl.ds(pl.multiple_of(common + (1 - replica) * third, 128), third)

    def rows(distance, flip):
        owner = ring_rank(position + distance, core if flip == 0 else 1 - core)
        return pl.ds(pl.multiple_of(owner * 32, 32), 32)

    for ref, (distance, flip, kind) in zip(refs, places):
        at = rows(distance, flip)
        if kind == "all":
            whole[at, :] = ref[...]
        elif kind == "main":
            whole[at, :common] = ref[:, :common]
            whole[at, own] = ref[:, common:]
        elif kind == "pair":
            whole[rows(8 - distance, flip), other] = ref[:, :third]
            whole[at, other] = ref[:, third:]
        elif kind == "common":
            whole[at, :common] = ref[...]
        else:
            whole[at, own if kind == "own" else other] = ref[...]


def whole_weights(items, width, before=None):
    places = tuple(item[1:] for item in items)
    arrays = [item[0] for item in items]
    kept = [] if before is None else [before]
    result = shape((width, arrays[0].shape[1] if before is None else before.shape[1]), bf16)
    return pl.pallas_call(
        functools.partial(lay_rows, places, bool(kept)),
        out_shape=result,
        in_specs=[VMEM] * len(arrays) + [VMEM] * len(kept),
        out_specs=VMEM,
        input_output_aliases={len(arrays): 0} if kept else {},
        compiler_params=pltpu.CompilerParams(vmem_limit_bytes=24 * 2**20),
        cost_estimate=pl.CostEstimate(flops=10**9, bytes_accessed=4 * 10**6, transcendentals=0),
    )(*arrays, *kept)


def spread(ring, grads, outs):
    if not ring:
        outs[0][...] = grads[...]
        return
    position, core = ring_ids()
    mine, mine_far, other, other_far = outs
    half = mine_far.shape[2]
    way = 1 - 2 * core

    def rows(place, k):
        return pl.ds(pl.multiple_of(ring_rank(place, k) * 32, 32), 32)

    def lanes(k):
        return pl.ds(pl.multiple_of(k * half, 128), half)

    for k in range(2):
        for distance in (3, 2, 1):
            at = 2 * (3 - distance) + k
            mine[at] = grads[rows(position + 8 + way * distance, k), :]
            other[at] = grads[rows(position + 8 - way * distance, k), :]
        mine_far[k] = grads[rows(position + 4, k), lanes(core)]
        other_far[k] = grads[rows(position + 4, k), lanes(1 - core)]
    mine[6] = grads[rows(position, core), :]
    other[6] = grads[rows(position, 1 - core), :]


def start_all(pairs, sems, first=0):
    copies = [pltpu.make_async_copy(a, b, sems.at[first + i]) for i, (a, b) in enumerate(pairs)]
    for copy in copies:
        copy.start()
    return copies


def wait_all(copies):
    for copy in copies:
        copy.wait()


def columns(width, hidden):
    return 5 * width, 6 * width, 6 * width + hidden, 6 * width + 2 * hidden


def head_masks():
    lane = lax.broadcasted_iota(jnp.int32, (1, 64 * QUAD), 1)
    return [(lane // 64 == h).astype(f32) for h in range(QUAD)]


def stacked(rows, masks):
    return jnp.concatenate([rows * m for m in masks], axis=0)


def unstacked(wide, masks):
    parts = [wide[GROUP * h : GROUP * (h + 1)] * masks[h] for h in range(QUAD)]
    return parts[0] + parts[1] + parts[2] + parts[3]


def added_mask(limit):
    row = lax.broadcasted_iota(jnp.int32, (KEYS, GROUP * QUAD), 0)
    query = lax.rem(lax.broadcasted_iota(jnp.int32, (KEYS, GROUP * QUAD), 1), GROUP)
    first = query // SEG * SEG + (LEAD - LEFT)
    inside = (row >= first) & (row < first + LEFT + SEG + RIGHT) & (row < limit)
    bank = (row >= SPAN) & (row < SPAN + MEM)
    return jnp.where((inside & (row < SPAN)) | bank, 0.0, masked_value)


def prepare_kernel(length, frames, out_grad, n_out, bias_out, nt_out, gt_out, nt, gt, sems):
    for start, size in row_tiles(length):
        rows = slice(start, start + size)
        n, _ = centred(frames[rows].astype(f32))
        n_out[rows] = n
        nt[:, rows] = n.astype(bf16).T
        gt[:, rows] = out_grad[rows].T
    copies = start_all([(nt, nt_out), (gt, gt_out)], sems)
    bias_out[...] = jnp.zeros(bias_out.shape, f32)
    bias_out[7:8] = colsum(out_grad[...].astype(f32))
    wait_all(copies)


def attention_forward_kernel(ring, length, *refs):
    normal, bank, cache_k, cache_v, vec, w = refs[:6]
    stored, (ctx, vec_out, cols_out) = refs[6:11], refs[11:14]
    q, kext, vext, kvmem, pt, mask, sems = refs[14:]
    width = normal.shape[1]
    groups = q.shape[0] // GROUP
    if not ring:
        vectors = vec[...]
    else:
        blocks = w[:, w.shape[1] - 256 :].astype(f32).reshape(16, 32, 256)
        total = jnp.sum(blocks, axis=0)
        vectors = jnp.concatenate([total[:16], total[16:]], axis=1)
    vec_out[...] = vectors
    cols_out[...] = vectors.T

    def left_rows(cache):
        rows = cache[0].astype(f32)
        return jnp.concatenate([jnp.zeros((LEAD - LEFT, width), f32), rows], axis=0).astype(bf16)

    kext[0:LEAD] = left_rows(cache_k)
    vext[0:LEAD] = left_rows(cache_v)
    tail = kext.shape[0] - LEAD - length
    kext[LEAD + length :] = jnp.zeros((tail, width), bf16)
    vext[LEAD + length :] = jnp.zeros((tail, width), bf16)
    q[length:] = jnp.zeros((q.shape[0] - length, width), bf16)
    bank_rows = jnp.concatenate(
        [bank[0].astype(f32), jnp.zeros((16 - MEM, width), f32)], axis=0
    ).astype(bf16)
    kvmem[...] = dot(bank_rows, w[:, 3 * width : 5 * width]).astype(bf16)

    for start, size in row_tiles(length):
        rows = (normal[start : start + size] * vectors[0:1] + vectors[1:2]).astype(bf16)
        q[start : start + size] = (dot(rows, w[:, :width]) + vectors[2:3]).astype(bf16)
        kext[LEAD + start : LEAD + start + size] = dot(rows, w[:, width : 2 * width]).astype(bf16)
        vext[LEAD + start : LEAD + start + size] = (
            dot(rows, w[:, 2 * width : 3 * width]) + vectors[3:4]
        ).astype(bf16)

    copies = start_all(zip((q, kext, vext, kvmem), stored), sems)
    masks = head_masks()
    scale = 64**-0.5
    q_masks = [(m * scale).astype(bf16) for m in masks]
    mask[0] = added_mask(KEYS)
    mask[1] = added_mask(LEAD + length - GROUP * (groups - 1))

    def step(g, carry):
        top = pl.multiple_of(g * GROUP, GROUP)
        hidden = mask[(g == groups - 1).astype(jnp.int32)]
        for j in range(HEADS // QUAD):
            lanes = slice(64 * QUAD * j, 64 * QUAD * (j + 1))
            keys = jnp.concatenate([kext[pl.ds(top, SPAN), lanes], kvmem[:, lanes]], axis=0)
            values = jnp.concatenate(
                [vext[pl.ds(top, SPAN), lanes], kvmem[:, width + lanes.start : width + lanes.stop]],
                axis=0,
            )
            queries = stacked(q[pl.ds(top, GROUP), lanes], q_masks)
            scores = dot_nt(keys, queries) + hidden
            raised = jnp.exp(scores - jnp.max(scores, axis=0, keepdims=True))
            weights = (raised / jnp.sum(raised, axis=0, keepdims=True)).astype(bf16)
            pt[j, g] = weights
            ctx[pl.ds(top, GROUP), lanes] = unstacked(dot_tn(weights, values), masks).astype(bf16)
        return carry

    lax.fori_loop(0, groups, step, 0, unroll=6)
    wait_all(copies + start_all([(pt, stored[4])], sems, 4))


def inner_kernel(length, *refs):
    frames, ctx, vec, w, residual, normed2, active, slope, residual_out, active_out, sems = refs
    width = frames.shape[1]
    hidden = active.shape[1]
    first, second, _, _ = columns(width, hidden)
    for start, size in row_tiles(length):
        rows = slice(start, start + size)
        res = frames[rows].astype(f32) + dot_nt(ctx[rows], w[:, first:second]) + vec[4:5]
        residual[rows] = res
        n, _ = centred(res)
        normed2[rows] = (n * vec[5:6] + vec[6:7]).astype(bf16)

    block = 512
    copies = start_all([(residual, residual_out)], sems, hidden // block)
    for b in range(hidden // block):
        cols = slice(b * block, (b + 1) * block)
        for start, size in row_tiles(length):
            rows = slice(start, start + size)
            u = dot(normed2[rows], w[:, second + cols.start : second + cols.stop]) + vec[8 + b : 9 + b]
            uu = u * u
            h = 0.5 + 0.5 * jnp.tanh(u * (gelu_a + gelu_b * uu))
            act = u * h
            active[rows, cols] = act.astype(bf16)
            slope[rows, cols] = (
                h + act * (1.0 - h) * (2 * gelu_a + 6 * gelu_b * uu)
            ).astype(bf16)
        part = pl.ds(b * block, block)
        copies += start_all([(active.at[:, part], active_out.at[:, part])], sems, b)
    wait_all(copies)


def grad_inner_kernel(length, out_grad, slope, vec_before, w, gi, vec_grads):
    width, hidden = out_grad.shape[1], slope.shape[1]
    third = columns(width, hidden)[2]
    block = 512
    vec_grads[...] = vec_before[...]
    for b in range(hidden // block):
        cols = slice(b * block, (b + 1) * block)
        sums = jnp.zeros((1, block), f32)
        for start, size in row_tiles(length):
            rows = slice(start, start + size)
            up = dot(out_grad[rows], w[:, third + cols.start : third + cols.stop])
            part = (up * slope[rows, cols].astype(f32)).astype(bf16)
            gi[rows, cols] = part
            sums += colsum(part.astype(f32))
        vec_grads[8 + b : 9 + b] = sums


def output_kernel(length, active_in, residual_in, vec, w, output, token, active, residual, sems):
    copies = start_all([(active_in, active), (residual_in, residual)], sems)
    _, _, third, last = columns(residual.shape[1], active.shape[1])
    token[...] = jnp.zeros(token.shape, f32)
    wait_all(copies)
    for start, size in row_tiles(length):
        rows = slice(start, start + size)
        output[rows] = (residual[rows] + dot_nt(active[rows], w[:, third:last]) + vec[7:8]).astype(bf16)


def hidden_weight_kernel(ring, length, *refs):
    normed2, gi, active, gt_in = refs[:4]
    outs, (n2t, gt, grads, sems) = refs[4:-4], refs[-4:]
    hidden = gi.shape[1]
    copies = start_all([(gt_in, gt)], sems)
    for start, size in row_tiles(length):
        rows = slice(start, start + size)
        n2t[:, rows] = normed2[rows].T
    for at in range(0, hidden, 512):
        grads[:, at : at + 512] = dot(n2t[...], gi[:, at : at + 512]).astype(bf16)
    wait_all(copies)
    for at in range(0, hidden, 512):
        cols = slice(hidden + at, hidden + at + 512)
        grads[:, cols] = dot(gt[...], active[:, at : at + 512]).astype(bf16)
    spread(ring, grads, outs)


def grad_residual_kernel(length, *refs):
    gi, residual, out_grad, vec, vec_before, w, nt_in, *stored = refs[:12]
    grad_att, grad_ctx, vec_grads, nt, *held = refs[12:21]
    grad_res_out, grad_res, sems = refs[21:]
    width = residual.shape[1]
    copies = start_all([(nt_in, nt), *quad_pairs(0, stored, held)], sems)
    first, second, third, _ = columns(width, gi.shape[1])
    sums = [jnp.zeros((1, width), f32) for _ in range(3)]
    for start, size in row_tiles(length):
        rows = slice(start, start + size)
        e = dot_nt(gi[rows], w[:, second:third])
        n, scale = centred(residual[rows])
        gres = out_grad[rows].astype(f32) + norm_back(e, n, scale, vec[5:6])
        grad_res[rows] = gres
        copies += start_all([(grad_res.at[rows], grad_res_out.at[rows])], sems, 7 + start // 256)
        gat_rows = gres.astype(bf16)
        grad_att[rows] = gat_rows
        grad_ctx[rows] = dot(gat_rows, w[:, first:second]).astype(bf16)
        sums = [s + colsum(v) for s, v in zip(sums, (gat_rows.astype(f32), e * n, e))]
    grad_ctx[length:] = jnp.zeros((grad_ctx.shape[0] - length, width), bf16)
    vec_grads[...] = vec_before[...]
    for i in range(3):
        vec_grads[4 + i : 5 + i] = sums[i]
    wait_all(copies)


def quad_pairs(j, stored, held):
    q, kext, vext, kvmem, pt = stored
    held_q, held_k, held_v, held_mem, held_pt = held
    size = 64 * QUAD
    width = q.shape[1]
    lanes, values = pl.ds(j * size, size), pl.ds(width + j * size, size)
    return [
        (q.at[:, lanes], held_q),
        (kext.at[:, lanes], held_k),
        (vext.at[:, lanes], held_v),
        (kvmem.at[:, lanes], held_mem.at[:, pl.ds(0, size)]),
        (kvmem.at[:, values], held_mem.at[:, pl.ds(size, size)]),
        (pt.at[j], held_pt),
    ]


def attention_backward(j, held, grad_ctx, gk, gv, gkm, gq):
    q, kext, vext, kvmem, pt = held
    groups = q.shape[0] // GROUP
    size = 64 * QUAD
    lanes = slice(size * j, size * (j + 1))
    gk[...] = jnp.zeros(gk.shape, f32)
    gv[...] = jnp.zeros(gv.shape, f32)
    gkm[...] = jnp.zeros(gkm.shape, f32)
    masks = head_masks()
    scale = 64**-0.5
    q_masks = [(m * scale).astype(bf16) for m in masks]
    c_masks = [m.astype(bf16) for m in masks]
    out_masks = [m * scale for m in masks]

    def step(g, carry):
        top = pl.multiple_of(g * GROUP, GROUP)
        keys = jnp.concatenate([kext[pl.ds(top, SPAN)], kvmem[:, :size]], axis=0)
        values = jnp.concatenate([vext[pl.ds(top, SPAN)], kvmem[:, size:]], axis=0)
        queries = stacked(q[pl.ds(top, GROUP)], q_masks)
        upstream = stacked(grad_ctx[pl.ds(top, GROUP), lanes], c_masks)
        weights = pt[g]
        wide = weights.astype(f32)
        gp = dot_nt(values, upstream)
        gs = (wide * (gp - colsum(gp * wide))).astype(bf16)
        gkeys = dot(gs, queries)
        gvalues = dot(weights, upstream)
        gk[pl.ds(top, SPAN)] += gkeys[:SPAN]
        gv[pl.ds(top, SPAN)] += gvalues[:SPAN]
        gkm[:, :size] += gkeys[SPAN:]
        gkm[:, size:] += gvalues[SPAN:]
        gq[pl.ds(top, GROUP)] = unstacked(dot_tn(gs, keys), out_masks).astype(bf16)
        return carry

    lax.fori_loop(0, groups, step, 0, unroll=6)


def bank_block(bank, width):
    return jnp.concatenate(
        [bank[0].astype(f32), jnp.zeros((16 - MEM, width), f32)], axis=0
    ).astype(bf16)


def pair_of(row):
    high = row.astype(bf16).astype(f32)
    zeros = jnp.zeros((14, row.shape[1]), f32)
    return jnp.concatenate([high, row - high, zeros], axis=0).astype(bf16)


def quad_kernel(j, ring, length, *refs):
    bank, grad_ctx, cols, vec_before, nt, w = refs[:6]
    held, refs = refs[6:11], refs[11:]
    width = nt.shape[0]
    size = 64 * QUAD
    first = width * (1 - j)
    if j == 0:
        grad_att, ctx, *stored = refs[:7]
        refs = refs[7:]
    gq, gk_rows, gv_rows, gk_left, gv_left, gbank, vec_grads = refs[:7]
    refs = refs[7:]
    if j == 0:
        more, refs = refs[:5], refs[5:]
    n_out = 4 if ring else 1
    outs = refs[:n_out]
    gk, gv, gkm, grads, *rest = refs[n_out:]
    copies = []
    if j == 0:
        gat, sems = rest
        copies = start_all(quad_pairs(1, stored, more), sems)
        for start, count in row_tiles(length):
            rows = slice(start, start + count)
            gat[:, rows] = grad_att[rows].T
        grads[:, :width] = dot(gat[...], ctx[:length]).astype(bf16)
    attention_backward(j, held, grad_ctx, gk, gv, gkm, gq)
    gk_left[...] = gk[0:LEAD]
    gv_left[...] = gv[0:LEAD]
    gk_rows[...] = gk[LEAD : LEAD + length].astype(bf16)
    gv_rows[...] = gv[LEAD : LEAD + length].astype(bf16)
    gbank[...] = gkm[...].astype(bf16)

    gain, shift = cols[:, 0:1], cols[:, 1:2]
    gains, shifts = jnp.zeros((width, 1), f32), jnp.zeros((16, width), f32)
    sums = []
    for i, g in enumerate((gq[:length], gk_rows[...], gv_rows[...])):
        m = dot(nt[...], g)
        sums.append(colsum(g.astype(f32)))
        at = first + i * size
        grads[:, at : at + size] = (gain * m + shift * sums[i]).astype(bf16)
        own = slice(i * width + j * size, i * width + (j + 1) * size)
        gains += jnp.sum(w[:, own].astype(f32) * m, axis=1, keepdims=True)
        shifts += dot_nt(pair_of(sums[i]), w[:, own])
    at = first + 3 * size
    grads[:, at : at + 2 * size] = dot_tn(bank_block(bank, width), gbank[...]).astype(bf16)
    vec_grads[...] = vec_before[...]
    vec_grads[0:1] += jnp.transpose(jnp.broadcast_to(gains, (width, 128)))[0:1]
    vec_grads[1:2] += colsum(shifts)
    vec_grads[2:3, size * j : size * (j + 1)] = sums[0]
    vec_grads[3:4, size * j : size * (j + 1)] = sums[2]
    if j == 1 and ring:
        vectors = vec_grads[...]
        block = jnp.concatenate([vectors[:, :256], vectors[:, 256:]], axis=0).astype(bf16)
        grads[:, at + 2 * size :] = jnp.concatenate([block] * 16, axis=0)
    spread(ring, grads, outs)
    wait_all(copies)


def lower_kernel(length, *refs):
    frames, grad_res_in, vec, w = refs[:4]
    gq, gk, gv, gk_left, gv_left, gbank = ([refs[4 + i], refs[10 + i]] for i in range(6))
    grad_frames, grad_bank, grad_ck, grad_cv, token, grad_res, sems = refs[16:]
    token[...] = jnp.zeros(token.shape, f32)
    width = frames.shape[1]
    part = gq[0].shape[1]
    copies = start_all([(grad_res_in, grad_res)], sems)
    grad_ck[0] = jnp.concatenate([v[...] for v in gk_left], axis=1)[LEAD - LEFT :]
    grad_cv[0] = jnp.concatenate([v[...] for v in gv_left], axis=1)[LEAD - LEFT :]
    bank_grads = jnp.concatenate(
        [v[:, at : at + part] for at in (0, part) for v in gbank], axis=1
    )
    grad_bank[0] = dot_nt(bank_grads, w[:, 3 * width : 5 * width])[:MEM]
    wait_all(copies)
    for start, size in row_tiles(length):
        rows = slice(start, start + size)
        parts = [jnp.concatenate([v[rows] for v in pair], axis=1) for pair in (gq, gk, gv)]
        e = (
            dot_nt(parts[0], w[:, :width])
            + dot_nt(parts[1], w[:, width : 2 * width])
            + dot_nt(parts[2], w[:, 2 * width : 3 * width])
        )
        n, s = centred(frames[rows].astype(f32))
        grad_frames[rows] = grad_res[rows] + norm_back(e, n, s, vec[0:1])


def pack_first_kernel(*refs):
    weights, vectors, inner_bias, out, main = refs[:7], refs[7:15], refs[15], refs[16], refs[17]
    held, bias_held, sems = refs[18:26], refs[26], refs[27]
    width = weights[0].shape[1]
    column = 0
    copies = []
    for ref in weights:
        copies.append((ref, out.at[:, pl.ds(column, ref.shape[1])]))
        column += ref.shape[1]
    copies += list(zip((*vectors, inner_bias), (*held, bias_held)))
    copies = [pltpu.make_async_copy(a, b, sems.at[i]) for i, (a, b) in enumerate(copies)]
    for copy in copies:
        copy.start()
    wait_all(copies)
    rank = lax.axis_index("fsdp")
    own = jnp.concatenate([ref[...].astype(f32) for ref in held], axis=0)
    part = own.shape[1]
    placed = jnp.where(
        lax.broadcasted_iota(jnp.int32, (8, width), 1) // part == rank,
        jnp.concatenate([own] * (width // part), axis=1),
        0.0,
    )
    bias = bias_held[...].astype(f32)
    count = bias.shape[1]
    row = lax.broadcasted_iota(jnp.int32, (4, width), 0)
    lane = lax.broadcasted_iota(jnp.int32, (4, width), 1)
    inner = jnp.where(
        (row * width + lane) // count == rank,
        jnp.concatenate([jnp.concatenate([bias] * (width // count), axis=1)] * 4, axis=0),
        0.0,
    )
    block = jnp.concatenate([placed, inner, jnp.zeros((4, width), f32)], axis=0)
    block = jnp.concatenate([block[:, : width // 2], block[:, width // 2 :]], axis=0)
    out[:, column:] = block.astype(bf16)
    common, third = shares(out.shape[1])
    main[:, :common] = out[:, :common]
    main[:, common:] = jnp.where(
        lax.axis_index("rep") == 0,
        out[:, common : common + third].astype(f32),
        out[:, common + third :].astype(f32),
    ).astype(bf16)


def first_sum_kernel(mine, other, *refs):
    refs[-1][...] = (mine[...].astype(f32) + other[...].astype(f32)).astype(bf16)


def step_sum_kernel(far, mine_0, other_0, mine_1, other_1, come, *refs):
    out = refs[-1]
    _, core = ring_ids()
    half = come.shape[2]
    for k, (mine, other) in enumerate(((mine_0, other_0), (mine_1, other_1))):
        own = mine[0].astype(f32) + other[0].astype(f32)
        if far:
            here = core == 0
            come_k = come[k].astype(f32)
            out[k, :, :half] = (own[:, :half] + jnp.where(here, come_k, 0.0)).astype(bf16)
            out[k, :, half:] = (own[:, half:] + jnp.where(here, 0.0, come_k)).astype(bf16)
        else:
            out[k] = (own + come[k].astype(f32)).astype(bf16)


def near_sum_kernel(mine_0, other_0, mine_1, other_1, come, *refs):
    same, crossed = refs[-2:]
    _, core = ring_ids()
    first = mine_0[0].astype(f32) + other_0[0].astype(f32) + come[0].astype(f32)
    second = mine_1[0].astype(f32) + other_1[0].astype(f32) + come[1].astype(f32)
    same[...] = jnp.where(core == 0, first, second).astype(bf16)
    crossed[...] = jnp.where(core == 0, second, first).astype(bf16)


def last_sum_kernel(mine, other, a, b, *refs):
    refs[-1][...] = (
        mine[0].astype(f32) + other[0].astype(f32) + a[...].astype(f32) + b[...].astype(f32)
    ).astype(bf16)


def hold_kernel(*refs):
    pass


def hold(v, after):
    return pl.pallas_call(
        hold_kernel,
        out_shape=shape(v.shape, v.dtype),
        in_specs=[ANY] * (1 + len(after)),
        out_specs=ANY,
        input_output_aliases={0: 0},
        compiler_params=pltpu.CompilerParams(vmem_limit_bytes=2**20),
        cost_estimate=pl.CostEstimate(flops=0, bytes_accessed=0, transcendentals=0),
    )(v, *after)


def chunk_spec(width, index):
    return pl.BlockSpec((1, 32, width), lambda i: (index, 0, 0))


class Reduction:
    def __init__(self, mine, mine_far, other, other_far, after=()):
        self.mine, self.mine_far = mine, mine_far
        other_far = hold(other_far, after) if after else other_far
        self.other, self.other_far = other, send(other_far, TO_CORE)
        self.width = mine.shape[2]
        self.distance = 4

    def follow(self, after=()):
        self.other = send(hold(self.other, after) if after else self.other, TO_CORE)
        return self

    def sums(self, kernel, shapes, places, partial, after):
        args, specs = [], []
        for place in places:
            args += [self.mine, self.other]
            specs += [chunk_spec(self.width, place)] * 2
        return call(
            kernel,
            shapes,
            [VMEM] * len(shapes),
            [],
            [*args, *partial, *after],
            [*specs, *[VMEM] * len(partial), *[ANY] * len(after)],
            0.5,
            limit=8,
            grid=(1,),
        )

    def advance(self, after=()):
        s = self.distance
        rows, pair = shape((32, self.width), bf16), shape((2, 32, self.width), bf16)
        places = [2 * (3 - s), 2 * (3 - s) + 1]
        self.distance -= 1
        if s == 0:
            made = self.sums(last_sum_kernel, [rows], [6], self.come, after)
            self.total = made[0]
            self.far = across(self.total)
        elif s == 4:
            made = self.sums(
                first_sum_kernel,
                [shape(self.mine_far.shape, bf16)],
                [],
                [self.mine_far, self.other_far],
                after,
            )
            self.come = [send(made[0], ALONG)]
        elif s > 1:
            kernel = functools.partial(step_sum_kernel, s == 3)
            made = self.sums(kernel, [pair], places, self.come, after)
            self.come = [send(made[0], ALONG)]
        else:
            made = self.sums(near_sum_kernel, [rows, rows], places, self.come, after)
            self.come = [send(made[0], ALONG), send(made[1], ACROSS)]
        return made

    def finish(self):
        while self.distance >= 0:
            self.advance()
        return self


def upper_result_kernel(both, both_far, inner_out, outer_out, token):
    token[...] = jnp.zeros(token.shape, f32)
    total = both[...].astype(f32) + both_far[...].astype(f32)
    hidden = inner_out.shape[1]
    inner_out[...] = total[:, :hidden]
    outer_out[...] = total[:, hidden:]


def lower_result_kernel(one, one_far, two, two_far, *refs):
    q_out, k_out, v_out, m_out, output_out = refs[:5]
    vector_outs, inner_out = refs[5:13], refs[13]
    width = output_out.shape[1]
    part = 64 * QUAD
    total = one[...].astype(f32) + one_far[...].astype(f32)
    output_out[...] = total[:, :width]
    pair = [total[:, width:], two[...].astype(f32) + two_far[...].astype(f32)]
    for i, out in enumerate((q_out, k_out, v_out)):
        for j in range(2):
            out[:, j * part : (j + 1) * part] = pair[j][:, i * part : (i + 1) * part]
    for i in range(2):
        for j in range(2):
            at = (2 * i + j) * part
            m_out[:, at : at + part] = pair[j][:, (3 + i) * part : (4 + i) * part]
    block = pair[1][:, 5 * part :]
    vectors = jnp.concatenate([block[:16], block[16:]], axis=1)
    rank = lax.axis_index("fsdp")
    quarter = lax.rem(rank, 4)

    def pick(v, index, size):
        found = jnp.zeros((v.shape[0], size), f32)
        for k in range(v.shape[1] // size):
            found += jnp.where(index == k, v[:, k * size : (k + 1) * size], 0.0)
        return found

    own = pick(pick(vectors[:8], lax.div(rank, 4), 128), quarter, 32)
    for i, out in enumerate(vector_outs):
        out[...] = own[i : i + 1]
    inner = pick(vectors[8:12], quarter, 128)
    found = jnp.zeros((1, 128), f32)
    for k in range(4):
        found += jnp.where(lax.div(rank, 4) == k, inner[k : k + 1], 0.0)
    inner_out[...] = found


def call(kernel, out_shapes, out_specs, scratch, args, specs, micros, limit=20, grid=()):
    specs = list(specs)
    args = [
        pltpu.with_memory_space_constraint(v, pltpu.HBM) if spec is HBM else v
        for v, spec in zip(args, specs)
    ]
    single = not isinstance(out_specs, (list, tuple))
    shapes = [out_shapes] if single else list(out_shapes)
    spaces = [out_specs] if single else list(out_specs)
    shapes = [
        pltpu.HBM(v.shape, v.dtype) if spec is HBM else v for v, spec in zip(shapes, spaces)
    ]
    return pl.pallas_call(
        kernel,
        grid=grid,
        out_shape=shapes[0] if single else tuple(shapes),
        in_specs=specs,
        out_specs=spaces[0] if single else tuple(spaces),
        scratch_shapes=scratch,
        compiler_params=pltpu.CompilerParams(vmem_limit_bytes=limit * 1024 * 1024),
        cost_estimate=pl.CostEstimate(
            flops=int(micros * 1.15e9), bytes_accessed=int(micros * 3.6e6), transcendentals=0
        ),
    )(*args)


def shape(dims, dtype):
    return jax.ShapeDtypeStruct(dims, dtype)


def per_device(ring, *args):
    (
        frames,
        memory_bank,
        cache_keys,
        cache_values,
        out_grad,
        first_gain,
        first_shift,
        query_weight,
        query_bias,
        key_weight,
        value_weight,
        value_bias,
        memory_weight,
        output_weight,
        output_bias,
        second_gain,
        second_shift,
        inner_weight,
        inner_bias,
        outer_weight,
        outer_bias,
    ) = args
    length, width = frames.shape
    ranks = width // first_gain.shape[0]
    part = width // ranks
    inner_part = inner_bias.shape[0]
    hidden = inner_part * ranks
    groups = -(-length // GROUP)
    padded = groups * GROUP
    extended = (groups - 1) * GROUP + SPAN
    quad = 64 * QUAD
    vectors = [
        first_gain,
        first_shift,
        query_bias,
        value_bias,
        output_bias,
        second_gain,
        second_shift,
        outer_bias,
    ]
    first = [query_weight, key_weight, value_weight, memory_weight]
    second = [output_weight.T, inner_weight, outer_weight.T]
    dma = pltpu.SemaphoreType.DMA
    row, wide_row = shape((length, width), bf16), shape((length, hidden), bf16)
    row_wide, vec_shape = shape((length, width), f32), shape((16, width), f32)
    turned = shape((width, length), bf16)

    def scratch_of(*shapes):
        return [pltpu.VMEM(v.shape, v.dtype) for v in shapes]

    if ring:
        total = 6 * width + 2 * hidden + 256
        weights, main = call(
            pack_first_kernel,
            (shape((part, total), bf16), shape((part, sum(shares(total))), bf16)),
            [VMEM] * 2,
            [
                *([pltpu.VMEM((1, part), bf16)] * 8),
                pltpu.VMEM((1, inner_part), bf16),
                pltpu.SemaphoreType.DMA((16,)),
            ],
            [
                *first,
                *second,
                *(v.reshape(1, part) for v in vectors),
                inner_bias.reshape(1, inner_part),
            ],
            [HBM] * 16,
            1,
            limit=8,
        )
        vec = jnp.zeros((16, width), f32)
    else:
        weights = jnp.concatenate(first + second, axis=1)
        vec = jnp.concatenate(
            [
                jnp.stack([lax.all_gather(v, "fsdp", axis=0, tiled=True) for v in vectors]),
                lax.all_gather(inner_bias, "fsdp", axis=0, tiled=True).reshape(-1, width),
                jnp.zeros((4, width), bf16),
            ],
            axis=0,
        ).astype(f32)
    normal, bias_grad, nt, gt = gated(
        functools.partial(prepare_kernel, length),
        (row_wide, vec_shape, turned, turned),
        [VMEM, VMEM, HBM, HBM],
        [*scratch_of(turned, turned), dma((2,))],
        [frames, out_grad],
        [VMEM] * 2,
        3,
        [weights],
    )
    if ring:
        items = ring_gather(weights, main, [bias_grad])
        early = [v for v in items if v[1] in (0, 1, 7)]
        late = [v for v in items if v[1] not in (0, 1, 7)]
        weights = whole_weights(late, width, whole_weights(early, width))
    else:
        weights = lax.all_gather(weights, "fsdp", axis=0, tiled=True)

    attended_shapes = (
        shape((padded, width), bf16),
        shape((extended, width), bf16),
        shape((extended, width), bf16),
        shape((16, 2 * width), bf16),
        shape((HEADS // QUAD, groups, KEYS, GROUP * QUAD), bf16),
    )
    held_shapes = (
        shape((padded, quad), bf16),
        shape((extended, quad), bf16),
        shape((extended, quad), bf16),
        shape((16, 2 * quad), bf16),
        shape((groups, KEYS, GROUP * QUAD), bf16),
    )
    *attended, ctx, vec, cols = call(
        functools.partial(attention_forward_kernel, ring, length),
        (
            *attended_shapes,
            shape((padded, width), bf16),
            vec_shape,
            shape((width, 16), f32),
        ),
        [HBM] * 5 + [VMEM] * 3,
        [
            *scratch_of(*attended_shapes),
            pltpu.VMEM((2, KEYS, GROUP * QUAD), f32),
            dma((5,)),
        ],
        [normal, memory_bank, cache_keys, cache_values, vec, weights],
        [VMEM] * 6,
        6,
    )

    def grad_shapes(w):
        if ring:
            dims = [(7, 32, w), (2, 32, w // 2)]
            return tuple(shape(v, bf16) for v in dims + dims)
        return (shape((width, w), bf16),)

    grad_specs = [VMEM] * (4 if ring else 1)
    token_shape = shape((8, 128), f32)
    residual, normed2, active, slope, residual_far, active_far = call(
        functools.partial(inner_kernel, length),
        (row_wide, row, wide_row, wide_row, row_wide, wide_row),
        [VMEM] * 4 + [HBM] * 2,
        [dma((hidden // 512 + 1,))],
        [frames, ctx, vec, weights],
        [VMEM] * 4,
        7,
    )

    gi, vec_grads = call(
        functools.partial(grad_inner_kernel, length),
        (wide_row, vec_shape),
        [VMEM] * 2,
        [],
        [out_grad, slope, bias_grad, weights],
        [VMEM] * 4,
        3,
    )
    both_grads = call(
        functools.partial(hidden_weight_kernel, ring, length),
        grad_shapes(2 * hidden),
        grad_specs,
        [
            *scratch_of(turned, turned),
            pltpu.VMEM((width, 2 * hidden), bf16),
            dma((1,)),
        ],
        [normed2, gi, active, gt],
        [VMEM] * 3 + [HBM],
        4,
    )
    both = Reduction(*both_grads).follow() if ring else None

    def steps(after, *reductions):
        made = []
        if ring:
            for reduction in reductions:
                made += reduction.advance([after])
        return made

    grad_att, grad_ctx, vec_grads, nt, *held, grad_res = gated(
        functools.partial(grad_residual_kernel, length),
        (row, shape((padded, width), bf16), vec_shape, turned, *held_shapes, row_wide),
        [VMEM] * 9 + [HBM],
        [*scratch_of(row_wide), dma((10,))],
        [gi, residual, out_grad, vec, vec_grads, weights, nt, *attended],
        [VMEM] * 6 + [HBM] * 6,
        4,
        both_grads[:1],
    )
    made = steps(vec_grads, both)
    part_row = shape((length, quad), bf16)
    left_row = shape((LEAD, quad), f32)
    quad_shapes = (
        shape((padded, quad), bf16),
        part_row,
        part_row,
        left_row,
        left_row,
        shape((16, 2 * quad), bf16),
    )
    quad_scratch = [
        pltpu.VMEM((extended, quad), f32),
        pltpu.VMEM((extended, quad), f32),
        pltpu.VMEM((16, 2 * quad), f32),
    ]
    results = gated(
        functools.partial(quad_kernel, 0, ring, length),
        (*quad_shapes, vec_shape, *held_shapes, *grad_shapes(width + 5 * quad)),
        [VMEM] * 12 + grad_specs,
        [
            *quad_scratch,
            pltpu.VMEM((width, width + 5 * quad), bf16),
            *scratch_of(turned),
            dma((6,)),
        ],
        [memory_bank, grad_ctx, cols, vec_grads, nt, weights, *held, grad_att, ctx, *attended],
        [VMEM] * 13 + [HBM] * 5,
        6,
        made,
    )
    quad_one, vec_grads, held, one_grads = results[:6], results[6], results[7:12], results[12:]
    made = steps(vec_grads, both)
    one = Reduction(*one_grads, after=made).follow(made) if ring else None
    two_width = 5 * quad + (256 if ring else 0)
    results = gated(
        functools.partial(quad_kernel, 1, ring, length),
        (*quad_shapes, vec_shape, *grad_shapes(two_width)),
        [VMEM] * 7 + grad_specs,
        [*quad_scratch, pltpu.VMEM((width, two_width), bf16)],
        [memory_bank, grad_ctx, cols, vec_grads, nt, weights, *held],
        [VMEM] * 11,
        6,
        made,
    )
    quad_two, vec_grads, two_grads = results[:6], results[6], results[7:]
    two = Reduction(*two_grads) if ring else None
    made = steps(vec_grads, both)
    made += steps(vec_grads, one)
    if ring:
        two.follow(made[:1])
    made = steps(made[-1] if ring else vec_grads, two)
    output, token = gated(
        functools.partial(output_kernel, length),
        (row, token_shape),
        [VMEM] * 2,
        [*scratch_of(wide_row, row_wide), dma((2,))],
        [active_far, residual_far, vec, weights],
        [HBM] * 2 + [VMEM] * 2,
        4,
        made,
    )
    made = steps(token, one, two)
    made += steps(made[0] if ring else token, both)
    grad_frames, grad_bank, grad_ck, grad_cv, token = gated(
        functools.partial(lower_kernel, length),
        (
            row_wide,
            shape((1, MEM, width), f32),
            shape((1, LEFT, width), f32),
            shape((1, LEFT, width), f32),
            token_shape,
        ),
        [VMEM] * 5,
        [*scratch_of(row_wide), dma((1,))],
        [frames, grad_res, vec, weights, *quad_one, *quad_two],
        [VMEM, HBM] + [VMEM] * 14,
        5,
        made,
    )
    if ring:
        made = steps(token, one, two)
        both.advance(made)
        inner_sum, outer_sum, token = call(
            upper_result_kernel,
            (shape((part, hidden), f32), shape((part, hidden), f32), token_shape),
            [VMEM] * 3,
            [],
            [both.total, both.far],
            [VMEM] * 2,
            1,
            limit=8,
        )
        one.advance()
        two.advance([token])
        one.finish()
        two.finish()
        square = shape((part, width), f32)
        q_sum, k_sum, v_sum, m_sum, output_sum, *own = call(
            lower_result_kernel,
            (
                square,
                square,
                square,
                shape((part, 2 * width), f32),
                square,
                *([shape((1, part), f32)] * 8),
                shape((1, inner_part), f32),
            ),
            [VMEM] * 14,
            [],
            [one.total, one.far, two.total, two.far],
            [VMEM] * 4,
            1,
            limit=8,
        )
        own_inner = own[8].reshape(inner_part)
        own = [v.reshape(part) for v in own[:8]]
    else:

        def reduce(v):
            total = lax.psum_scatter(v, "fsdp", scatter_dimension=0, tiled=True)
            return lax.psum(total, "rep").astype(f32)

        total = reduce(both_grads[0])
        inner_sum, outer_sum = total[:, :hidden], total[:, hidden:]
        low, high = reduce(one_grads[0]), reduce(two_grads[0])
        output_sum = low[:, :width]
        sums = [v.reshape(part, 5, quad) for v in (low[:, width:], high)]
        q_sum, k_sum, v_sum, m_low, m_high = (
            jnp.concatenate([v[:, i] for v in sums], axis=1) for i in range(5)
        )
        m_sum = jnp.concatenate([m_low, m_high], axis=1)
        vec_sum = lax.psum(vec_grads, ("rep", "fsdp"))
        rank = lax.axis_index("fsdp")
        own = lax.dynamic_slice(vec_sum[:8], (0, rank * part), (8, part))
        own_inner = lax.dynamic_slice(
            vec_sum[8:12].reshape(-1), (rank * inner_part,), (inner_part,)
        )
    return (
        output,
        grad_frames,
        grad_bank,
        grad_ck,
        grad_cv,
        own[0],
        own[1],
        q_sum,
        own[2],
        k_sum,
        v_sum,
        own[3],
        m_sum,
        output_sum.T,
        own[4],
        own[5],
        own[6],
        inner_sum,
        own_inner,
        outer_sum.T,
        own[7],
    )


def without_gates(kernel, n_args, n_gates, *refs):
    kernel(*refs[:n_args], *refs[n_args + n_gates :])


def gated(kernel, out_shapes, out_specs, scratch, args, specs, micros, made):
    return call(
        functools.partial(without_gates, kernel, len(args), len(made)),
        out_shapes,
        out_specs,
        scratch,
        [*args, *made],
        [*specs, *[ANY] * len(made)],
        micros,
    )


def solution(mesh):
    both = ("rep", "fsdp")
    rows, vector = P("fsdp", None), P("fsdp")
    columns = P(None, "fsdp")
    weights = (
        vector,
        vector,
        rows,
        vector,
        rows,
        rows,
        vector,
        rows,
        columns,
        vector,
        vector,
        vector,
        rows,
        vector,
        columns,
        vector,
    )
    blocks = P(both, None, None)
    in_specs = (P(both, None), blocks, blocks, blocks, P(both, None), *weights)
    out_specs = (P(both, None), P(both, None), blocks, blocks, blocks, *weights)
    ring = mesh.shape["fsdp"] == 16 and mesh.shape["rep"] == 2
    return jax.shard_map(
        functools.partial(per_device, ring),
        mesh=mesh,
        in_specs=in_specs,
        out_specs=out_specs,
        check_vma=False,
    )
```

```python
import functools

import jax
import jax.numpy as jnp
from jax import lax
from jax.experimental import pallas as pl
from jax.experimental.pallas import tpu as pltpu
from jax.sharding import PartitionSpec as P

HEADS = 8
SEG = 16
RIGHT = 4
LEFT = 30
MEM = 4

LEAD = 32
GROUP = 64
SPAN = 112
KEYS = 128
QUAD = 4
masked_value = -1e30
epsilon = 1e-05
gelu_a = 0.7978845608028654
gelu_b = gelu_a * 0.044715

bf16 = jnp.bfloat16
f32 = jnp.float32
VMEM = pl.BlockSpec(memory_space=pltpu.VMEM)
ANY = pl.BlockSpec(memory_space=pl.ANY)
HBM = pl.BlockSpec(memory_space=pltpu.HBM)


def dot(a, b):
    return lax.dot_general(a, b, (((1,), (0,)), ((), ())), preferred_element_type=f32)


def dot_nt(a, b):
    return lax.dot_general(a, b, (((1,), (1,)), ((), ())), preferred_element_type=f32)


def dot_tn(a, b):
    return lax.dot_general(a, b, (((0,), (0,)), ((), ())), preferred_element_type=f32)


def row_tiles(rows):
    return [(start, min(256, rows - start)) for start in range(0, rows, 256)]


def centred(v):
    center = v - jnp.mean(v, axis=-1, keepdims=True)
    spread = jnp.mean(center * center, axis=-1, keepdims=True)
    scale = lax.rsqrt(spread + epsilon)
    return center * scale, scale


def norm_back(e, n, scale, gain):
    eg = e * gain
    return scale * (
        eg - jnp.mean(eg, axis=-1, keepdims=True) - n * jnp.mean(eg * n, axis=-1, keepdims=True)
    )


def colsum(v):
    return jnp.sum(v, axis=0, keepdims=True)


RING = (0, 2, 4, 6, 7, 5, 3, 1)


def ring_pairs(step):
    pairs = []
    for k in range(8):
        for core in range(2):
            pairs.append((2 * RING[k] + core, 2 * RING[(k + step) % 8] + core))
    return pairs


TO_RIGHT, TO_LEFT = ring_pairs(1), ring_pairs(-1)
TO_CORE = [(i, i ^ 1) for i in range(16)]


def two_way(cross):
    pairs = []
    for k in range(8):
        pairs.append((2 * RING[k], 2 * RING[(k + 1) % 8] + cross))
        pairs.append((2 * RING[k] + 1, 2 * RING[(k - 1) % 8] + 1 - cross))
    return pairs


ALONG, ACROSS = two_way(0), two_way(1)


def ring_ids():
    rank = lax.axis_index("fsdp")
    core, chip = lax.rem(rank, 2), lax.div(rank, 2)
    z, x = lax.div(chip, 2), lax.rem(chip, 2)
    return jnp.where(x == 0, z, 7 - z), core


def ring_rank(position, core):
    position = lax.rem(position, 8)
    return 2 * jnp.where(position < 4, 2 * position, 15 - 2 * position) + core


def halves(width):
    return width // 2 // 128 * 128


def send(v, pairs):
    return lax.ppermute(v, "fsdp", pairs)


def across(v):
    return lax.ppermute(v, "rep", [(0, 1), (1, 0)])


def shares(width):
    third = width // 3 // 128 * 128
    return width - 2 * third, third


def ring_gather(shard, main, after):
    common, third = shares(shard.shape[1])
    got = [(shard, 0, "all")]
    a = b = main
    for step in (1, 2, 3):
        a, b = send(a, TO_RIGHT), send(b, TO_LEFT)
        pair = call(
            tails_kernel,
            shape((shard.shape[0], 2 * third), bf16),
            VMEM,
            [],
            [a, b],
            [VMEM] * 2,
            0.3,
            limit=4,
        )
        pair = across(pair)
        if step == 1:
            pair = hold(pair, after)
        got += [(a, 8 - step, "main"), (b, step, "main"), (pair, step, "pair")]
    a, b = send(a[:, :common], TO_RIGHT), send(b[:, common:], TO_LEFT)
    got += [(a, 4, "common"), (b, 4, "own"), (across(b), 4, "other")]
    return [(v, d, 0, k) for v, d, k in got] + [(send(v, TO_CORE), d, 1, k) for v, d, k in got]


def tails_kernel(a, b, *refs):
    out = refs[-1]
    third = out.shape[1] // 2
    out[:, :third] = a[:, a.shape[1] - third :]
    out[:, third:] = b[:, b.shape[1] - third :]


def lay_rows(places, has_before, *refs):
    refs, whole = refs[: len(places)], refs[-1]
    common, third = shares(whole.shape[1])
    position, core = ring_ids()
    replica = lax.axis_index("rep")
    own = pl.ds(pl.multiple_of(common + replica * third, 128), third)
    other = pl.ds(pl.multiple_of(common + (1 - replica) * third, 128), third)

    def rows(distance, flip):
        owner = ring_rank(position + distance, core if flip == 0 else 1 - core)
        return pl.ds(pl.multiple_of(owner * 32, 32), 32)

    for ref, (distance, flip, kind) in zip(refs, places):
        at = rows(distance, flip)
        if kind == "all":
            whole[at, :] = ref[...]
        elif kind == "main":
            whole[at, :common] = ref[:, :common]
            whole[at, own] = ref[:, common:]
        elif kind == "pair":
            whole[rows(8 - distance, flip), other] = ref[:, :third]
            whole[at, other] = ref[:, third:]
        elif kind == "common":
            whole[at, :common] = ref[...]
        else:
            whole[at, own if kind == "own" else other] = ref[...]


def whole_weights(items, width, before=None):
    places = tuple(item[1:] for item in items)
    arrays = [item[0] for item in items]
    kept = [] if before is None else [before]
    result = shape((width, arrays[0].shape[1] if before is None else before.shape[1]), bf16)
    return pl.pallas_call(
        functools.partial(lay_rows, places, bool(kept)),
        out_shape=result,
        in_specs=[VMEM] * len(arrays) + [VMEM] * len(kept),
        out_specs=VMEM,
        input_output_aliases={len(arrays): 0} if kept else {},
        compiler_params=pltpu.CompilerParams(vmem_limit_bytes=24 * 2**20),
        cost_estimate=pl.CostEstimate(flops=10**9, bytes_accessed=4 * 10**6, transcendentals=0),
    )(*arrays, *kept)


def spread(ring, grads, outs):
    if not ring:
        outs[0][...] = grads[...]
        return
    position, core = ring_ids()
    mine, mine_far, other, other_far = outs
    half = mine_far.shape[2]
    way = 1 - 2 * core

    def rows(place, k):
        return pl.ds(pl.multiple_of(ring_rank(place, k) * 32, 32), 32)

    def lanes(k):
        return pl.ds(pl.multiple_of(k * half, 128), half)

    for k in range(2):
        for distance in (3, 2, 1):
            at = 2 * (3 - distance) + k
            mine[at] = grads[rows(position + 8 + way * distance, k), :]
            other[at] = grads[rows(position + 8 - way * distance, k), :]
        mine_far[k] = grads[rows(position + 4, k), lanes(core)]
        other_far[k] = grads[rows(position + 4, k), lanes(1 - core)]
    mine[6] = grads[rows(position, core), :]
    other[6] = grads[rows(position, 1 - core), :]


def start_all(pairs, sems, first=0):
    copies = [pltpu.make_async_copy(a, b, sems.at[first + i]) for i, (a, b) in enumerate(pairs)]
    for copy in copies:
        copy.start()
    return copies


def wait_all(copies):
    for copy in copies:
        copy.wait()


def columns(width, hidden):
    return 5 * width, 6 * width, 6 * width + hidden, 6 * width + 2 * hidden


def head_masks():
    lane = lax.broadcasted_iota(jnp.int32, (1, 64 * QUAD), 1)
    return [(lane // 64 == h).astype(f32) for h in range(QUAD)]


def stacked(rows, masks):
    return jnp.concatenate([rows * m for m in masks], axis=0)


def unstacked(wide, masks):
    parts = [wide[GROUP * h : GROUP * (h + 1)] * masks[h] for h in range(QUAD)]
    return parts[0] + parts[1] + parts[2] + parts[3]


def added_mask(limit):
    row = lax.broadcasted_iota(jnp.int32, (KEYS, GROUP * QUAD), 0)
    query = lax.rem(lax.broadcasted_iota(jnp.int32, (KEYS, GROUP * QUAD), 1), GROUP)
    first = query // SEG * SEG + (LEAD - LEFT)
    inside = (row >= first) & (row < first + LEFT + SEG + RIGHT) & (row < limit)
    bank = (row >= SPAN) & (row < SPAN + MEM)
    return jnp.where((inside & (row < SPAN)) | bank, 0.0, masked_value)


def prepare_kernel(length, frames, out_grad, n_out, bias_out, nt_out, gt_out, nt, gt, sems):
    for start, size in row_tiles(length):
        rows = slice(start, start + size)
        n, _ = centred(frames[rows].astype(f32))
        n_out[rows] = n
        nt[:, rows] = n.astype(bf16).T
        gt[:, rows] = out_grad[rows].T
    copies = start_all([(nt, nt_out), (gt, gt_out)], sems)
    bias_out[...] = jnp.zeros(bias_out.shape, f32)
    bias_out[7:8] = colsum(out_grad[...].astype(f32))
    wait_all(copies)


def attention_forward_kernel(ring, length, *refs):
    normal, bank, cache_k, cache_v, vec, w = refs[:6]
    q, kext, vext, kvmem, pt, ctx, vec_out, cols_out, mask = refs[6:]
    width = normal.shape[1]
    groups = q.shape[0] // GROUP
    if not ring:
        vectors = vec[...]
    else:
        blocks = w[:, w.shape[1] - 256 :].astype(f32).reshape(16, 32, 256)
        total = jnp.sum(blocks, axis=0)
        vectors = jnp.concatenate([total[:16], total[16:]], axis=1)
    vec_out[...] = vectors
    cols_out[...] = vectors.T

    def left_rows(cache):
        rows = cache[0].astype(f32)
        return jnp.concatenate([jnp.zeros((LEAD - LEFT, width), f32), rows], axis=0).astype(bf16)

    kext[0:LEAD] = left_rows(cache_k)
    vext[0:LEAD] = left_rows(cache_v)
    tail = kext.shape[0] - LEAD - length
    kext[LEAD + length :] = jnp.zeros((tail, width), bf16)
    vext[LEAD + length :] = jnp.zeros((tail, width), bf16)
    q[length:] = jnp.zeros((q.shape[0] - length, width), bf16)
    bank_rows = jnp.concatenate(
        [bank[0].astype(f32), jnp.zeros((16 - MEM, width), f32)], axis=0
    ).astype(bf16)
    kvmem[...] = dot(bank_rows, w[:, 3 * width : 5 * width]).astype(bf16)

    for start, size in row_tiles(length):
        rows = (normal[start : start + size] * vectors[0:1] + vectors[1:2]).astype(bf16)
        q[start : start + size] = (dot(rows, w[:, :width]) + vectors[2:3]).astype(bf16)
        kext[LEAD + start : LEAD + start + size] = dot(rows, w[:, width : 2 * width]).astype(bf16)
        vext[LEAD + start : LEAD + start + size] = (
            dot(rows, w[:, 2 * width : 3 * width]) + vectors[3:4]
        ).astype(bf16)

    masks = head_masks()
    scale = 64**-0.5
    q_masks = [(m * scale).astype(bf16) for m in masks]
    mask[0] = added_mask(KEYS)
    mask[1] = added_mask(LEAD + length - GROUP * (groups - 1))

    def step(g, carry):
        top = pl.multiple_of(g * GROUP, GROUP)
        hidden = mask[(g == groups - 1).astype(jnp.int32)]
        for j in range(HEADS // QUAD):
            lanes = slice(64 * QUAD * j, 64 * QUAD * (j + 1))
            keys = jnp.concatenate([kext[pl.ds(top, SPAN), lanes], kvmem[:, lanes]], axis=0)
            values = jnp.concatenate(
                [vext[pl.ds(top, SPAN), lanes], kvmem[:, width + lanes.start : width + lanes.stop]],
                axis=0,
            )
            queries = stacked(q[pl.ds(top, GROUP), lanes], q_masks)
            scores = dot_nt(keys, queries) + hidden
            raised = jnp.exp(scores - jnp.max(scores, axis=0, keepdims=True))
            weights = (raised / jnp.sum(raised, axis=0, keepdims=True)).astype(bf16)
            pt[j, g] = weights
            ctx[pl.ds(top, GROUP), lanes] = unstacked(dot_tn(weights, values), masks).astype(bf16)
        return carry

    lax.fori_loop(0, groups, step, 0, unroll=6)


def inner_kernel(length, *refs):
    frames, ctx, vec, w, residual, normed2, active, slope = refs
    width = frames.shape[1]
    hidden = active.shape[1]
    first, second, _, _ = columns(width, hidden)
    for start, size in row_tiles(length):
        rows = slice(start, start + size)
        res = frames[rows].astype(f32) + dot_nt(ctx[rows], w[:, first:second]) + vec[4:5]
        residual[rows] = res
        n, _ = centred(res)
        normed2[rows] = (n * vec[5:6] + vec[6:7]).astype(bf16)

    block = 512
    for b in range(hidden // block):
        cols = slice(b * block, (b + 1) * block)
        for start, size in row_tiles(length):
            rows = slice(start, start + size)
            u = dot(normed2[rows], w[:, second + cols.start : second + cols.stop]) + vec[8 + b : 9 + b]
            uu = u * u
            h = 0.5 + 0.5 * jnp.tanh(u * (gelu_a + gelu_b * uu))
            act = u * h
            active[rows, cols] = act.astype(bf16)
            slope[rows, cols] = (
                h + act * (1.0 - h) * (2 * gelu_a + 6 * gelu_b * uu)
            ).astype(bf16)


def grad_inner_kernel(length, out_grad, slope, vec_before, w, gi, vec_grads):
    width, hidden = out_grad.shape[1], slope.shape[1]
    third = columns(width, hidden)[2]
    block = 512
    vec_grads[...] = vec_before[...]
    for b in range(hidden // block):
        cols = slice(b * block, (b + 1) * block)
        sums = jnp.zeros((1, block), f32)
        for start, size in row_tiles(length):
            rows = slice(start, start + size)
            up = dot(out_grad[rows], w[:, third + cols.start : third + cols.stop])
            part = (up * slope[rows, cols].astype(f32)).astype(bf16)
            gi[rows, cols] = part
            sums += colsum(part.astype(f32))
        vec_grads[8 + b : 9 + b] = sums


def output_kernel(length, active, residual, vec, w, output, token):
    _, _, third, last = columns(residual.shape[1], active.shape[1])
    token[...] = jnp.zeros(token.shape, f32)
    for start, size in row_tiles(length):
        rows = slice(start, start + size)
        output[rows] = (residual[rows] + dot_nt(active[rows], w[:, third:last]) + vec[7:8]).astype(bf16)


def hidden_weight_kernel(ring, length, *refs):
    normed2, gi, active, gt_in = refs[:4]
    outs, (n2t, gt, grads, sems) = refs[4:-4], refs[-4:]
    hidden = gi.shape[1]
    copies = start_all([(gt_in, gt)], sems)
    for start, size in row_tiles(length):
        rows = slice(start, start + size)
        n2t[:, rows] = normed2[rows].T
    for at in range(0, hidden, 512):
        grads[:, at : at + 512] = dot(n2t[...], gi[:, at : at + 512]).astype(bf16)
    wait_all(copies)
    for at in range(0, hidden, 512):
        cols = slice(hidden + at, hidden + at + 512)
        grads[:, cols] = dot(gt[...], active[:, at : at + 512]).astype(bf16)
    spread(ring, grads, outs)


def grad_residual_kernel(length, *refs):
    gi, residual, out_grad, vec, vec_before, w, nt_in = refs[:7]
    grad_att, grad_ctx, vec_grads, nt, grad_res, sems = refs[7:]
    width = residual.shape[1]
    copies = start_all([(nt_in, nt)], sems)
    first, second, third, _ = columns(width, gi.shape[1])
    sums = [jnp.zeros((1, width), f32) for _ in range(3)]
    for start, size in row_tiles(length):
        rows = slice(start, start + size)
        e = dot_nt(gi[rows], w[:, second:third])
        n, scale = centred(residual[rows])
        gres = out_grad[rows].astype(f32) + norm_back(e, n, scale, vec[5:6])
        grad_res[rows] = gres
        gat_rows = gres.astype(bf16)
        grad_att[rows] = gat_rows
        grad_ctx[rows] = dot(gat_rows, w[:, first:second]).astype(bf16)
        sums = [s + colsum(v) for s, v in zip(sums, (gat_rows.astype(f32), e * n, e))]
    grad_ctx[length:] = jnp.zeros((grad_ctx.shape[0] - length, width), bf16)
    vec_grads[...] = vec_before[...]
    for i in range(3):
        vec_grads[4 + i : 5 + i] = sums[i]
    wait_all(copies)


def attention_backward(j, attended, grad_ctx, gk, gv, gkm, gq):
    q, kext, vext, kvmem, pt = attended
    width = q.shape[1]
    groups = q.shape[0] // GROUP
    size = 64 * QUAD
    lanes = slice(size * j, size * (j + 1))
    value_lanes = slice(width + size * j, width + size * (j + 1))
    gk[...] = jnp.zeros(gk.shape, f32)
    gv[...] = jnp.zeros(gv.shape, f32)
    gkm[...] = jnp.zeros(gkm.shape, f32)
    masks = head_masks()
    scale = 64**-0.5
    q_masks = [(m * scale).astype(bf16) for m in masks]
    c_masks = [m.astype(bf16) for m in masks]
    out_masks = [m * scale for m in masks]

    def step(g, carry):
        top = pl.multiple_of(g * GROUP, GROUP)
        keys = jnp.concatenate([kext[pl.ds(top, SPAN), lanes], kvmem[:, lanes]], axis=0)
        values = jnp.concatenate([vext[pl.ds(top, SPAN), lanes], kvmem[:, value_lanes]], axis=0)
        queries = stacked(q[pl.ds(top, GROUP), lanes], q_masks)
        upstream = stacked(grad_ctx[pl.ds(top, GROUP), lanes], c_masks)
        weights = pt[j, g]
        wide = weights.astype(f32)
        gp = dot_nt(values, upstream)
        gs = (wide * (gp - colsum(gp * wide))).astype(bf16)
        gkeys = dot(gs, queries)
        gvalues = dot(weights, upstream)
        gk[pl.ds(top, SPAN)] += gkeys[:SPAN]
        gv[pl.ds(top, SPAN)] += gvalues[:SPAN]
        gkm[:, :size] += gkeys[SPAN:]
        gkm[:, size:] += gvalues[SPAN:]
        gq[pl.ds(top, GROUP)] = unstacked(dot_tn(gs, keys), out_masks).astype(bf16)
        return carry

    lax.fori_loop(0, groups, step, 0, unroll=6)


def bank_block(bank, width):
    return jnp.concatenate(
        [bank[0].astype(f32), jnp.zeros((16 - MEM, width), f32)], axis=0
    ).astype(bf16)


def pair_of(row):
    high = row.astype(bf16).astype(f32)
    zeros = jnp.zeros((14, row.shape[1]), f32)
    return jnp.concatenate([high, row - high, zeros], axis=0).astype(bf16)


def quad_kernel(j, ring, length, *refs):
    bank, grad_ctx, cols, vec_before, nt, w = refs[:6]
    attended, refs = refs[6:11], refs[11:]
    width = nt.shape[0]
    size = 64 * QUAD
    first = width * (1 - j)
    if j == 0:
        grad_att, ctx = refs[:2]
        refs = refs[2:]
    gq, gk_rows, gv_rows, gk_left, gv_left, gbank, vec_grads = refs[:7]
    refs = refs[7:]
    n_out = 4 if ring else 1
    outs = refs[:n_out]
    gk, gv, gkm, grads, *rest = refs[n_out:]
    if j == 0:
        gat = rest[0]
        for start, count in row_tiles(length):
            rows = slice(start, start + count)
            gat[:, rows] = grad_att[rows].T
        grads[:, :width] = dot(gat[...], ctx[:length]).astype(bf16)
    attention_backward(j, attended, grad_ctx, gk, gv, gkm, gq)
    gk_left[...] = gk[0:LEAD]
    gv_left[...] = gv[0:LEAD]
    gk_rows[...] = gk[LEAD : LEAD + length].astype(bf16)
    gv_rows[...] = gv[LEAD : LEAD + length].astype(bf16)
    gbank[...] = gkm[...].astype(bf16)

    gain, shift = cols[:, 0:1], cols[:, 1:2]
    gains, shifts = jnp.zeros((width, 1), f32), jnp.zeros((16, width), f32)
    sums = []
    for i, g in enumerate((gq[:length], gk_rows[...], gv_rows[...])):
        m = dot(nt[...], g)
        sums.append(colsum(g.astype(f32)))
        at = first + i * size
        grads[:, at : at + size] = (gain * m + shift * sums[i]).astype(bf16)
        own = slice(i * width + j * size, i * width + (j + 1) * size)
        gains += jnp.sum(w[:, own].astype(f32) * m, axis=1, keepdims=True)
        shifts += dot_nt(pair_of(sums[i]), w[:, own])
    at = first + 3 * size
    grads[:, at : at + 2 * size] = dot_tn(bank_block(bank, width), gbank[...]).astype(bf16)
    vec_grads[...] = vec_before[...]
    vec_grads[0:1] += jnp.transpose(jnp.broadcast_to(gains, (width, 128)))[0:1]
    vec_grads[1:2] += colsum(shifts)
    vec_grads[2:3, size * j : size * (j + 1)] = sums[0]
    vec_grads[3:4, size * j : size * (j + 1)] = sums[2]
    if j == 1 and ring:
        vectors = vec_grads[...]
        block = jnp.concatenate([vectors[:, :256], vectors[:, 256:]], axis=0).astype(bf16)
        grads[:, at + 2 * size :] = jnp.concatenate([block] * 16, axis=0)
    spread(ring, grads, outs)


def lower_kernel(length, *refs):
    frames, grad_res, vec, w = refs[:4]
    gq, gk, gv, gk_left, gv_left, gbank = ([refs[4 + i], refs[10 + i]] for i in range(6))
    grad_frames, grad_bank, grad_ck, grad_cv, token = refs[16:]
    token[...] = jnp.zeros(token.shape, f32)
    width = frames.shape[1]
    part = gq[0].shape[1]
    for out, parts in ((grad_ck, gk_left), (grad_cv, gv_left)):
        left = jnp.concatenate([v[...] for v in parts], axis=1)
        for row in range(LEFT):
            out[row] = left[LEAD - LEFT + row : LEAD - LEFT + row + 1]
    bank_grads = jnp.concatenate(
        [v[:, at : at + part] for at in (0, part) for v in gbank], axis=1
    )
    grad_bank[0] = dot_nt(bank_grads, w[:, 3 * width : 5 * width])[:MEM]
    for start, size in row_tiles(length):
        rows = slice(start, start + size)
        parts = [jnp.concatenate([v[rows] for v in pair], axis=1) for pair in (gq, gk, gv)]
        e = (
            dot_nt(parts[0], w[:, :width])
            + dot_nt(parts[1], w[:, width : 2 * width])
            + dot_nt(parts[2], w[:, 2 * width : 3 * width])
        )
        n, s = centred(frames[rows].astype(f32))
        grad_frames[rows] = grad_res[rows] + norm_back(e, n, s, vec[0:1])


def pack_first_kernel(*refs):
    weights, vectors, inner_bias, out, main = refs[:7], refs[7:15], refs[15], refs[16], refs[17]
    held, bias_held, sems = refs[18:26], refs[26], refs[27]
    width = weights[0].shape[1]
    column = 0
    copies = []
    for ref in weights:
        copies.append((ref, out.at[:, pl.ds(column, ref.shape[1])]))
        column += ref.shape[1]
    copies += list(zip((*vectors, inner_bias), (*held, bias_held)))
    copies = [pltpu.make_async_copy(a, b, sems.at[i]) for i, (a, b) in enumerate(copies)]
    for copy in copies:
        copy.start()
    wait_all(copies)
    rank = lax.axis_index("fsdp")
    own = jnp.concatenate([ref[...].astype(f32) for ref in held], axis=0)
    part = own.shape[1]
    placed = jnp.where(
        lax.broadcasted_iota(jnp.int32, (8, width), 1) // part == rank,
        jnp.concatenate([own] * (width // part), axis=1),
        0.0,
    )
    bias = bias_held[...].astype(f32)
    count = bias.shape[1]
    row = lax.broadcasted_iota(jnp.int32, (4, width), 0)
    lane = lax.broadcasted_iota(jnp.int32, (4, width), 1)
    inner = jnp.where(
        (row * width + lane) // count == rank,
        jnp.concatenate([jnp.concatenate([bias] * (width // count), axis=1)] * 4, axis=0),
        0.0,
    )
    block = jnp.concatenate([placed, inner, jnp.zeros((4, width), f32)], axis=0)
    block = jnp.concatenate([block[:, : width // 2], block[:, width // 2 :]], axis=0)
    out[:, column:] = block.astype(bf16)
    common, third = shares(out.shape[1])
    main[:, :common] = out[:, :common]
    main[:, common:] = jnp.where(
        lax.axis_index("rep") == 0,
        out[:, common : common + third].astype(f32),
        out[:, common + third :].astype(f32),
    ).astype(bf16)


def first_sum_kernel(mine, other, *refs):
    refs[-1][...] = (mine[...].astype(f32) + other[...].astype(f32)).astype(bf16)


def step_sum_kernel(far, mine_0, other_0, mine_1, other_1, come, *refs):
    out = refs[-1]
    _, core = ring_ids()
    half = come.shape[2]
    for k, (mine, other) in enumerate(((mine_0, other_0), (mine_1, other_1))):
        own = mine[0].astype(f32) + other[0].astype(f32)
        if far:
            here = core == 0
            come_k = come[k].astype(f32)
            out[k, :, :half] = (own[:, :half] + jnp.where(here, come_k, 0.0)).astype(bf16)
            out[k, :, half:] = (own[:, half:] + jnp.where(here, 0.0, come_k)).astype(bf16)
        else:
            out[k] = (own + come[k].astype(f32)).astype(bf16)


def near_sum_kernel(mine_0, other_0, mine_1, other_1, come, *refs):
    same, crossed = refs[-2:]
    _, core = ring_ids()
    first = mine_0[0].astype(f32) + other_0[0].astype(f32) + come[0].astype(f32)
    second = mine_1[0].astype(f32) + other_1[0].astype(f32) + come[1].astype(f32)
    same[...] = jnp.where(core == 0, first, second).astype(bf16)
    crossed[...] = jnp.where(core == 0, second, first).astype(bf16)


def last_sum_kernel(mine, other, a, b, *refs):
    refs[-1][...] = (
        mine[0].astype(f32) + other[0].astype(f32) + a[...].astype(f32) + b[...].astype(f32)
    ).astype(bf16)


def hold_kernel(*refs):
    pass


def hold(v, after):
    return pl.pallas_call(
        hold_kernel,
        out_shape=shape(v.shape, v.dtype),
        in_specs=[ANY] * (1 + len(after)),
        out_specs=ANY,
        input_output_aliases={0: 0},
        compiler_params=pltpu.CompilerParams(vmem_limit_bytes=2**20),
        cost_estimate=pl.CostEstimate(flops=0, bytes_accessed=0, transcendentals=0),
    )(v, *after)


def fence_kernel(*refs):
    refs[-1][...] = jnp.zeros(refs[-1].shape, f32)


def fence(arrays):
    return call(
        fence_kernel, shape((8, 128), f32), VMEM, [], arrays, [ANY] * len(arrays), 20, limit=2
    )


def chunk_spec(width, index):
    return pl.BlockSpec((1, 32, width), lambda i: (index, 0, 0))


class Reduction:
    def __init__(self, mine, mine_far, other, other_far, after=()):
        self.mine, self.mine_far = mine, mine_far
        other_far = hold(other_far, after) if after else other_far
        self.other, self.other_far = other, send(other_far, TO_CORE)
        self.width = mine.shape[2]
        self.distance = 4

    def follow(self, after=()):
        self.other = send(hold(self.other, after) if after else self.other, TO_CORE)
        return self

    def sums(self, kernel, shapes, places, partial, after):
        args, specs = [], []
        for place in places:
            args += [self.mine, self.other]
            specs += [chunk_spec(self.width, place)] * 2
        return call(
            kernel,
            shapes,
            [VMEM] * len(shapes),
            [],
            [*args, *partial, *after],
            [*specs, *[VMEM] * len(partial), *[ANY] * len(after)],
            0.5,
            limit=8,
            grid=(1,),
        )

    def advance(self, after=()):
        s = self.distance
        rows, pair = shape((32, self.width), bf16), shape((2, 32, self.width), bf16)
        places = [2 * (3 - s), 2 * (3 - s) + 1]
        self.distance -= 1
        if s == 0:
            made = self.sums(last_sum_kernel, [rows], [6], self.come, after)
            self.total = made[0]
            self.far = across(self.total)
        elif s == 4:
            made = self.sums(
                first_sum_kernel,
                [shape(self.mine_far.shape, bf16)],
                [],
                [self.mine_far, self.other_far],
                after,
            )
            self.come = [send(made[0], ALONG)]
        elif s > 1:
            kernel = functools.partial(step_sum_kernel, s == 3)
            made = self.sums(kernel, [pair], places, self.come, after)
            self.come = [send(made[0], ALONG)]
        else:
            made = self.sums(near_sum_kernel, [rows, rows], places, self.come, after)
            self.come = [send(made[0], ALONG), send(made[1], ACROSS)]
        return made

    def finish(self):
        while self.distance >= 0:
            self.advance()
        return self


def upper_result_kernel(both, both_far, inner_out, outer_out, token):
    token[...] = jnp.zeros(token.shape, f32)
    total = both[...].astype(f32) + both_far[...].astype(f32)
    hidden = inner_out.shape[1]
    inner_out[...] = total[:, :hidden]
    outer_out[...] = total[:, hidden:]


def lower_result_kernel(one, one_far, two, two_far, _, *refs):
    q_out, k_out, v_out, m_out, output_out = refs[:5]
    vector_outs, inner_out = refs[5:13], refs[13]
    width = output_out.shape[1]
    part = 64 * QUAD
    total = one[...].astype(f32) + one_far[...].astype(f32)
    output_out[...] = total[:, :width]
    pair = [total[:, width:], two[...].astype(f32) + two_far[...].astype(f32)]
    for i, out in enumerate((q_out, k_out, v_out)):
        for j in range(2):
            out[:, j * part : (j + 1) * part] = pair[j][:, i * part : (i + 1) * part]
    for i in range(2):
        for j in range(2):
            at = (2 * i + j) * part
            m_out[:, at : at + part] = pair[j][:, (3 + i) * part : (4 + i) * part]
    block = pair[1][:, 5 * part :]
    vectors = jnp.concatenate([block[:16], block[16:]], axis=1)
    rank = lax.axis_index("fsdp")
    quarter = lax.rem(rank, 4)

    def pick(v, index, size):
        found = jnp.zeros((v.shape[0], size), f32)
        for k in range(v.shape[1] // size):
            found += jnp.where(index == k, v[:, k * size : (k + 1) * size], 0.0)
        return found

    own = pick(pick(vectors[:8], lax.div(rank, 4), 128), quarter, 32)
    for i, out in enumerate(vector_outs):
        out[...] = own[i : i + 1]
    inner = pick(vectors[8:12], quarter, 128)
    found = jnp.zeros((1, 128), f32)
    for k in range(4):
        found += jnp.where(lax.div(rank, 4) == k, inner[k : k + 1], 0.0)
    inner_out[...] = found


def without_carried(kernel, n_in, n_carried, n_out, *refs):
    outs = refs[n_in + n_carried : n_in + n_carried + n_out]
    kernel(*refs[:n_in], *outs, *refs[n_in + n_out + 2 * n_carried :])


def call(
    kernel, out_shapes, out_specs, scratch, args, specs, micros, limit=20, grid=(), carried=()
):
    specs = list(specs)
    args = [
        pltpu.with_memory_space_constraint(v, pltpu.HBM) if spec is HBM else v
        for v, spec in zip(args, specs)
    ]
    single = not isinstance(out_specs, (list, tuple))
    shapes = [out_shapes] if single else list(out_shapes)
    spaces = [out_specs] if single else list(out_specs)
    shapes = [
        pltpu.HBM(v.shape, v.dtype) if spec is HBM else v for v, spec in zip(shapes, spaces)
    ]
    aliases = {}
    if carried:
        kernel = functools.partial(without_carried, kernel, len(args), len(carried), len(shapes))
        aliases = {len(args) + i: len(shapes) + i for i in range(len(carried))}
        args, specs = [*args, *carried], [*specs, *[ANY] * len(carried)]
        shapes += [shape(v.shape, v.dtype) for v in carried]
        spaces += [ANY] * len(carried)
        single = False
    return pl.pallas_call(
        kernel,
        grid=grid,
        out_shape=shapes[0] if single else tuple(shapes),
        in_specs=specs,
        out_specs=spaces[0] if single else tuple(spaces),
        input_output_aliases=aliases,
        scratch_shapes=scratch,
        compiler_params=pltpu.CompilerParams(vmem_limit_bytes=limit * 1024 * 1024),
        cost_estimate=pl.CostEstimate(
            flops=int(micros * 1.15e9), bytes_accessed=int(micros * 3.6e6), transcendentals=0
        ),
    )(*args)


def shape(dims, dtype):
    return jax.ShapeDtypeStruct(dims, dtype)


def per_device(ring, *args):
    (
        frames,
        memory_bank,
        cache_keys,
        cache_values,
        out_grad,
        first_gain,
        first_shift,
        query_weight,
        query_bias,
        key_weight,
        value_weight,
        value_bias,
        memory_weight,
        output_weight,
        output_bias,
        second_gain,
        second_shift,
        inner_weight,
        inner_bias,
        outer_weight,
        outer_bias,
    ) = args
    length, width = frames.shape
    ranks = width // first_gain.shape[0]
    part = width // ranks
    inner_part = inner_bias.shape[0]
    hidden = inner_part * ranks
    groups = -(-length // GROUP)
    padded = groups * GROUP
    extended = (groups - 1) * GROUP + SPAN
    quad = 64 * QUAD
    vectors = [
        first_gain,
        first_shift,
        query_bias,
        value_bias,
        output_bias,
        second_gain,
        second_shift,
        outer_bias,
    ]
    first = [query_weight, key_weight, value_weight, memory_weight]
    second = [output_weight.T, inner_weight, outer_weight.T]
    dma = pltpu.SemaphoreType.DMA
    row, wide_row = shape((length, width), bf16), shape((length, hidden), bf16)
    row_wide, vec_shape = shape((length, width), f32), shape((16, width), f32)
    turned = shape((width, length), bf16)

    def scratch_of(*shapes):
        return [pltpu.VMEM(v.shape, v.dtype) for v in shapes]

    if ring:
        total = 6 * width + 2 * hidden + 256
        weights, main = call(
            pack_first_kernel,
            (shape((part, total), bf16), shape((part, sum(shares(total))), bf16)),
            [VMEM] * 2,
            [
                *([pltpu.VMEM((1, part), bf16)] * 8),
                pltpu.VMEM((1, inner_part), bf16),
                pltpu.SemaphoreType.DMA((16,)),
            ],
            [
                *first,
                *second,
                *(v.reshape(1, part) for v in vectors),
                inner_bias.reshape(1, inner_part),
            ],
            [HBM] * 16,
            1,
            limit=8,
        )
        vec = jnp.zeros((16, width), f32)
    else:
        weights = jnp.concatenate(first + second, axis=1)
        vec = jnp.concatenate(
            [
                jnp.stack([lax.all_gather(v, "fsdp", axis=0, tiled=True) for v in vectors]),
                lax.all_gather(inner_bias, "fsdp", axis=0, tiled=True).reshape(-1, width),
                jnp.zeros((4, width), bf16),
            ],
            axis=0,
        ).astype(f32)
    normal, bias_grad, nt, gt = gated(
        functools.partial(prepare_kernel, length),
        (row_wide, vec_shape, turned, turned),
        [VMEM, VMEM, HBM, HBM],
        [*scratch_of(turned, turned), dma((2,))],
        [frames, out_grad],
        [VMEM] * 2,
        3,
        [weights],
    )
    if ring:
        items = ring_gather(weights, main, [bias_grad])
        early = [v for v in items if v[1] in (0, 1, 7)]
        late = [v for v in items if v[1] not in (0, 1, 7)]
        weights = whole_weights(late, width, whole_weights(early, width))
    else:
        weights = lax.all_gather(weights, "fsdp", axis=0, tiled=True)

    attended_shapes = (
        shape((padded, width), bf16),
        shape((extended, width), bf16),
        shape((extended, width), bf16),
        shape((16, 2 * width), bf16),
        shape((HEADS // QUAD, groups, KEYS, GROUP * QUAD), bf16),
    )
    *attended, ctx, vec, cols = call(
        functools.partial(attention_forward_kernel, ring, length),
        (
            *attended_shapes,
            shape((padded, width), bf16),
            vec_shape,
            shape((width, 16), f32),
        ),
        [VMEM] * 8,
        [pltpu.VMEM((2, KEYS, GROUP * QUAD), f32)],
        [normal, memory_bank, cache_keys, cache_values, vec, weights],
        [VMEM] * 6,
        6,
    )

    def grad_shapes(w):
        if ring:
            dims = [(7, 32, w), (2, 32, w // 2)]
            return tuple(shape(v, bf16) for v in dims + dims)
        return (shape((width, w), bf16),)

    grad_specs = [VMEM] * (4 if ring else 1)
    token_shape = shape((8, 128), f32)
    residual, normed2, active, slope, *attended = call(
        functools.partial(inner_kernel, length),
        (row_wide, row, wide_row, wide_row),
        [VMEM] * 4,
        [],
        [frames, ctx, vec, weights],
        [VMEM] * 4,
        5,
        carried=attended,
    )

    gi, vec_grads, active, residual, *attended = call(
        functools.partial(grad_inner_kernel, length),
        (wide_row, vec_shape),
        [VMEM] * 2,
        [],
        [out_grad, slope, bias_grad, weights],
        [VMEM] * 4,
        2,
        carried=[active, residual, *attended],
    )
    results = call(
        functools.partial(hidden_weight_kernel, ring, length),
        grad_shapes(2 * hidden),
        grad_specs,
        [
            *scratch_of(turned, turned),
            pltpu.VMEM((width, 2 * hidden), bf16),
            dma((1,)),
        ],
        [normed2, gi, active, gt],
        [VMEM] * 3 + [HBM],
        5,
        carried=[residual, *attended],
    )
    both_grads, (residual, *attended) = results[:-6], results[-6:]
    both = Reduction(*both_grads).follow() if ring else None

    def steps(after, *reductions):
        made = []
        if ring:
            for reduction in reductions:
                made += reduction.advance([after])
        return made

    grad_att, grad_ctx, vec_grads, nt, grad_res, active, *attended = gated(
        functools.partial(grad_residual_kernel, length),
        (row, shape((padded, width), bf16), vec_shape, turned, row_wide),
        [VMEM] * 5,
        [dma((1,))],
        [gi, residual, out_grad, vec, vec_grads, weights, nt],
        [VMEM] * 6 + [HBM],
        4,
        both_grads[:1],
        carried=[active, *attended],
    )
    made = steps(vec_grads, both)
    part_row = shape((length, quad), bf16)
    left_row = shape((LEAD, quad), f32)
    quad_shapes = (
        shape((padded, quad), bf16),
        part_row,
        part_row,
        left_row,
        left_row,
        shape((16, 2 * quad), bf16),
    )
    quad_scratch = [
        pltpu.VMEM((extended, quad), f32),
        pltpu.VMEM((extended, quad), f32),
        pltpu.VMEM((16, 2 * quad), f32),
    ]
    results = gated(
        functools.partial(quad_kernel, 0, ring, length),
        (*quad_shapes, vec_shape, *grad_shapes(width + 5 * quad)),
        [VMEM] * 7 + grad_specs,
        [
            *quad_scratch,
            pltpu.VMEM((width, width + 5 * quad), bf16),
            *scratch_of(turned),
        ],
        [memory_bank, grad_ctx, cols, vec_grads, nt, weights, *attended, grad_att, ctx],
        [VMEM] * 13,
        6,
        made,
        carried=[active, residual, grad_res],
    )
    quad_one, vec_grads, one_grads = results[:6], results[6], results[7:-3]
    carried = results[-3:]
    made = steps(vec_grads, both)
    one = Reduction(*one_grads, after=made).follow(made) if ring else None
    two_width = 5 * quad + (256 if ring else 0)
    results = gated(
        functools.partial(quad_kernel, 1, ring, length),
        (*quad_shapes, vec_shape, *grad_shapes(two_width)),
        [VMEM] * 7 + grad_specs,
        [*quad_scratch, pltpu.VMEM((width, two_width), bf16)],
        [memory_bank, grad_ctx, cols, vec_grads, nt, weights, *attended],
        [VMEM] * 11,
        6,
        made,
        carried=carried,
    )
    quad_two, vec_grads, two_grads = results[:6], results[6], results[7:-3]
    active, residual, grad_res = results[-3:]
    two = Reduction(*two_grads) if ring else None
    made = steps(vec_grads, both)
    made += steps(vec_grads, one)
    if ring:
        two.follow(made[:1])
    made = steps(made[-1] if ring else vec_grads, two)
    output, token, grad_res = gated(
        functools.partial(output_kernel, length),
        (row, token_shape),
        [VMEM] * 2,
        [],
        [active, residual, vec, weights],
        [VMEM] * 4,
        3,
        made,
        carried=[grad_res],
    )
    if ring:
        made = one.advance([token]) + two.advance([token])
        both.advance([fence(made)])
        made = one.advance() + two.advance()
        made = both.advance([fence(made)])
        inner_sum, outer_sum, token = call(
            upper_result_kernel,
            (shape((part, hidden), f32), shape((part, hidden), f32), token_shape),
            [VMEM] * 3,
            [],
            [both.total, both.far],
            [VMEM] * 2,
            1,
            limit=8,
        )
        made = one.advance(made) + two.advance(made)
        token = fence(made)
        made = one.advance([token]) + two.advance([token])
        grad_frames, grad_bank, grad_ck, grad_cv, token = gated(
            functools.partial(lower_kernel, length),
            (
                row_wide,
                shape((1, MEM, width), f32),
                shape((LEFT, 1, width), f32),
                shape((LEFT, 1, width), f32),
                token_shape,
            ),
            [VMEM] * 5,
            [],
            [frames, grad_res, vec, weights, *quad_one, *quad_two],
            [VMEM] * 16,
            5,
            made,
        )
        square = shape((part, width), f32)
        q_sum, k_sum, v_sum, m_sum, output_sum, *own = call(
            lower_result_kernel,
            (
                square,
                square,
                square,
                shape((part, 2 * width), f32),
                square,
                *([shape((1, part), f32)] * 8),
                shape((1, inner_part), f32),
            ),
            [VMEM] * 14,
            [],
            [one.total, one.far, two.total, two.far, token],
            [VMEM] * 4 + [ANY],
            1,
            limit=8,
        )
        own_inner = own[8].reshape(inner_part)
        own = [v.reshape(part) for v in own[:8]]
    else:
        grad_frames, grad_bank, grad_ck, grad_cv, token = gated(
            functools.partial(lower_kernel, length),
            (
                row_wide,
                shape((1, MEM, width), f32),
                shape((LEFT, 1, width), f32),
                shape((LEFT, 1, width), f32),
                token_shape,
            ),
            [VMEM] * 5,
            [],
            [frames, grad_res, vec, weights, *quad_one, *quad_two],
            [VMEM] * 16,
            5,
            made,
        )

        def reduce(v):
            total = lax.psum_scatter(v, "fsdp", scatter_dimension=0, tiled=True)
            return lax.psum(total, "rep").astype(f32)

        total = reduce(both_grads[0])
        inner_sum, outer_sum = total[:, :hidden], total[:, hidden:]
        low, high = reduce(one_grads[0]), reduce(two_grads[0])
        output_sum = low[:, :width]
        sums = [v.reshape(part, 5, quad) for v in (low[:, width:], high)]
        q_sum, k_sum, v_sum, m_low, m_high = (
            jnp.concatenate([v[:, i] for v in sums], axis=1) for i in range(5)
        )
        m_sum = jnp.concatenate([m_low, m_high], axis=1)
        vec_sum = lax.psum(vec_grads, ("rep", "fsdp"))
        rank = lax.axis_index("fsdp")
        own = lax.dynamic_slice(vec_sum[:8], (0, rank * part), (8, part))
        own_inner = lax.dynamic_slice(
            vec_sum[8:12].reshape(-1), (rank * inner_part,), (inner_part,)
        )
    return (
        output,
        grad_frames,
        grad_bank,
        jnp.swapaxes(grad_ck, 0, 1),
        jnp.swapaxes(grad_cv, 0, 1),
        own[0],
        own[1],
        q_sum,
        own[2],
        k_sum,
        v_sum,
        own[3],
        m_sum,
        output_sum.T,
        own[4],
        own[5],
        own[6],
        inner_sum,
        own_inner,
        outer_sum.T,
        own[7],
    )


def without_gates(kernel, n_args, n_gates, *refs):
    kernel(*refs[:n_args], *refs[n_args + n_gates :])


def gated(kernel, out_shapes, out_specs, scratch, args, specs, micros, made, carried=()):
    return call(
        functools.partial(without_gates, kernel, len(args), len(made)),
        out_shapes,
        out_specs,
        scratch,
        [*args, *made],
        [*specs, *[ANY] * len(made)],
        micros,
        carried=carried,
    )


def solution(mesh):
    both = ("rep", "fsdp")
    rows, vector = P("fsdp", None), P("fsdp")
    columns = P(None, "fsdp")
    weights = (
        vector,
        vector,
        rows,
        vector,
        rows,
        rows,
        vector,
        rows,
        columns,
        vector,
        vector,
        vector,
        rows,
        vector,
        columns,
        vector,
    )
    blocks = P(both, None, None)
    in_specs = (P(both, None), blocks, blocks, blocks, P(both, None), *weights)
    out_specs = (P(both, None), P(both, None), blocks, blocks, blocks, *weights)
    ring = mesh.shape["fsdp"] == 16 and mesh.shape["rep"] == 2
    return jax.shard_map(
        functools.partial(per_device, ring),
        mesh=mesh,
        in_specs=in_specs,
        out_specs=out_specs,
        check_vma=False,
    )
```

```python
import functools

import jax
import jax.numpy as jnp
from jax import lax
from jax.experimental import pallas as pl
from jax.experimental.pallas import tpu as pltpu
from jax.sharding import PartitionSpec as P

HEADS = 8
SEG = 16
RIGHT = 4
LEFT = 30
MEM = 4

LEAD = 32
GROUP = 64
SPAN = 112
KEYS = 128
QUAD = 4
masked_value = -1e30
epsilon = 1e-05
gelu_a = 0.7978845608028654
gelu_b = gelu_a * 0.044715

bf16 = jnp.bfloat16
f32 = jnp.float32
VMEM = pl.BlockSpec(memory_space=pltpu.VMEM)
ANY = pl.BlockSpec(memory_space=pl.ANY)
HBM = pl.BlockSpec(memory_space=pltpu.HBM)


def dot(a, b):
    return lax.dot_general(a, b, (((1,), (0,)), ((), ())), preferred_element_type=f32)


def dot_nt(a, b):
    return lax.dot_general(a, b, (((1,), (1,)), ((), ())), preferred_element_type=f32)


def dot_tn(a, b):
    return lax.dot_general(a, b, (((0,), (0,)), ((), ())), preferred_element_type=f32)


def row_tiles(rows):
    return [(start, min(256, rows - start)) for start in range(0, rows, 256)]


def centred(v):
    center = v - jnp.mean(v, axis=-1, keepdims=True)
    spread = jnp.mean(center * center, axis=-1, keepdims=True)
    scale = lax.rsqrt(spread + epsilon)
    return center * scale, scale


def norm_back(e, n, scale, gain):
    eg = e * gain
    return scale * (
        eg - jnp.mean(eg, axis=-1, keepdims=True) - n * jnp.mean(eg * n, axis=-1, keepdims=True)
    )


def colsum(v):
    return jnp.sum(v, axis=0, keepdims=True)


RING = (0, 2, 4, 6, 7, 5, 3, 1)


def ring_pairs(step):
    pairs = []
    for k in range(8):
        for core in range(2):
            pairs.append((2 * RING[k] + core, 2 * RING[(k + step) % 8] + core))
    return pairs


TO_RIGHT, TO_LEFT = ring_pairs(1), ring_pairs(-1)
TO_CORE = [(i, i ^ 1) for i in range(16)]


def two_way(cross):
    pairs = []
    for k in range(8):
        pairs.append((2 * RING[k], 2 * RING[(k + 1) % 8] + cross))
        pairs.append((2 * RING[k] + 1, 2 * RING[(k - 1) % 8] + 1 - cross))
    return pairs


ALONG, ACROSS = two_way(0), two_way(1)


def ring_ids():
    rank = lax.axis_index("fsdp")
    core, chip = lax.rem(rank, 2), lax.div(rank, 2)
    z, x = lax.div(chip, 2), lax.rem(chip, 2)
    return jnp.where(x == 0, z, 7 - z), core


def ring_rank(position, core):
    position = lax.rem(position, 8)
    return 2 * jnp.where(position < 4, 2 * position, 15 - 2 * position) + core


def halves(width):
    return width // 2 // 128 * 128


def send(v, pairs):
    return lax.ppermute(v, "fsdp", pairs)


def across(v):
    return lax.ppermute(v, "rep", [(0, 1), (1, 0)])


def shares(width, hidden):
    return 5 * width + 256, (width + 2 * hidden) // 2


def ring_gather(shard, main, common, after):
    third = main.shape[1] - common
    got = [(shard, 0, "all")]
    a = b = main
    for step in (1, 2, 3):
        a, b = send(a, TO_RIGHT), send(b, TO_LEFT)
        pair = call(
            tails_kernel,
            shape((shard.shape[0], 2 * third), bf16),
            VMEM,
            [],
            [a, b],
            [VMEM] * 2,
            0.3,
            limit=4,
        )
        pair = across(pair)
        if step == 1:
            pair = hold(pair, after)
        got += [(a, 8 - step, "main"), (b, step, "main"), (pair, step, "pair")]
    a, b = send(a[:, :common], TO_RIGHT), send(b[:, common:], TO_LEFT)
    return got + [(a, 4, "common"), (b, 4, "own"), (across(b), 4, "other")]


def both_cores(items, after=()):
    items = [(hold(v, after) if after else v, d, k) for v, d, k in items]
    return [(v, d, 0, k) for v, d, k in items] + [(send(v, TO_CORE), d, 1, k) for v, d, k in items]


def tails_kernel(a, b, *refs):
    out = refs[-1]
    third = out.shape[1] // 2
    out[:, :third] = a[:, a.shape[1] - third :]
    out[:, third:] = b[:, b.shape[1] - third :]


def lay_rows(places, common, *refs):
    refs, whole = refs[: len(places)], refs[-1]
    position, core = ring_ids()
    replica = lax.axis_index("rep")
    third = whole.shape[1] // 2
    own = pl.ds(pl.multiple_of(replica * third, 128), third)
    other = pl.ds(pl.multiple_of((1 - replica) * third, 128), third)

    def rows(distance, flip):
        owner = ring_rank(position + distance, core if flip == 0 else 1 - core)
        return pl.ds(pl.multiple_of(owner * 32, 32), 32)

    for ref, (distance, flip, kind) in zip(refs, places):
        at = rows(distance, flip)
        if common:
            whole[at, :] = ref[:, :common]
        elif kind == "all":
            whole[at, :] = ref[:, ref.shape[1] - 2 * third :]
        elif kind == "main":
            whole[at, own] = ref[:, ref.shape[1] - third :]
        elif kind == "pair":
            whole[rows(8 - distance, flip), other] = ref[:, :third]
            whole[at, other] = ref[:, third:]
        else:
            whole[at, own if kind == "own" else other] = ref[...]


def whole_weights(items, kinds, dims, common, after=()):
    items = [v for v in items if v[3] in kinds]
    return call(
        functools.partial(lay_rows, tuple(v[1:] for v in items), common),
        shape(dims, bf16),
        VMEM,
        [],
        [*(v[0] for v in items), *after],
        [VMEM] * len(items) + [ANY] * len(after),
        0.5,
        limit=24,
    )


def spread(ring, grads, outs):
    if not ring:
        outs[0][...] = grads[...]
        return
    position, core = ring_ids()
    mine, mine_far, other, other_far = outs
    half = mine_far.shape[2]
    way = 1 - 2 * core

    def rows(place, k):
        return pl.ds(pl.multiple_of(ring_rank(place, k) * 32, 32), 32)

    def lanes(k):
        return pl.ds(pl.multiple_of(k * half, 128), half)

    for k in range(2):
        for distance in (3, 2, 1):
            at = 2 * (3 - distance) + k
            mine[at] = grads[rows(position + 8 + way * distance, k), :]
            other[at] = grads[rows(position + 8 - way * distance, k), :]
        mine_far[k] = grads[rows(position + 4, k), lanes(core)]
        other_far[k] = grads[rows(position + 4, k), lanes(1 - core)]
    mine[6] = grads[rows(position, core), :]
    other[6] = grads[rows(position, 1 - core), :]


def start_all(pairs, sems, first=0):
    copies = [pltpu.make_async_copy(a, b, sems.at[first + i]) for i, (a, b) in enumerate(pairs)]
    for copy in copies:
        copy.start()
    return copies


def wait_all(copies):
    for copy in copies:
        copy.wait()


def columns(width, hidden):
    return width, width + hidden, width + 2 * hidden


def head_masks():
    lane = lax.broadcasted_iota(jnp.int32, (1, 64 * QUAD), 1)
    return [(lane // 64 == h).astype(f32) for h in range(QUAD)]


def stacked(rows, masks):
    return jnp.concatenate([rows * m for m in masks], axis=0)


def unstacked(wide, masks):
    parts = [wide[GROUP * h : GROUP * (h + 1)] * masks[h] for h in range(QUAD)]
    return parts[0] + parts[1] + parts[2] + parts[3]


def added_mask(limit):
    row = lax.broadcasted_iota(jnp.int32, (KEYS, GROUP * QUAD), 0)
    query = lax.rem(lax.broadcasted_iota(jnp.int32, (KEYS, GROUP * QUAD), 1), GROUP)
    first = query // SEG * SEG + (LEAD - LEFT)
    inside = (row >= first) & (row < first + LEFT + SEG + RIGHT) & (row < limit)
    bank = (row >= SPAN) & (row < SPAN + MEM)
    return jnp.where((inside & (row < SPAN)) | bank, 0.0, masked_value)


def prepare_kernel(length, frames, out_grad, n_out, bias_out, nt_out, gt_out, nt, gt, sems):
    for start, size in row_tiles(length):
        rows = slice(start, start + size)
        n, _ = centred(frames[rows].astype(f32))
        n_out[rows] = n
        nt[:, rows] = n.astype(bf16).T
        gt[:, rows] = out_grad[rows].T
    copies = start_all([(nt, nt_out), (gt, gt_out)], sems)
    bias_out[...] = jnp.zeros(bias_out.shape, f32)
    bias_out[7:8] = colsum(out_grad[...].astype(f32))
    wait_all(copies)


def attention_forward_kernel(ring, length, *refs):
    normal, bank, cache_k, cache_v, vec, w = refs[:6]
    q, kext, vext, kvmem, pt, ctx, vec_out, cols_out, mask = refs[6:]
    width = normal.shape[1]
    groups = q.shape[0] // GROUP
    if not ring:
        vectors = vec[...]
    else:
        blocks = w[:, 5 * width :].astype(f32).reshape(16, 32, 256)
        total = jnp.sum(blocks, axis=0)
        vectors = jnp.concatenate([total[:16], total[16:]], axis=1)
    vec_out[...] = vectors
    cols_out[...] = vectors.T

    def left_rows(cache):
        rows = cache[0].astype(f32)
        return jnp.concatenate([jnp.zeros((LEAD - LEFT, width), f32), rows], axis=0).astype(bf16)

    kext[0:LEAD] = left_rows(cache_k)
    vext[0:LEAD] = left_rows(cache_v)
    tail = kext.shape[0] - LEAD - length
    kext[LEAD + length :] = jnp.zeros((tail, width), bf16)
    vext[LEAD + length :] = jnp.zeros((tail, width), bf16)
    q[length:] = jnp.zeros((q.shape[0] - length, width), bf16)
    bank_rows = jnp.concatenate(
        [bank[0].astype(f32), jnp.zeros((16 - MEM, width), f32)], axis=0
    ).astype(bf16)
    kvmem[...] = dot(bank_rows, w[:, 3 * width : 5 * width]).astype(bf16)

    for start, size in row_tiles(length):
        rows = (normal[start : start + size] * vectors[0:1] + vectors[1:2]).astype(bf16)
        q[start : start + size] = (dot(rows, w[:, :width]) + vectors[2:3]).astype(bf16)
        kext[LEAD + start : LEAD + start + size] = dot(rows, w[:, width : 2 * width]).astype(bf16)
        vext[LEAD + start : LEAD + start + size] = (
            dot(rows, w[:, 2 * width : 3 * width]) + vectors[3:4]
        ).astype(bf16)

    masks = head_masks()
    scale = 64**-0.5
    q_masks = [(m * scale).astype(bf16) for m in masks]
    mask[0] = added_mask(KEYS)
    mask[1] = added_mask(LEAD + length - GROUP * (groups - 1))

    def step(g, carry):
        top = pl.multiple_of(g * GROUP, GROUP)
        hidden = mask[(g == groups - 1).astype(jnp.int32)]
        for j in range(HEADS // QUAD):
            lanes = slice(64 * QUAD * j, 64 * QUAD * (j + 1))
            keys = jnp.concatenate([kext[pl.ds(top, SPAN), lanes], kvmem[:, lanes]], axis=0)
            values = jnp.concatenate(
                [vext[pl.ds(top, SPAN), lanes], kvmem[:, width + lanes.start : width + lanes.stop]],
                axis=0,
            )
            queries = stacked(q[pl.ds(top, GROUP), lanes], q_masks)
            scores = dot_nt(keys, queries) + hidden
            raised = jnp.exp(scores - jnp.max(scores, axis=0, keepdims=True))
            weights = (raised / jnp.sum(raised, axis=0, keepdims=True)).astype(bf16)
            pt[j, g] = weights
            ctx[pl.ds(top, GROUP), lanes] = unstacked(dot_tn(weights, values), masks).astype(bf16)
        return carry

    lax.fori_loop(0, groups, step, 0, unroll=6)


def inner_kernel(length, *refs):
    frames, ctx, vec, w, residual, normed2, active, slope = refs
    width = frames.shape[1]
    hidden = active.shape[1]
    second, _, _ = columns(width, hidden)
    for start, size in row_tiles(length):
        rows = slice(start, start + size)
        res = frames[rows].astype(f32) + dot_nt(ctx[rows], w[:, :second]) + vec[4:5]
        residual[rows] = res
        n, _ = centred(res)
        normed2[rows] = (n * vec[5:6] + vec[6:7]).astype(bf16)

    block = 512
    for b in range(hidden // block):
        cols = slice(b * block, (b + 1) * block)
        for start, size in row_tiles(length):
            rows = slice(start, start + size)
            u = dot(normed2[rows], w[:, second + cols.start : second + cols.stop]) + vec[8 + b : 9 + b]
            uu = u * u
            h = 0.5 + 0.5 * jnp.tanh(u * (gelu_a + gelu_b * uu))
            act = u * h
            active[rows, cols] = act.astype(bf16)
            slope[rows, cols] = (
                h + act * (1.0 - h) * (2 * gelu_a + 6 * gelu_b * uu)
            ).astype(bf16)


def grad_inner_kernel(length, out_grad, slope, vec_before, w, gi, vec_grads):
    width, hidden = out_grad.shape[1], slope.shape[1]
    third = columns(width, hidden)[1]
    block = 512
    vec_grads[...] = vec_before[...]
    for b in range(hidden // block):
        cols = slice(b * block, (b + 1) * block)
        sums = jnp.zeros((1, block), f32)
        for start, size in row_tiles(length):
            rows = slice(start, start + size)
            up = dot(out_grad[rows], w[:, third + cols.start : third + cols.stop])
            part = (up * slope[rows, cols].astype(f32)).astype(bf16)
            gi[rows, cols] = part
            sums += colsum(part.astype(f32))
        vec_grads[8 + b : 9 + b] = sums


def output_kernel(length, active, residual, vec, w, output, token):
    _, third, last = columns(residual.shape[1], active.shape[1])
    token[...] = jnp.zeros(token.shape, f32)
    for start, size in row_tiles(length):
        rows = slice(start, start + size)
        output[rows] = (residual[rows] + dot_nt(active[rows], w[:, third:last]) + vec[7:8]).astype(bf16)


def hidden_weight_kernel(ring, length, *refs):
    normed2, gi, active, gt_in = refs[:4]
    outs, (n2t, gt, grads, sems) = refs[4:-4], refs[-4:]
    hidden = gi.shape[1]
    copies = start_all([(gt_in, gt)], sems)
    for start, size in row_tiles(length):
        rows = slice(start, start + size)
        n2t[:, rows] = normed2[rows].T
    for at in range(0, hidden, 512):
        grads[:, at : at + 512] = dot(n2t[...], gi[:, at : at + 512]).astype(bf16)
    wait_all(copies)
    for at in range(0, hidden, 512):
        cols = slice(hidden + at, hidden + at + 512)
        grads[:, cols] = dot(gt[...], active[:, at : at + 512]).astype(bf16)
    spread(ring, grads, outs)


def grad_residual_kernel(length, *refs):
    gi, residual, out_grad, vec, vec_before, w, nt_in = refs[:7]
    grad_att, grad_ctx, vec_grads, nt, grad_res, sems = refs[7:]
    width = residual.shape[1]
    copies = start_all([(nt_in, nt)], sems)
    second, third, _ = columns(width, gi.shape[1])
    sums = [jnp.zeros((1, width), f32) for _ in range(3)]
    for start, size in row_tiles(length):
        rows = slice(start, start + size)
        e = dot_nt(gi[rows], w[:, second:third])
        n, scale = centred(residual[rows])
        gres = out_grad[rows].astype(f32) + norm_back(e, n, scale, vec[5:6])
        grad_res[rows] = gres
        gat_rows = gres.astype(bf16)
        grad_att[rows] = gat_rows
        grad_ctx[rows] = dot(gat_rows, w[:, :second]).astype(bf16)
        sums = [s + colsum(v) for s, v in zip(sums, (gat_rows.astype(f32), e * n, e))]
    grad_ctx[length:] = jnp.zeros((grad_ctx.shape[0] - length, width), bf16)
    vec_grads[...] = vec_before[...]
    for i in range(3):
        vec_grads[4 + i : 5 + i] = sums[i]
    wait_all(copies)


def attention_backward(j, attended, grad_ctx, gk, gv, gkm, gq):
    q, kext, vext, kvmem, pt = attended
    width = q.shape[1]
    groups = q.shape[0] // GROUP
    size = 64 * QUAD
    lanes = slice(size * j, size * (j + 1))
    value_lanes = slice(width + size * j, width + size * (j + 1))
    gk[...] = jnp.zeros(gk.shape, f32)
    gv[...] = jnp.zeros(gv.shape, f32)
    gkm[...] = jnp.zeros(gkm.shape, f32)
    masks = head_masks()
    scale = 64**-0.5
    q_masks = [(m * scale).astype(bf16) for m in masks]
    c_masks = [m.astype(bf16) for m in masks]
    out_masks = [m * scale for m in masks]

    def step(g, carry):
        top = pl.multiple_of(g * GROUP, GROUP)
        keys = jnp.concatenate([kext[pl.ds(top, SPAN), lanes], kvmem[:, lanes]], axis=0)
        values = jnp.concatenate([vext[pl.ds(top, SPAN), lanes], kvmem[:, value_lanes]], axis=0)
        queries = stacked(q[pl.ds(top, GROUP), lanes], q_masks)
        upstream = stacked(grad_ctx[pl.ds(top, GROUP), lanes], c_masks)
        weights = pt[j, g]
        wide = weights.astype(f32)
        gp = dot_nt(values, upstream)
        gs = (wide * (gp - colsum(gp * wide))).astype(bf16)
        gkeys = dot(gs, queries)
        gvalues = dot(weights, upstream)
        gk[pl.ds(top, SPAN)] += gkeys[:SPAN]
        gv[pl.ds(top, SPAN)] += gvalues[:SPAN]
        gkm[:, :size] += gkeys[SPAN:]
        gkm[:, size:] += gvalues[SPAN:]
        gq[pl.ds(top, GROUP)] = unstacked(dot_tn(gs, keys), out_masks).astype(bf16)
        return carry

    lax.fori_loop(0, groups, step, 0, unroll=6)


def bank_block(bank, width):
    return jnp.concatenate(
        [bank[0].astype(f32), jnp.zeros((16 - MEM, width), f32)], axis=0
    ).astype(bf16)


def pair_of(row):
    high = row.astype(bf16).astype(f32)
    zeros = jnp.zeros((14, row.shape[1]), f32)
    return jnp.concatenate([high, row - high, zeros], axis=0).astype(bf16)


def quad_kernel(j, ring, length, *refs):
    bank, grad_ctx, cols, vec_before, nt, w = refs[:6]
    attended, refs = refs[6:11], refs[11:]
    width = nt.shape[0]
    size = 64 * QUAD
    first = width * (1 - j)
    if j == 0:
        grad_att, ctx = refs[:2]
        refs = refs[2:]
    gq, gk_rows, gv_rows, gk_left, gv_left, gbank, vec_grads = refs[:7]
    refs = refs[7:]
    n_out = 4 if ring else 1
    outs = refs[:n_out]
    gk, gv, gkm, grads, *rest = refs[n_out:]
    if j == 0:
        gat = rest[0]
        for start, count in row_tiles(length):
            rows = slice(start, start + count)
            gat[:, rows] = grad_att[rows].T
        grads[:, :width] = dot(gat[...], ctx[:length]).astype(bf16)
    attention_backward(j, attended, grad_ctx, gk, gv, gkm, gq)
    gk_left[...] = gk[0:LEAD]
    gv_left[...] = gv[0:LEAD]
    gk_rows[...] = gk[LEAD : LEAD + length].astype(bf16)
    gv_rows[...] = gv[LEAD : LEAD + length].astype(bf16)
    gbank[...] = gkm[...].astype(bf16)

    gain, shift = cols[:, 0:1], cols[:, 1:2]
    gains, shifts = jnp.zeros((width, 1), f32), jnp.zeros((16, width), f32)
    sums = []
    for i, g in enumerate((gq[:length], gk_rows[...], gv_rows[...])):
        m = dot(nt[...], g)
        sums.append(colsum(g.astype(f32)))
        at = first + i * size
        grads[:, at : at + size] = (gain * m + shift * sums[i]).astype(bf16)
        own = slice(i * width + j * size, i * width + (j + 1) * size)
        gains += jnp.sum(w[:, own].astype(f32) * m, axis=1, keepdims=True)
        shifts += dot_nt(pair_of(sums[i]), w[:, own])
    at = first + 3 * size
    grads[:, at : at + 2 * size] = dot_tn(bank_block(bank, width), gbank[...]).astype(bf16)
    vec_grads[...] = vec_before[...]
    vec_grads[0:1] += jnp.transpose(jnp.broadcast_to(gains, (width, 128)))[0:1]
    vec_grads[1:2] += colsum(shifts)
    vec_grads[2:3, size * j : size * (j + 1)] = sums[0]
    vec_grads[3:4, size * j : size * (j + 1)] = sums[2]
    if j == 1 and ring:
        vectors = vec_grads[...]
        block = jnp.concatenate([vectors[:, :256], vectors[:, 256:]], axis=0).astype(bf16)
        grads[:, at + 2 * size :] = jnp.concatenate([block] * 16, axis=0)
    spread(ring, grads, outs)


def lower_kernel(length, *refs):
    frames, grad_res, vec, w = refs[:4]
    gq, gk, gv, gk_left, gv_left, gbank = ([refs[4 + i], refs[10 + i]] for i in range(6))
    grad_frames, grad_bank, grad_ck, grad_cv, token = refs[16:]
    token[...] = jnp.zeros(token.shape, f32)
    width = frames.shape[1]
    part = gq[0].shape[1]
    for out, parts in ((grad_ck, gk_left), (grad_cv, gv_left)):
        left = jnp.concatenate([v[...] for v in parts], axis=1)
        for row in range(LEFT):
            out[row] = left[LEAD - LEFT + row : LEAD - LEFT + row + 1]
    bank_grads = jnp.concatenate(
        [v[:, at : at + part] for at in (0, part) for v in gbank], axis=1
    )
    grad_bank[0] = dot_nt(bank_grads, w[:, 3 * width : 5 * width])[:MEM]
    for start, size in row_tiles(length):
        rows = slice(start, start + size)
        parts = [jnp.concatenate([v[rows] for v in pair], axis=1) for pair in (gq, gk, gv)]
        e = (
            dot_nt(parts[0], w[:, :width])
            + dot_nt(parts[1], w[:, width : 2 * width])
            + dot_nt(parts[2], w[:, 2 * width : 3 * width])
        )
        n, s = centred(frames[rows].astype(f32))
        grad_frames[rows] = grad_res[rows] + norm_back(e, n, s, vec[0:1])


def pack_first_kernel(*refs):
    weights, vectors, inner_bias, out, main = refs[:7], refs[7:15], refs[15], refs[16], refs[17]
    held, bias_held, sems = refs[18:26], refs[26], refs[27]
    width = weights[0].shape[1]
    column = 0
    copies = []
    for i, ref in enumerate(weights):
        if i == 4:
            column += 256
        copies.append((ref, out.at[:, pl.ds(column, ref.shape[1])]))
        column += ref.shape[1]
    copies += list(zip((*vectors, inner_bias), (*held, bias_held)))
    copies = [pltpu.make_async_copy(a, b, sems.at[i]) for i, (a, b) in enumerate(copies)]
    for copy in copies:
        copy.start()
    wait_all(copies)
    rank = lax.axis_index("fsdp")
    own = jnp.concatenate([ref[...].astype(f32) for ref in held], axis=0)
    part = own.shape[1]
    placed = jnp.where(
        lax.broadcasted_iota(jnp.int32, (8, width), 1) // part == rank,
        jnp.concatenate([own] * (width // part), axis=1),
        0.0,
    )
    bias = bias_held[...].astype(f32)
    count = bias.shape[1]
    row = lax.broadcasted_iota(jnp.int32, (4, width), 0)
    lane = lax.broadcasted_iota(jnp.int32, (4, width), 1)
    inner = jnp.where(
        (row * width + lane) // count == rank,
        jnp.concatenate([jnp.concatenate([bias] * (width // count), axis=1)] * 4, axis=0),
        0.0,
    )
    block = jnp.concatenate([placed, inner, jnp.zeros((4, width), f32)], axis=0)
    block = jnp.concatenate([block[:, : width // 2], block[:, width // 2 :]], axis=0)
    out[:, 5 * width : 5 * width + 256] = block.astype(bf16)
    common, third = 5 * width + 256, main.shape[1] - 5 * width - 256
    main[:, :common] = out[:, :common]
    main[:, common:] = jnp.where(
        lax.axis_index("rep") == 0,
        out[:, common : common + third].astype(f32),
        out[:, common + third :].astype(f32),
    ).astype(bf16)


def first_sum_kernel(mine, other, *refs):
    refs[-1][...] = (mine[...].astype(f32) + other[...].astype(f32)).astype(bf16)


def step_sum_kernel(far, mine_0, other_0, mine_1, other_1, come, *refs):
    out = refs[-1]
    _, core = ring_ids()
    half = come.shape[2]
    for k, (mine, other) in enumerate(((mine_0, other_0), (mine_1, other_1))):
        own = mine[0].astype(f32) + other[0].astype(f32)
        if far:
            here = core == 0
            come_k = come[k].astype(f32)
            out[k, :, :half] = (own[:, :half] + jnp.where(here, come_k, 0.0)).astype(bf16)
            out[k, :, half:] = (own[:, half:] + jnp.where(here, 0.0, come_k)).astype(bf16)
        else:
            out[k] = (own + come[k].astype(f32)).astype(bf16)


def near_sum_kernel(mine_0, other_0, mine_1, other_1, come, *refs):
    same, crossed = refs[-2:]
    _, core = ring_ids()
    first = mine_0[0].astype(f32) + other_0[0].astype(f32) + come[0].astype(f32)
    second = mine_1[0].astype(f32) + other_1[0].astype(f32) + come[1].astype(f32)
    same[...] = jnp.where(core == 0, first, second).astype(bf16)
    crossed[...] = jnp.where(core == 0, second, first).astype(bf16)


def last_sum_kernel(mine, other, a, b, *refs):
    refs[-1][...] = (
        mine[0].astype(f32) + other[0].astype(f32) + a[...].astype(f32) + b[...].astype(f32)
    ).astype(bf16)


def hold_kernel(*refs):
    pass


def hold(v, after):
    return pl.pallas_call(
        hold_kernel,
        out_shape=shape(v.shape, v.dtype),
        in_specs=[ANY] * (1 + len(after)),
        out_specs=ANY,
        input_output_aliases={0: 0},
        compiler_params=pltpu.CompilerParams(vmem_limit_bytes=2**20),
        cost_estimate=pl.CostEstimate(flops=0, bytes_accessed=0, transcendentals=0),
    )(v, *after)


def fence_kernel(*refs):
    refs[-1][...] = jnp.zeros(refs[-1].shape, f32)


def fence(arrays):
    return call(
        fence_kernel, shape((8, 128), f32), VMEM, [], arrays, [ANY] * len(arrays), 20, limit=2
    )


def chunk_spec(width, index):
    return pl.BlockSpec((1, 32, width), lambda i: (index, 0, 0))


class Reduction:
    def __init__(self, mine, mine_far, other, other_far, after=()):
        self.mine, self.mine_far = mine, mine_far
        other_far = hold(other_far, after) if after else other_far
        self.other, self.other_far = other, send(other_far, TO_CORE)
        self.width = mine.shape[2]
        self.distance = 4

    def follow(self, after=()):
        self.other = send(hold(self.other, after) if after else self.other, TO_CORE)
        return self

    def sums(self, kernel, shapes, places, partial, after):
        args, specs = [], []
        for place in places:
            args += [self.mine, self.other]
            specs += [chunk_spec(self.width, place)] * 2
        return call(
            kernel,
            shapes,
            [VMEM] * len(shapes),
            [],
            [*args, *partial, *after],
            [*specs, *[VMEM] * len(partial), *[ANY] * len(after)],
            0.5,
            limit=8,
            grid=(1,),
        )

    def advance(self, after=()):
        s = self.distance
        rows, pair = shape((32, self.width), bf16), shape((2, 32, self.width), bf16)
        places = [2 * (3 - s), 2 * (3 - s) + 1]
        self.distance -= 1
        if s == 0:
            made = self.sums(last_sum_kernel, [rows], [6], self.come, after)
            self.total = made[0]
            self.far = across(self.total)
        elif s == 4:
            made = self.sums(
                first_sum_kernel,
                [shape(self.mine_far.shape, bf16)],
                [],
                [self.mine_far, self.other_far],
                after,
            )
            self.come = [send(made[0], ALONG)]
        elif s > 1:
            kernel = functools.partial(step_sum_kernel, s == 3)
            made = self.sums(kernel, [pair], places, self.come, after)
            self.come = [send(made[0], ALONG)]
        else:
            made = self.sums(near_sum_kernel, [rows, rows], places, self.come, after)
            self.come = [send(made[0], ALONG), send(made[1], ACROSS)]
        return made

    def finish(self):
        while self.distance >= 0:
            self.advance()
        return self


def upper_result_kernel(both, both_far, inner_out, outer_out, token):
    token[...] = jnp.zeros(token.shape, f32)
    total = both[...].astype(f32) + both_far[...].astype(f32)
    hidden = inner_out.shape[1]
    inner_out[...] = total[:, :hidden]
    outer_out[...] = total[:, hidden:]


def lower_result_kernel(one, one_far, two, two_far, _, *refs):
    q_out, k_out, v_out, m_out, output_out = refs[:5]
    vector_outs, inner_out = refs[5:13], refs[13]
    width = output_out.shape[1]
    part = 64 * QUAD
    total = one[...].astype(f32) + one_far[...].astype(f32)
    output_out[...] = total[:, :width]
    pair = [total[:, width:], two[...].astype(f32) + two_far[...].astype(f32)]
    for i, out in enumerate((q_out, k_out, v_out)):
        for j in range(2):
            out[:, j * part : (j + 1) * part] = pair[j][:, i * part : (i + 1) * part]
    for i in range(2):
        for j in range(2):
            at = (2 * i + j) * part
            m_out[:, at : at + part] = pair[j][:, (3 + i) * part : (4 + i) * part]
    block = pair[1][:, 5 * part :]
    vectors = jnp.concatenate([block[:16], block[16:]], axis=1)
    rank = lax.axis_index("fsdp")
    quarter = lax.rem(rank, 4)

    def pick(v, index, size):
        found = jnp.zeros((v.shape[0], size), f32)
        for k in range(v.shape[1] // size):
            found += jnp.where(index == k, v[:, k * size : (k + 1) * size], 0.0)
        return found

    own = pick(pick(vectors[:8], lax.div(rank, 4), 128), quarter, 32)
    for i, out in enumerate(vector_outs):
        out[...] = own[i : i + 1]
    inner = pick(vectors[8:12], quarter, 128)
    found = jnp.zeros((1, 128), f32)
    for k in range(4):
        found += jnp.where(lax.div(rank, 4) == k, inner[k : k + 1], 0.0)
    inner_out[...] = found


def without_carried(kernel, n_in, n_carried, n_out, *refs):
    outs = refs[n_in + n_carried : n_in + n_carried + n_out]
    kernel(*refs[:n_in], *outs, *refs[n_in + n_out + 2 * n_carried :])


def call(
    kernel, out_shapes, out_specs, scratch, args, specs, micros, limit=20, grid=(), carried=()
):
    specs = list(specs)
    args = [
        pltpu.with_memory_space_constraint(v, pltpu.HBM) if spec is HBM else v
        for v, spec in zip(args, specs)
    ]
    single = not isinstance(out_specs, (list, tuple))
    shapes = [out_shapes] if single else list(out_shapes)
    spaces = [out_specs] if single else list(out_specs)
    shapes = [
        pltpu.HBM(v.shape, v.dtype) if spec is HBM else v for v, spec in zip(shapes, spaces)
    ]
    aliases = {}
    if carried:
        kernel = functools.partial(without_carried, kernel, len(args), len(carried), len(shapes))
        aliases = {len(args) + i: len(shapes) + i for i in range(len(carried))}
        args, specs = [*args, *carried], [*specs, *[ANY] * len(carried)]
        shapes += [shape(v.shape, v.dtype) for v in carried]
        spaces += [ANY] * len(carried)
        single = False
    return pl.pallas_call(
        kernel,
        grid=grid,
        out_shape=shapes[0] if single else tuple(shapes),
        in_specs=specs,
        out_specs=spaces[0] if single else tuple(spaces),
        input_output_aliases=aliases,
        scratch_shapes=scratch,
        compiler_params=pltpu.CompilerParams(vmem_limit_bytes=limit * 1024 * 1024),
        cost_estimate=pl.CostEstimate(
            flops=int(micros * 1e6), bytes_accessed=int(micros * 1e3), transcendentals=0
        ),
    )(*args)


def shape(dims, dtype):
    return jax.ShapeDtypeStruct(dims, dtype)


def per_device(ring, *args):
    (
        frames,
        memory_bank,
        cache_keys,
        cache_values,
        out_grad,
        first_gain,
        first_shift,
        query_weight,
        query_bias,
        key_weight,
        value_weight,
        value_bias,
        memory_weight,
        output_weight,
        output_bias,
        second_gain,
        second_shift,
        inner_weight,
        inner_bias,
        outer_weight,
        outer_bias,
    ) = args
    length, width = frames.shape
    ranks = width // first_gain.shape[0]
    part = width // ranks
    inner_part = inner_bias.shape[0]
    hidden = inner_part * ranks
    groups = -(-length // GROUP)
    padded = groups * GROUP
    extended = (groups - 1) * GROUP + SPAN
    quad = 64 * QUAD
    vectors = [
        first_gain,
        first_shift,
        query_bias,
        value_bias,
        output_bias,
        second_gain,
        second_shift,
        outer_bias,
    ]
    first = [query_weight, key_weight, value_weight, memory_weight]
    second = [output_weight.T, inner_weight, outer_weight.T]
    dma = pltpu.SemaphoreType.DMA
    row, wide_row = shape((length, width), bf16), shape((length, hidden), bf16)
    row_wide, vec_shape = shape((length, width), f32), shape((16, width), f32)
    turned = shape((width, length), bf16)

    def scratch_of(*shapes):
        return [pltpu.VMEM(v.shape, v.dtype) for v in shapes]

    if ring:
        common, third = shares(width, hidden)
        total = common + 2 * third
        weights, main = call(
            pack_first_kernel,
            (shape((part, total), bf16), shape((part, common + third), bf16)),
            [VMEM] * 2,
            [
                *([pltpu.VMEM((1, part), bf16)] * 8),
                pltpu.VMEM((1, inner_part), bf16),
                pltpu.SemaphoreType.DMA((16,)),
            ],
            [
                *first,
                *second,
                *(v.reshape(1, part) for v in vectors),
                inner_bias.reshape(1, inner_part),
            ],
            [HBM] * 16,
            1,
            limit=8,
        )
        vec = jnp.zeros((16, width), f32)
    else:
        weights = query_weight
        vec = jnp.concatenate(
            [
                jnp.stack([lax.all_gather(v, "fsdp", axis=0, tiled=True) for v in vectors]),
                lax.all_gather(inner_bias, "fsdp", axis=0, tiled=True).reshape(-1, width),
                jnp.zeros((4, width), bf16),
            ],
            axis=0,
        ).astype(f32)
    normal, bias_grad, nt, gt = gated(
        functools.partial(prepare_kernel, length),
        (row_wide, vec_shape, turned, turned),
        [VMEM, VMEM, HBM, HBM],
        [*scratch_of(turned, turned), dma((2,))],
        [frames, out_grad],
        [VMEM] * 2,
        3,
        [weights],
    )
    if ring:
        got = ring_gather(weights, main, common, [bias_grad])
        others = [v for v in got if v[2] in ("pair", "own")]
        items = both_cores([v for v in got if v[2] in ("all", "main", "common")])
        weights = whole_weights(
            items, ("all", "main", "common"), (width, common), common, [v[0] for v in others]
        )
    else:
        weights, second = (
            lax.all_gather(jnp.concatenate(v, axis=1), "fsdp", axis=0, tiled=True)
            for v in (first, second)
        )

    attended_shapes = (
        shape((padded, width), bf16),
        shape((extended, width), bf16),
        shape((extended, width), bf16),
        shape((16, 2 * width), bf16),
        shape((HEADS // QUAD, groups, KEYS, GROUP * QUAD), bf16),
    )
    *attended, ctx, vec, cols = call(
        functools.partial(attention_forward_kernel, ring, length),
        (
            *attended_shapes,
            shape((padded, width), bf16),
            vec_shape,
            shape((width, 16), f32),
        ),
        [VMEM] * 8,
        [pltpu.VMEM((2, KEYS, GROUP * QUAD), f32)],
        [normal, memory_bank, cache_keys, cache_values, vec, weights],
        [VMEM] * 6,
        6,
    )

    def grad_shapes(w):
        if ring:
            dims = [(7, 32, w), (2, 32, w // 2)]
            return tuple(shape(v, bf16) for v in dims + dims)
        return (shape((width, w), bf16),)

    grad_specs = [VMEM] * (4 if ring else 1)
    token_shape = shape((8, 128), f32)
    if ring:
        items += both_cores(others + got[-1:], [vec])
        second = whole_weights(
            items, ("all", "main", "pair", "own", "other"), (width, 2 * third), 0
        )
    residual, normed2, active, slope, *attended = call(
        functools.partial(inner_kernel, length),
        (row_wide, row, wide_row, wide_row),
        [VMEM] * 4,
        [],
        [frames, ctx, vec, second],
        [VMEM] * 4,
        5,
        carried=attended,
    )

    gi, vec_grads, active, residual, *attended = call(
        functools.partial(grad_inner_kernel, length),
        (wide_row, vec_shape),
        [VMEM] * 2,
        [],
        [out_grad, slope, bias_grad, second],
        [VMEM] * 4,
        2,
        carried=[active, residual, *attended],
    )
    results = call(
        functools.partial(hidden_weight_kernel, ring, length),
        grad_shapes(2 * hidden),
        grad_specs,
        [
            *scratch_of(turned, turned),
            pltpu.VMEM((width, 2 * hidden), bf16),
            dma((1,)),
        ],
        [normed2, gi, active, gt],
        [VMEM] * 3 + [HBM],
        5,
        carried=[residual, *attended],
    )
    both_grads, (residual, *attended) = results[:-6], results[-6:]
    both = Reduction(*both_grads).follow() if ring else None

    def steps(after, *reductions):
        made = []
        if ring:
            for reduction in reductions:
                made += reduction.advance([after])
        return made

    grad_att, grad_ctx, vec_grads, nt, grad_res, active, *attended = gated(
        functools.partial(grad_residual_kernel, length),
        (row, shape((padded, width), bf16), vec_shape, turned, row_wide),
        [VMEM] * 5,
        [dma((1,))],
        [gi, residual, out_grad, vec, vec_grads, second, nt],
        [VMEM] * 6 + [HBM],
        4,
        both_grads[:1],
        carried=[active, *attended],
    )
    made = steps(vec_grads, both)
    part_row = shape((length, quad), bf16)
    left_row = shape((LEAD, quad), f32)
    quad_shapes = (
        shape((padded, quad), bf16),
        part_row,
        part_row,
        left_row,
        left_row,
        shape((16, 2 * quad), bf16),
    )
    quad_scratch = [
        pltpu.VMEM((extended, quad), f32),
        pltpu.VMEM((extended, quad), f32),
        pltpu.VMEM((16, 2 * quad), f32),
    ]
    results = gated(
        functools.partial(quad_kernel, 0, ring, length),
        (*quad_shapes, vec_shape, *grad_shapes(width + 5 * quad)),
        [VMEM] * 7 + grad_specs,
        [
            *quad_scratch,
            pltpu.VMEM((width, width + 5 * quad), bf16),
            *scratch_of(turned),
        ],
        [memory_bank, grad_ctx, cols, vec_grads, nt, weights, *attended, grad_att, ctx],
        [VMEM] * 13,
        6,
        made,
        carried=[active, residual, grad_res],
    )
    quad_one, vec_grads, one_grads = results[:6], results[6], results[7:-3]
    carried = results[-3:]
    made = steps(vec_grads, both)
    one = Reduction(*one_grads, after=made).follow(made) if ring else None
    two_width = 5 * quad + (256 if ring else 0)
    results = gated(
        functools.partial(quad_kernel, 1, ring, length),
        (*quad_shapes, vec_shape, *grad_shapes(two_width)),
        [VMEM] * 7 + grad_specs,
        [*quad_scratch, pltpu.VMEM((width, two_width), bf16)],
        [memory_bank, grad_ctx, cols, vec_grads, nt, weights, *attended],
        [VMEM] * 11,
        6,
        made,
        carried=carried,
    )
    quad_two, vec_grads, two_grads = results[:6], results[6], results[7:-3]
    active, residual, grad_res = results[-3:]
    two = Reduction(*two_grads) if ring else None
    made = steps(vec_grads, both)
    made += steps(vec_grads, one)
    if ring:
        two.follow(made[:1])
    made = steps(made[-1] if ring else vec_grads, two)
    output, token, grad_res = gated(
        functools.partial(output_kernel, length),
        (row, token_shape),
        [VMEM] * 2,
        [],
        [active, residual, vec, second],
        [VMEM] * 4,
        3,
        made,
        carried=[grad_res],
    )
    if ring:
        made = one.advance([token]) + two.advance([token])
        both.advance([fence(made)])
        made = one.advance() + two.advance()
        made = both.advance([fence(made)])
        inner_sum, outer_sum, token = call(
            upper_result_kernel,
            (shape((part, hidden), f32), shape((part, hidden), f32), token_shape),
            [VMEM] * 3,
            [],
            [both.total, both.far],
            [VMEM] * 2,
            1,
            limit=8,
        )
        made = one.advance(made) + two.advance(made)
        token = fence(made)
        made = one.advance([token]) + two.advance([token])
        grad_frames, grad_bank, grad_ck, grad_cv, token = gated(
            functools.partial(lower_kernel, length),
            (
                row_wide,
                shape((1, MEM, width), f32),
                shape((LEFT, 1, width), f32),
                shape((LEFT, 1, width), f32),
                token_shape,
            ),
            [VMEM] * 5,
            [],
            [frames, grad_res, vec, weights, *quad_one, *quad_two],
            [VMEM] * 16,
            5,
            made,
        )
        square = shape((part, width), f32)
        q_sum, k_sum, v_sum, m_sum, output_sum, *own = call(
            lower_result_kernel,
            (
                square,
                square,
                square,
                shape((part, 2 * width), f32),
                square,
                *([shape((1, part), f32)] * 8),
                shape((1, inner_part), f32),
            ),
            [VMEM] * 14,
            [],
            [one.total, one.far, two.total, two.far, token],
            [VMEM] * 4 + [ANY],
            1,
            limit=8,
        )
        own_inner = own[8].reshape(inner_part)
        own = [v.reshape(part) for v in own[:8]]
    else:
        grad_frames, grad_bank, grad_ck, grad_cv, token = gated(
            functools.partial(lower_kernel, length),
            (
                row_wide,
                shape((1, MEM, width), f32),
                shape((LEFT, 1, width), f32),
                shape((LEFT, 1, width), f32),
                token_shape,
            ),
            [VMEM] * 5,
            [],
            [frames, grad_res, vec, weights, *quad_one, *quad_two],
            [VMEM] * 16,
            5,
            made,
        )

        def reduce(v):
            total = lax.psum_scatter(v, "fsdp", scatter_dimension=0, tiled=True)
            return lax.psum(total, "rep").astype(f32)

        total = reduce(both_grads[0])
        inner_sum, outer_sum = total[:, :hidden], total[:, hidden:]
        low, high = reduce(one_grads[0]), reduce(two_grads[0])
        output_sum = low[:, :width]
        sums = [v.reshape(part, 5, quad) for v in (low[:, width:], high)]
        q_sum, k_sum, v_sum, m_low, m_high = (
            jnp.concatenate([v[:, i] for v in sums], axis=1) for i in range(5)
        )
        m_sum = jnp.concatenate([m_low, m_high], axis=1)
        vec_sum = lax.psum(vec_grads, ("rep", "fsdp"))
        rank = lax.axis_index("fsdp")
        own = lax.dynamic_slice(vec_sum[:8], (0, rank * part), (8, part))
        own_inner = lax.dynamic_slice(
            vec_sum[8:12].reshape(-1), (rank * inner_part,), (inner_part,)
        )
    return (
        output,
        grad_frames,
        grad_bank,
        jnp.swapaxes(grad_ck, 0, 1),
        jnp.swapaxes(grad_cv, 0, 1),
        own[0],
        own[1],
        q_sum,
        own[2],
        k_sum,
        v_sum,
        own[3],
        m_sum,
        output_sum.T,
        own[4],
        own[5],
        own[6],
        inner_sum,
        own_inner,
        outer_sum.T,
        own[7],
    )


def without_gates(kernel, n_args, n_gates, *refs):
    kernel(*refs[:n_args], *refs[n_args + n_gates :])


def gated(kernel, out_shapes, out_specs, scratch, args, specs, micros, made, carried=()):
    return call(
        functools.partial(without_gates, kernel, len(args), len(made)),
        out_shapes,
        out_specs,
        scratch,
        [*args, *made],
        [*specs, *[ANY] * len(made)],
        micros,
        carried=carried,
    )


def solution(mesh):
    both = ("rep", "fsdp")
    rows, vector = P("fsdp", None), P("fsdp")
    columns = P(None, "fsdp")
    weights = (
        vector,
        vector,
        rows,
        vector,
        rows,
        rows,
        vector,
        rows,
        columns,
        vector,
        vector,
        vector,
        rows,
        vector,
        columns,
        vector,
    )
    blocks = P(both, None, None)
    in_specs = (P(both, None), blocks, blocks, blocks, P(both, None), *weights)
    out_specs = (P(both, None), P(both, None), blocks, blocks, blocks, *weights)
    ring = mesh.shape["fsdp"] == 16 and mesh.shape["rep"] == 2
    return jax.shard_map(
        functools.partial(per_device, ring),
        mesh=mesh,
        in_specs=in_specs,
        out_specs=out_specs,
        check_vma=False,
    )
```

```python
import functools

import jax
import jax.numpy as jnp
from jax import lax
from jax.experimental import pallas as pl
from jax.experimental.pallas import tpu as pltpu
from jax.sharding import PartitionSpec as P

HEADS = 8
SEG = 16
RIGHT = 4
LEFT = 30
MEM = 4

LEAD = 32
GROUP = 64
SPAN = 112
KEYS = 128
QUAD = 4
masked_value = -1e30
epsilon = 1e-05
gelu_a = 0.7978845608028654
gelu_b = gelu_a * 0.044715

bf16 = jnp.bfloat16
f32 = jnp.float32
VMEM = pl.BlockSpec(memory_space=pltpu.VMEM)
ANY = pl.BlockSpec(memory_space=pl.ANY)
HBM = pl.BlockSpec(memory_space=pltpu.HBM)


def dot(a, b):
    return lax.dot_general(a, b, (((1,), (0,)), ((), ())), preferred_element_type=f32)


def dot_nt(a, b):
    return lax.dot_general(a, b, (((1,), (1,)), ((), ())), preferred_element_type=f32)


def dot_tn(a, b):
    return lax.dot_general(a, b, (((0,), (0,)), ((), ())), preferred_element_type=f32)


def row_tiles(rows):
    return [(start, min(256, rows - start)) for start in range(0, rows, 256)]


def centred(v):
    center = v - jnp.mean(v, axis=-1, keepdims=True)
    spread = jnp.mean(center * center, axis=-1, keepdims=True)
    scale = lax.rsqrt(spread + epsilon)
    return center * scale, scale


def norm_back(e, n, scale, gain):
    eg = e * gain
    return scale * (
        eg - jnp.mean(eg, axis=-1, keepdims=True) - n * jnp.mean(eg * n, axis=-1, keepdims=True)
    )


def colsum(v):
    return jnp.sum(v, axis=0, keepdims=True)


RING = (0, 2, 4, 6, 7, 5, 3, 1)


def ring_pairs(step):
    pairs = []
    for k in range(8):
        for core in range(2):
            pairs.append((2 * RING[k] + core, 2 * RING[(k + step) % 8] + core))
    return pairs


TO_RIGHT, TO_LEFT = ring_pairs(1), ring_pairs(-1)
TO_CORE = [(i, i ^ 1) for i in range(16)]


def two_way(cross):
    pairs = []
    for k in range(8):
        pairs.append((2 * RING[k], 2 * RING[(k + 1) % 8] + cross))
        pairs.append((2 * RING[k] + 1, 2 * RING[(k - 1) % 8] + 1 - cross))
    return pairs


ALONG, ACROSS = two_way(0), two_way(1)


def ring_ids():
    rank = lax.axis_index("fsdp")
    core, chip = lax.rem(rank, 2), lax.div(rank, 2)
    z, x = lax.div(chip, 2), lax.rem(chip, 2)
    return jnp.where(x == 0, z, 7 - z), core


def ring_rank(position, core):
    position = lax.rem(position, 8)
    return 2 * jnp.where(position < 4, 2 * position, 15 - 2 * position) + core


def halves(width):
    return width // 2 // 128 * 128


def send(v, pairs):
    return lax.ppermute(v, "fsdp", pairs)


def across(v):
    return lax.ppermute(v, "rep", [(0, 1), (1, 0)])


def shares(width, hidden):
    return 5 * width + 256, (width + 2 * hidden) // 2


def ring_gather(shard, main, common, after):
    third = main.shape[1] - common
    got = [(shard, 0, "all")]
    a = b = main
    for step in (1, 2, 3):
        a, b = send(a, TO_RIGHT), send(b, TO_LEFT)
        pair = call(
            tails_kernel,
            shape((shard.shape[0], 2 * third), bf16),
            VMEM,
            [],
            [a, b],
            [VMEM] * 2,
            0.3,
            limit=4,
        )
        pair = across(pair)
        if step == 1:
            pair = hold(pair, after)
        got += [(a, 8 - step, "main"), (b, step, "main"), (pair, step, "pair")]
    a, b = send(a[:, :common], TO_RIGHT), send(b[:, common:], TO_LEFT)
    return got + [(a, 4, "common"), (b, 4, "own"), (across(b), 4, "other")]


def both_cores(items, after=()):
    items = [(hold(v, after) if after else v, d, k) for v, d, k in items]
    return [(v, d, 0, k) for v, d, k in items] + [(send(v, TO_CORE), d, 1, k) for v, d, k in items]


def tails_kernel(a, b, *refs):
    out = refs[-1]
    third = out.shape[1] // 2
    out[:, :third] = a[:, a.shape[1] - third :]
    out[:, third:] = b[:, b.shape[1] - third :]


def lay_rows(places, common, *refs):
    refs, whole = refs[: len(places)], refs[-1]
    position, core = ring_ids()
    replica = lax.axis_index("rep")
    third = whole.shape[1] // 2
    own = pl.ds(pl.multiple_of(replica * third, 128), third)
    other = pl.ds(pl.multiple_of((1 - replica) * third, 128), third)

    def rows(distance, flip):
        owner = ring_rank(position + distance, core if flip == 0 else 1 - core)
        return pl.ds(pl.multiple_of(owner * 32, 32), 32)

    for ref, (distance, flip, kind) in zip(refs, places):
        at = rows(distance, flip)
        if common:
            whole[at, :] = ref[:, :common]
        elif kind == "all":
            whole[at, :] = ref[:, ref.shape[1] - 2 * third :]
        elif kind == "main":
            whole[at, own] = ref[:, ref.shape[1] - third :]
        elif kind == "pair":
            whole[rows(8 - distance, flip), other] = ref[:, :third]
            whole[at, other] = ref[:, third:]
        else:
            whole[at, own if kind == "own" else other] = ref[...]


def whole_weights(items, kinds, dims, common, after=()):
    items = [v for v in items if v[3] in kinds]
    return call(
        functools.partial(lay_rows, tuple(v[1:] for v in items), common),
        shape(dims, bf16),
        VMEM,
        [],
        [*(v[0] for v in items), *after],
        [VMEM] * len(items) + [ANY] * len(after),
        0.5,
        limit=24,
    )


def spread(ring, grads, outs):
    if not ring:
        outs[0][...] = grads[...]
        return
    position, core = ring_ids()
    mine, mine_far, other, other_far = outs
    half = mine_far.shape[2]
    way = 1 - 2 * core

    def rows(place, k):
        return pl.ds(pl.multiple_of(ring_rank(place, k) * 32, 32), 32)

    def lanes(k):
        return pl.ds(pl.multiple_of(k * half, 128), half)

    for k in range(2):
        for distance in (3, 2, 1):
            at = 2 * (3 - distance) + k
            mine[at] = grads[rows(position + 8 + way * distance, k), :]
            other[at] = grads[rows(position + 8 - way * distance, k), :]
        mine_far[k] = grads[rows(position + 4, k), lanes(core)]
        other_far[k] = grads[rows(position + 4, k), lanes(1 - core)]
    mine[6] = grads[rows(position, core), :]
    other[6] = grads[rows(position, 1 - core), :]


def start_all(pairs, sems, first=0):
    copies = [pltpu.make_async_copy(a, b, sems.at[first + i]) for i, (a, b) in enumerate(pairs)]
    for copy in copies:
        copy.start()
    return copies


def wait_all(copies):
    for copy in copies:
        copy.wait()


def columns(width, hidden):
    return width, width + hidden, width + 2 * hidden


def head_masks():
    lane = lax.broadcasted_iota(jnp.int32, (1, 64 * QUAD), 1)
    return [(lane // 64 == h).astype(f32) for h in range(QUAD)]


def stacked(rows, masks):
    return jnp.concatenate([rows * m for m in masks], axis=0)


def unstacked(wide, masks):
    parts = [wide[GROUP * h : GROUP * (h + 1)] * masks[h] for h in range(QUAD)]
    return parts[0] + parts[1] + parts[2] + parts[3]


def added_mask(limit):
    row = lax.broadcasted_iota(jnp.int32, (KEYS, GROUP * QUAD), 0)
    query = lax.rem(lax.broadcasted_iota(jnp.int32, (KEYS, GROUP * QUAD), 1), GROUP)
    first = query // SEG * SEG + (LEAD - LEFT)
    inside = (row >= first) & (row < first + LEFT + SEG + RIGHT) & (row < limit)
    bank = (row >= SPAN) & (row < SPAN + MEM)
    return jnp.where((inside & (row < SPAN)) | bank, 0.0, masked_value)


def prepare_kernel(length, frames, out_grad, n_out, bias_out, nt_out, gt_out, nt, gt, sems):
    for start, size in row_tiles(length):
        rows = slice(start, start + size)
        n, _ = centred(frames[rows].astype(f32))
        n_out[rows] = n
        nt[:, rows] = n.astype(bf16).T
        gt[:, rows] = out_grad[rows].T
    copies = start_all([(nt, nt_out), (gt, gt_out)], sems)
    bias_out[...] = jnp.zeros(bias_out.shape, f32)
    bias_out[7:8] = colsum(out_grad[...].astype(f32))
    wait_all(copies)


def attention_forward_kernel(ring, length, *refs):
    normal, bank, cache_k, cache_v, vec, w = refs[:6]
    q, kext, vext, kvmem, pt, ctx, vec_out, cols_out, mask = refs[6:]
    width = normal.shape[1]
    groups = q.shape[0] // GROUP
    if not ring:
        vectors = vec[...]
    else:
        blocks = w[:, 5 * width :].astype(f32).reshape(16, 32, 256)
        total = jnp.sum(blocks, axis=0)
        vectors = jnp.concatenate([total[:16], total[16:]], axis=1)
    vec_out[...] = vectors
    cols_out[...] = vectors.T

    def left_rows(cache):
        rows = cache[0].astype(f32)
        return jnp.concatenate([jnp.zeros((LEAD - LEFT, width), f32), rows], axis=0).astype(bf16)

    kext[0:LEAD] = left_rows(cache_k)
    vext[0:LEAD] = left_rows(cache_v)
    tail = kext.shape[0] - LEAD - length
    kext[LEAD + length :] = jnp.zeros((tail, width), bf16)
    vext[LEAD + length :] = jnp.zeros((tail, width), bf16)
    q[length:] = jnp.zeros((q.shape[0] - length, width), bf16)
    bank_rows = jnp.concatenate(
        [bank[0].astype(f32), jnp.zeros((16 - MEM, width), f32)], axis=0
    ).astype(bf16)
    kvmem[...] = dot(bank_rows, w[:, 3 * width : 5 * width]).astype(bf16)

    for start, size in row_tiles(length):
        rows = (normal[start : start + size] * vectors[0:1] + vectors[1:2]).astype(bf16)
        q[start : start + size] = (dot(rows, w[:, :width]) + vectors[2:3]).astype(bf16)
        kext[LEAD + start : LEAD + start + size] = dot(rows, w[:, width : 2 * width]).astype(bf16)
        vext[LEAD + start : LEAD + start + size] = (
            dot(rows, w[:, 2 * width : 3 * width]) + vectors[3:4]
        ).astype(bf16)

    masks = head_masks()
    scale = 64**-0.5
    q_masks = [(m * scale).astype(bf16) for m in masks]
    mask[0] = added_mask(KEYS)
    mask[1] = added_mask(LEAD + length - GROUP * (groups - 1))

    def step(g, carry):
        top = pl.multiple_of(g * GROUP, GROUP)
        hidden = mask[(g == groups - 1).astype(jnp.int32)]
        for j in range(HEADS // QUAD):
            lanes = slice(64 * QUAD * j, 64 * QUAD * (j + 1))
            keys = jnp.concatenate([kext[pl.ds(top, SPAN), lanes], kvmem[:, lanes]], axis=0)
            values = jnp.concatenate(
                [vext[pl.ds(top, SPAN), lanes], kvmem[:, width + lanes.start : width + lanes.stop]],
                axis=0,
            )
            queries = stacked(q[pl.ds(top, GROUP), lanes], q_masks)
            scores = dot_nt(keys, queries) + hidden
            raised = jnp.exp(scores - jnp.max(scores, axis=0, keepdims=True))
            weights = (raised / jnp.sum(raised, axis=0, keepdims=True)).astype(bf16)
            pt[j, g] = weights
            ctx[pl.ds(top, GROUP), lanes] = unstacked(dot_tn(weights, values), masks).astype(bf16)
        return carry

    lax.fori_loop(0, groups, step, 0, unroll=6)


def inner_kernel(length, *refs):
    frames, ctx, vec, w, residual, normed2, active, slope = refs
    width = frames.shape[1]
    hidden = active.shape[1]
    second, _, _ = columns(width, hidden)
    for start, size in row_tiles(length):
        rows = slice(start, start + size)
        res = frames[rows].astype(f32) + dot_nt(ctx[rows], w[:, :second]) + vec[4:5]
        residual[rows] = res
        n, _ = centred(res)
        normed2[rows] = (n * vec[5:6] + vec[6:7]).astype(bf16)

    block = 512
    for b in range(hidden // block):
        cols = slice(b * block, (b + 1) * block)
        for start, size in row_tiles(length):
            rows = slice(start, start + size)
            u = dot(normed2[rows], w[:, second + cols.start : second + cols.stop]) + vec[8 + b : 9 + b]
            uu = u * u
            h = 0.5 + 0.5 * jnp.tanh(u * (gelu_a + gelu_b * uu))
            act = u * h
            active[rows, cols] = act.astype(bf16)
            slope[rows, cols] = (
                h + act * (1.0 - h) * (2 * gelu_a + 6 * gelu_b * uu)
            ).astype(bf16)


def grad_inner_kernel(length, out_grad, slope, vec_before, w, gi, vec_grads):
    width, hidden = out_grad.shape[1], slope.shape[1]
    third = columns(width, hidden)[1]
    block = 512
    vec_grads[...] = vec_before[...]
    for b in range(hidden // block):
        cols = slice(b * block, (b + 1) * block)
        sums = jnp.zeros((1, block), f32)
        for start, size in row_tiles(length):
            rows = slice(start, start + size)
            up = dot(out_grad[rows], w[:, third + cols.start : third + cols.stop])
            part = (up * slope[rows, cols].astype(f32)).astype(bf16)
            gi[rows, cols] = part
            sums += colsum(part.astype(f32))
        vec_grads[8 + b : 9 + b] = sums


def output_kernel(length, active, residual, vec, w, output, token):
    _, third, last = columns(residual.shape[1], active.shape[1])
    token[...] = jnp.zeros(token.shape, f32)
    for start, size in row_tiles(length):
        rows = slice(start, start + size)
        output[rows] = (residual[rows] + dot_nt(active[rows], w[:, third:last]) + vec[7:8]).astype(bf16)


def hidden_weight_kernel(ring, length, *refs):
    normed2, gi, active, gt_in = refs[:4]
    outs, (n2t, gt, grads, sems) = refs[4:-4], refs[-4:]
    hidden = gi.shape[1]
    copies = start_all([(gt_in, gt)], sems)
    for start, size in row_tiles(length):
        rows = slice(start, start + size)
        n2t[:, rows] = normed2[rows].T
    for at in range(0, hidden, 512):
        grads[:, at : at + 512] = dot(n2t[...], gi[:, at : at + 512]).astype(bf16)
    wait_all(copies)
    for at in range(0, hidden, 512):
        cols = slice(hidden + at, hidden + at + 512)
        grads[:, cols] = dot(gt[...], active[:, at : at + 512]).astype(bf16)
    spread(ring, grads, outs)


def grad_residual_kernel(length, *refs):
    gi, residual, out_grad, vec, vec_before, w, nt_in = refs[:7]
    grad_att, grad_ctx, vec_grads, nt, grad_res, sems = refs[7:]
    width = residual.shape[1]
    copies = start_all([(nt_in, nt)], sems)
    second, third, _ = columns(width, gi.shape[1])
    sums = [jnp.zeros((1, width), f32) for _ in range(3)]
    for start, size in row_tiles(length):
        rows = slice(start, start + size)
        e = dot_nt(gi[rows], w[:, second:third])
        n, scale = centred(residual[rows])
        gres = out_grad[rows].astype(f32) + norm_back(e, n, scale, vec[5:6])
        grad_res[rows] = gres
        gat_rows = gres.astype(bf16)
        grad_att[rows] = gat_rows
        grad_ctx[rows] = dot(gat_rows, w[:, :second]).astype(bf16)
        sums = [s + colsum(v) for s, v in zip(sums, (gat_rows.astype(f32), e * n, e))]
    grad_ctx[length:] = jnp.zeros((grad_ctx.shape[0] - length, width), bf16)
    vec_grads[...] = vec_before[...]
    for i in range(3):
        vec_grads[4 + i : 5 + i] = sums[i]
    wait_all(copies)


def attention_backward(j, attended, grad_ctx, gk, gv, gkm, gq):
    q, kext, vext, kvmem, pt = attended
    width = q.shape[1]
    groups = q.shape[0] // GROUP
    size = 64 * QUAD
    lanes = slice(size * j, size * (j + 1))
    value_lanes = slice(width + size * j, width + size * (j + 1))
    gk[...] = jnp.zeros(gk.shape, f32)
    gv[...] = jnp.zeros(gv.shape, f32)
    gkm[...] = jnp.zeros(gkm.shape, f32)
    masks = head_masks()
    scale = 64**-0.5
    q_masks = [(m * scale).astype(bf16) for m in masks]
    c_masks = [m.astype(bf16) for m in masks]
    out_masks = [m * scale for m in masks]

    def step(g, carry):
        top = pl.multiple_of(g * GROUP, GROUP)
        keys = jnp.concatenate([kext[pl.ds(top, SPAN), lanes], kvmem[:, lanes]], axis=0)
        values = jnp.concatenate([vext[pl.ds(top, SPAN), lanes], kvmem[:, value_lanes]], axis=0)
        queries = stacked(q[pl.ds(top, GROUP), lanes], q_masks)
        upstream = stacked(grad_ctx[pl.ds(top, GROUP), lanes], c_masks)
        weights = pt[j, g]
        wide = weights.astype(f32)
        gp = dot_nt(values, upstream)
        gs = (wide * (gp - colsum(gp * wide))).astype(bf16)
        gkeys = dot(gs, queries)
        gvalues = dot(weights, upstream)
        gk[pl.ds(top, SPAN)] += gkeys[:SPAN]
        gv[pl.ds(top, SPAN)] += gvalues[:SPAN]
        gkm[:, :size] += gkeys[SPAN:]
        gkm[:, size:] += gvalues[SPAN:]
        gq[pl.ds(top, GROUP)] = unstacked(dot_tn(gs, keys), out_masks).astype(bf16)
        return carry

    lax.fori_loop(0, groups, step, 0, unroll=6)


def bank_block(bank, width):
    return jnp.concatenate(
        [bank[0].astype(f32), jnp.zeros((16 - MEM, width), f32)], axis=0
    ).astype(bf16)


def pair_of(row):
    high = row.astype(bf16).astype(f32)
    zeros = jnp.zeros((14, row.shape[1]), f32)
    return jnp.concatenate([high, row - high, zeros], axis=0).astype(bf16)


def quad_kernel(j, length, *refs):
    grad_ctx, *attended = refs[:6]
    gq, gk_rows, gv_rows, gk_left, gv_left, gbank, gk, gv, gkm = refs[6:]
    attention_backward(j, attended, grad_ctx, gk, gv, gkm, gq)
    gk_left[...] = gk[0:LEAD]
    gv_left[...] = gv[0:LEAD]
    gk_rows[...] = gk[LEAD : LEAD + length].astype(bf16)
    gv_rows[...] = gv[LEAD : LEAD + length].astype(bf16)
    gbank[...] = gkm[...].astype(bf16)


def quad_weight_kernel(j, ring, length, *refs):
    bank, cols, vec_before, nt, w, gq, gk_rows, gv_rows, gbank = refs[:9]
    width = nt.shape[0]
    size = 64 * QUAD
    first = width * (1 - j)
    refs = refs[9:]
    if j == 0:
        grad_att, ctx = refs[:2]
        refs = refs[2:]
    n_out = 4 if ring else 1
    vec_grads, *outs = refs[: 1 + n_out]
    grads, *rest = refs[1 + n_out :]
    if j == 0:
        gat = rest[0]
        for start, count in row_tiles(length):
            rows = slice(start, start + count)
            gat[:, rows] = grad_att[rows].T
        grads[:, :width] = dot(gat[...], ctx[:length]).astype(bf16)
    gain, shift = cols[:, 0:1], cols[:, 1:2]
    gains, shifts = jnp.zeros((width, 1), f32), jnp.zeros((16, width), f32)
    sums = []
    for i, g in enumerate((gq[:length], gk_rows[...], gv_rows[...])):
        m = dot(nt[...], g)
        sums.append(colsum(g.astype(f32)))
        at = first + i * size
        grads[:, at : at + size] = (gain * m + shift * sums[i]).astype(bf16)
        own = slice(i * width + j * size, i * width + (j + 1) * size)
        gains += jnp.sum(w[:, own].astype(f32) * m, axis=1, keepdims=True)
        shifts += dot_nt(pair_of(sums[i]), w[:, own])
    at = first + 3 * size
    grads[:, at : at + 2 * size] = dot_tn(bank_block(bank, width), gbank[...]).astype(bf16)
    vec_grads[...] = vec_before[...]
    vec_grads[0:1] += jnp.transpose(jnp.broadcast_to(gains, (width, 128)))[0:1]
    vec_grads[1:2] += colsum(shifts)
    vec_grads[2:3, size * j : size * (j + 1)] = sums[0]
    vec_grads[3:4, size * j : size * (j + 1)] = sums[2]
    if j == 1 and ring:
        vectors = vec_grads[...]
        block = jnp.concatenate([vectors[:, :256], vectors[:, 256:]], axis=0).astype(bf16)
        grads[:, at + 2 * size :] = jnp.concatenate([block] * 16, axis=0)
    spread(ring, grads, outs)


def lower_kernel(length, *refs):
    frames, grad_res, vec, w = refs[:4]
    gq, gk, gv, gk_left, gv_left, gbank = ([refs[4 + i], refs[10 + i]] for i in range(6))
    grad_frames, grad_bank, grad_ck, grad_cv, token = refs[16:]
    token[...] = jnp.zeros(token.shape, f32)
    width = frames.shape[1]
    part = gq[0].shape[1]
    for out, parts in ((grad_ck, gk_left), (grad_cv, gv_left)):
        left = jnp.concatenate([v[...] for v in parts], axis=1)
        for row in range(LEFT):
            out[row] = left[LEAD - LEFT + row : LEAD - LEFT + row + 1]
    bank_grads = jnp.concatenate(
        [v[:, at : at + part] for at in (0, part) for v in gbank], axis=1
    )
    grad_bank[0] = dot_nt(bank_grads, w[:, 3 * width : 5 * width])[:MEM]
    for start, size in row_tiles(length):
        rows = slice(start, start + size)
        parts = [jnp.concatenate([v[rows] for v in pair], axis=1) for pair in (gq, gk, gv)]
        e = (
            dot_nt(parts[0], w[:, :width])
            + dot_nt(parts[1], w[:, width : 2 * width])
            + dot_nt(parts[2], w[:, 2 * width : 3 * width])
        )
        n, s = centred(frames[rows].astype(f32))
        grad_frames[rows] = grad_res[rows] + norm_back(e, n, s, vec[0:1])


def pack_first_kernel(*refs):
    weights, vectors, inner_bias, out, main = refs[:7], refs[7:15], refs[15], refs[16], refs[17]
    held, bias_held, sems = refs[18:26], refs[26], refs[27]
    width = weights[0].shape[1]
    column = 0
    copies = []
    for i, ref in enumerate(weights):
        if i == 4:
            column += 256
        copies.append((ref, out.at[:, pl.ds(column, ref.shape[1])]))
        column += ref.shape[1]
    copies += list(zip((*vectors, inner_bias), (*held, bias_held)))
    copies = [pltpu.make_async_copy(a, b, sems.at[i]) for i, (a, b) in enumerate(copies)]
    for copy in copies:
        copy.start()
    wait_all(copies)
    rank = lax.axis_index("fsdp")
    own = jnp.concatenate([ref[...].astype(f32) for ref in held], axis=0)
    part = own.shape[1]
    placed = jnp.where(
        lax.broadcasted_iota(jnp.int32, (8, width), 1) // part == rank,
        jnp.concatenate([own] * (width // part), axis=1),
        0.0,
    )
    bias = bias_held[...].astype(f32)
    count = bias.shape[1]
    row = lax.broadcasted_iota(jnp.int32, (4, width), 0)
    lane = lax.broadcasted_iota(jnp.int32, (4, width), 1)
    inner = jnp.where(
        (row * width + lane) // count == rank,
        jnp.concatenate([jnp.concatenate([bias] * (width // count), axis=1)] * 4, axis=0),
        0.0,
    )
    block = jnp.concatenate([placed, inner, jnp.zeros((4, width), f32)], axis=0)
    block = jnp.concatenate([block[:, : width // 2], block[:, width // 2 :]], axis=0)
    out[:, 5 * width : 5 * width + 256] = block.astype(bf16)
    common, third = 5 * width + 256, main.shape[1] - 5 * width - 256
    main[:, :common] = out[:, :common]
    main[:, common:] = jnp.where(
        lax.axis_index("rep") == 0,
        out[:, common : common + third].astype(f32),
        out[:, common + third :].astype(f32),
    ).astype(bf16)


def first_sum_kernel(mine, other, *refs):
    refs[-1][...] = (mine[...].astype(f32) + other[...].astype(f32)).astype(bf16)


def step_sum_kernel(far, mine_0, other_0, mine_1, other_1, come, *refs):
    out = refs[-1]
    _, core = ring_ids()
    half = come.shape[2]
    for k, (mine, other) in enumerate(((mine_0, other_0), (mine_1, other_1))):
        own = mine[0].astype(f32) + other[0].astype(f32)
        if far:
            here = core == 0
            come_k = come[k].astype(f32)
            out[k, :, :half] = (own[:, :half] + jnp.where(here, come_k, 0.0)).astype(bf16)
            out[k, :, half:] = (own[:, half:] + jnp.where(here, 0.0, come_k)).astype(bf16)
        else:
            out[k] = (own + come[k].astype(f32)).astype(bf16)


def near_sum_kernel(mine_0, other_0, mine_1, other_1, come, *refs):
    same, crossed = refs[-2:]
    _, core = ring_ids()
    first = mine_0[0].astype(f32) + other_0[0].astype(f32) + come[0].astype(f32)
    second = mine_1[0].astype(f32) + other_1[0].astype(f32) + come[1].astype(f32)
    same[...] = jnp.where(core == 0, first, second).astype(bf16)
    crossed[...] = jnp.where(core == 0, second, first).astype(bf16)


def last_sum_kernel(mine, other, a, b, *refs):
    refs[-1][...] = (
        mine[0].astype(f32) + other[0].astype(f32) + a[...].astype(f32) + b[...].astype(f32)
    ).astype(bf16)


def hold_kernel(*refs):
    pass


def hold(v, after):
    return pl.pallas_call(
        hold_kernel,
        out_shape=shape(v.shape, v.dtype),
        in_specs=[ANY] * (1 + len(after)),
        out_specs=ANY,
        input_output_aliases={0: 0},
        compiler_params=pltpu.CompilerParams(vmem_limit_bytes=2**20),
        cost_estimate=pl.CostEstimate(flops=0, bytes_accessed=0, transcendentals=0),
    )(v, *after)


def fence_kernel(*refs):
    refs[-1][...] = jnp.zeros(refs[-1].shape, f32)


def fence(arrays):
    return call(
        fence_kernel, shape((8, 128), f32), VMEM, [], arrays, [ANY] * len(arrays), 20, limit=2
    )


def chunk_spec(width, index):
    return pl.BlockSpec((1, 32, width), lambda i: (index, 0, 0))


class Reduction:
    def __init__(self, mine, mine_far, other, other_far, after=()):
        self.mine, self.mine_far = mine, mine_far
        other_far = hold(other_far, after) if after else other_far
        self.other, self.other_far = other, send(other_far, TO_CORE)
        self.width = mine.shape[2]
        self.distance = 4

    def follow(self, after=()):
        self.other = send(hold(self.other, after) if after else self.other, TO_CORE)
        return self

    def sums(self, kernel, shapes, places, partial, after):
        args, specs = [], []
        for place in places:
            args += [self.mine, self.other]
            specs += [chunk_spec(self.width, place)] * 2
        return call(
            kernel,
            shapes,
            [VMEM] * len(shapes),
            [],
            [*args, *partial, *after],
            [*specs, *[VMEM] * len(partial), *[ANY] * len(after)],
            0.5,
            limit=8,
            grid=(1,),
        )

    def advance(self, after=()):
        s = self.distance
        rows, pair = shape((32, self.width), bf16), shape((2, 32, self.width), bf16)
        places = [2 * (3 - s), 2 * (3 - s) + 1]
        self.distance -= 1
        if s == 0:
            made = self.sums(last_sum_kernel, [rows], [6], self.come, after)
            self.total = made[0]
            self.far = across(self.total)
        elif s == 4:
            made = self.sums(
                first_sum_kernel,
                [shape(self.mine_far.shape, bf16)],
                [],
                [self.mine_far, self.other_far],
                after,
            )
            self.come = [send(made[0], ALONG)]
        elif s > 1:
            kernel = functools.partial(step_sum_kernel, s == 3)
            made = self.sums(kernel, [pair], places, self.come, after)
            self.come = [send(made[0], ALONG)]
        else:
            made = self.sums(near_sum_kernel, [rows, rows], places, self.come, after)
            self.come = [send(made[0], ALONG), send(made[1], ACROSS)]
        return made

    def finish(self):
        while self.distance >= 0:
            self.advance()
        return self


def upper_result_kernel(both, both_far, inner_out, outer_out, token):
    token[...] = jnp.zeros(token.shape, f32)
    total = both[...].astype(f32) + both_far[...].astype(f32)
    hidden = inner_out.shape[1]
    inner_out[...] = total[:, :hidden]
    outer_out[...] = total[:, hidden:]


def lower_result_kernel(one, one_far, two, two_far, _, *refs):
    q_out, k_out, v_out, m_out, output_out = refs[:5]
    vector_outs, inner_out = refs[5:13], refs[13]
    width = output_out.shape[1]
    part = 64 * QUAD
    total = one[...].astype(f32) + one_far[...].astype(f32)
    output_out[...] = total[:, :width]
    pair = [total[:, width:], two[...].astype(f32) + two_far[...].astype(f32)]
    for i, out in enumerate((q_out, k_out, v_out)):
        for j in range(2):
            out[:, j * part : (j + 1) * part] = pair[j][:, i * part : (i + 1) * part]
    for i in range(2):
        for j in range(2):
            at = (2 * i + j) * part
            m_out[:, at : at + part] = pair[j][:, (3 + i) * part : (4 + i) * part]
    block = pair[1][:, 5 * part :]
    vectors = jnp.concatenate([block[:16], block[16:]], axis=1)
    rank = lax.axis_index("fsdp")
    quarter = lax.rem(rank, 4)

    def pick(v, index, size):
        found = jnp.zeros((v.shape[0], size), f32)
        for k in range(v.shape[1] // size):
            found += jnp.where(index == k, v[:, k * size : (k + 1) * size], 0.0)
        return found

    own = pick(pick(vectors[:8], lax.div(rank, 4), 128), quarter, 32)
    for i, out in enumerate(vector_outs):
        out[...] = own[i : i + 1]
    inner = pick(vectors[8:12], quarter, 128)
    found = jnp.zeros((1, 128), f32)
    for k in range(4):
        found += jnp.where(lax.div(rank, 4) == k, inner[k : k + 1], 0.0)
    inner_out[...] = found


def without_carried(kernel, n_in, n_carried, n_out, *refs):
    outs = refs[n_in + n_carried : n_in + n_carried + n_out]
    kernel(*refs[:n_in], *outs, *refs[n_in + n_out + 2 * n_carried :])


def call(
    kernel, out_shapes, out_specs, scratch, args, specs, micros, limit=20, grid=(), carried=()
):
    specs = list(specs)
    args = [
        pltpu.with_memory_space_constraint(v, pltpu.HBM) if spec is HBM else v
        for v, spec in zip(args, specs)
    ]
    single = not isinstance(out_specs, (list, tuple))
    shapes = [out_shapes] if single else list(out_shapes)
    spaces = [out_specs] if single else list(out_specs)
    shapes = [
        pltpu.HBM(v.shape, v.dtype) if spec is HBM else v for v, spec in zip(shapes, spaces)
    ]
    aliases = {}
    if carried:
        kernel = functools.partial(without_carried, kernel, len(args), len(carried), len(shapes))
        aliases = {len(args) + i: len(shapes) + i for i in range(len(carried))}
        args, specs = [*args, *carried], [*specs, *[ANY] * len(carried)]
        shapes += [shape(v.shape, v.dtype) for v in carried]
        spaces += [ANY] * len(carried)
        single = False
    return pl.pallas_call(
        kernel,
        grid=grid,
        out_shape=shapes[0] if single else tuple(shapes),
        in_specs=specs,
        out_specs=spaces[0] if single else tuple(spaces),
        input_output_aliases=aliases,
        scratch_shapes=scratch,
        compiler_params=pltpu.CompilerParams(vmem_limit_bytes=limit * 1024 * 1024),
        cost_estimate=pl.CostEstimate(
            flops=int(micros * 1e6), bytes_accessed=int(micros * 1e3), transcendentals=0
        ),
    )(*args)


def shape(dims, dtype):
    return jax.ShapeDtypeStruct(dims, dtype)


def per_device(ring, *args):
    (
        frames,
        memory_bank,
        cache_keys,
        cache_values,
        out_grad,
        first_gain,
        first_shift,
        query_weight,
        query_bias,
        key_weight,
        value_weight,
        value_bias,
        memory_weight,
        output_weight,
        output_bias,
        second_gain,
        second_shift,
        inner_weight,
        inner_bias,
        outer_weight,
        outer_bias,
    ) = args
    length, width = frames.shape
    ranks = width // first_gain.shape[0]
    part = width // ranks
    inner_part = inner_bias.shape[0]
    hidden = inner_part * ranks
    groups = -(-length // GROUP)
    padded = groups * GROUP
    extended = (groups - 1) * GROUP + SPAN
    quad = 64 * QUAD
    vectors = [
        first_gain,
        first_shift,
        query_bias,
        value_bias,
        output_bias,
        second_gain,
        second_shift,
        outer_bias,
    ]
    first = [query_weight, key_weight, value_weight, memory_weight]
    second = [output_weight.T, inner_weight, outer_weight.T]
    dma = pltpu.SemaphoreType.DMA
    row, wide_row = shape((length, width), bf16), shape((length, hidden), bf16)
    row_wide, vec_shape = shape((length, width), f32), shape((16, width), f32)
    turned = shape((width, length), bf16)

    def scratch_of(*shapes):
        return [pltpu.VMEM(v.shape, v.dtype) for v in shapes]

    if ring:
        common, third = shares(width, hidden)
        total = common + 2 * third
        weights, main = call(
            pack_first_kernel,
            (shape((part, total), bf16), shape((part, common + third), bf16)),
            [VMEM] * 2,
            [
                *([pltpu.VMEM((1, part), bf16)] * 8),
                pltpu.VMEM((1, inner_part), bf16),
                pltpu.SemaphoreType.DMA((16,)),
            ],
            [
                *first,
                *second,
                *(v.reshape(1, part) for v in vectors),
                inner_bias.reshape(1, inner_part),
            ],
            [HBM] * 16,
            1,
            limit=8,
        )
        vec = jnp.zeros((16, width), f32)
    else:
        weights = query_weight
        vec = jnp.concatenate(
            [
                jnp.stack([lax.all_gather(v, "fsdp", axis=0, tiled=True) for v in vectors]),
                lax.all_gather(inner_bias, "fsdp", axis=0, tiled=True).reshape(-1, width),
                jnp.zeros((4, width), bf16),
            ],
            axis=0,
        ).astype(f32)
    normal, bias_grad, nt, gt = gated(
        functools.partial(prepare_kernel, length),
        (row_wide, vec_shape, turned, turned),
        [VMEM, VMEM, HBM, HBM],
        [*scratch_of(turned, turned), dma((2,))],
        [frames, out_grad],
        [VMEM] * 2,
        3,
        [weights],
    )
    if ring:
        got = ring_gather(weights, main, common, [bias_grad])
        others = [v for v in got if v[2] in ("pair", "own")]
        items = both_cores([v for v in got if v[2] in ("all", "main", "common")])
        weights = whole_weights(
            items, ("all", "main", "common"), (width, common), common, [v[0] for v in others]
        )
    else:
        weights, second = (
            lax.all_gather(jnp.concatenate(v, axis=1), "fsdp", axis=0, tiled=True)
            for v in (first, second)
        )

    attended_shapes = (
        shape((padded, width), bf16),
        shape((extended, width), bf16),
        shape((extended, width), bf16),
        shape((16, 2 * width), bf16),
        shape((HEADS // QUAD, groups, KEYS, GROUP * QUAD), bf16),
    )
    *attended, ctx, vec, cols = call(
        functools.partial(attention_forward_kernel, ring, length),
        (
            *attended_shapes,
            shape((padded, width), bf16),
            vec_shape,
            shape((width, 16), f32),
        ),
        [VMEM] * 8,
        [pltpu.VMEM((2, KEYS, GROUP * QUAD), f32)],
        [normal, memory_bank, cache_keys, cache_values, vec, weights],
        [VMEM] * 6,
        6,
    )

    def grad_shapes(w):
        if ring:
            dims = [(7, 32, w), (2, 32, w // 2)]
            return tuple(shape(v, bf16) for v in dims + dims)
        return (shape((width, w), bf16),)

    grad_specs = [VMEM] * (4 if ring else 1)
    token_shape = shape((8, 128), f32)
    if ring:
        items += both_cores(others + got[-1:], [vec])
        second = whole_weights(
            items, ("all", "main", "pair", "own", "other"), (width, 2 * third), 0
        )
    residual, normed2, active, slope, *attended = call(
        functools.partial(inner_kernel, length),
        (row_wide, row, wide_row, wide_row),
        [VMEM] * 4,
        [],
        [frames, ctx, vec, second],
        [VMEM] * 4,
        5,
        carried=attended,
    )

    gi, vec_grads, active, residual, *attended = call(
        functools.partial(grad_inner_kernel, length),
        (wide_row, vec_shape),
        [VMEM] * 2,
        [],
        [out_grad, slope, bias_grad, second],
        [VMEM] * 4,
        2,
        carried=[active, residual, *attended],
    )
    results = call(
        functools.partial(hidden_weight_kernel, ring, length),
        grad_shapes(2 * hidden),
        grad_specs,
        [
            *scratch_of(turned, turned),
            pltpu.VMEM((width, 2 * hidden), bf16),
            dma((1,)),
        ],
        [normed2, gi, active, gt],
        [VMEM] * 3 + [HBM],
        5,
        carried=[residual, *attended],
    )
    both_grads, (residual, *attended) = results[:-6], results[-6:]
    both = Reduction(*both_grads).follow() if ring else None

    def steps(after, *reductions):
        made = []
        if ring:
            for reduction in reductions:
                made += reduction.advance([after])
        return made

    grad_att, grad_ctx, vec_grads, nt, grad_res, active, *attended = gated(
        functools.partial(grad_residual_kernel, length),
        (row, shape((padded, width), bf16), vec_shape, turned, row_wide),
        [VMEM] * 5,
        [dma((1,))],
        [gi, residual, out_grad, vec, vec_grads, second, nt],
        [VMEM] * 6 + [HBM],
        4,
        both_grads[:1],
        carried=[active, *attended],
    )
    made = steps(vec_grads, both)
    part_row = shape((length, quad), bf16)
    left_row = shape((LEAD, quad), f32)
    quad_shapes = (
        shape((padded, quad), bf16),
        part_row,
        part_row,
        left_row,
        left_row,
        shape((16, 2 * quad), bf16),
    )
    quad_scratch = [
        pltpu.VMEM((extended, quad), f32),
        pltpu.VMEM((extended, quad), f32),
        pltpu.VMEM((16, 2 * quad), f32),
    ]
    def quad_attention(j, made, carried):
        return gated(
            functools.partial(quad_kernel, j, length),
            quad_shapes,
            [VMEM] * 6,
            quad_scratch,
            [grad_ctx, *attended],
            [VMEM] * 6,
            4,
            made,
            carried=carried,
        )

    def quad_weights(j, grads, vec_grads, extra, w, made, carried):
        return gated(
            functools.partial(quad_weight_kernel, j, ring, length),
            (vec_shape, *grad_shapes(w)),
            [VMEM] + grad_specs,
            [pltpu.VMEM((width, w), bf16), *(scratch_of(turned) if extra else [])],
            [memory_bank, cols, vec_grads, nt, weights, *grads[:3], grads[5], *extra],
            [VMEM] * (9 + len(extra)),
            3,
            made,
            carried=carried,
        )

    results = quad_attention(0, made, [active, residual, grad_res])
    quad_one, carried = results[:6], results[6:]
    made = steps(quad_one[5], both)
    results = quad_weights(
        0, quad_one, vec_grads, [grad_att, ctx], width + 5 * quad, made, [*carried, *attended]
    )
    vec_grads, one_grads = results[0], results[1:-8]
    carried, attended = results[-8:-5], results[-5:]
    results = quad_attention(1, [vec_grads], carried)
    quad_two, carried = results[:6], results[6:]
    two_width = 5 * quad + (256 if ring else 0)
    results = quad_weights(1, quad_two, vec_grads, [], two_width, [], carried)
    vec_grads, two_grads = results[0], results[1:-3]
    active, residual, grad_res = results[-3:]
    made = [vec_grads]
    if ring:
        one = Reduction(*one_grads, after=made).follow(made)
        two = Reduction(*two_grads)
        made = both.advance(made) + one.advance(made)
        two.follow(made[:1])
        made = two.advance(made[-1:])
    output, token, grad_res = gated(
        functools.partial(output_kernel, length),
        (row, token_shape),
        [VMEM] * 2,
        [],
        [active, residual, vec, second],
        [VMEM] * 4,
        3,
        made,
        carried=[grad_res],
    )
    if ring:
        made = one.advance([token]) + two.advance([token])
        both.advance([fence(made)])
        made = one.advance() + two.advance()
        made = both.advance([fence(made)])
        inner_sum, outer_sum, token = call(
            upper_result_kernel,
            (shape((part, hidden), f32), shape((part, hidden), f32), token_shape),
            [VMEM] * 3,
            [],
            [both.total, both.far],
            [VMEM] * 2,
            1,
            limit=8,
        )
        made = one.advance(made) + two.advance(made)
        token = fence(made)
        made = one.advance([token]) + two.advance([token])
        grad_frames, grad_bank, grad_ck, grad_cv, token = gated(
            functools.partial(lower_kernel, length),
            (
                row_wide,
                shape((1, MEM, width), f32),
                shape((LEFT, 1, width), f32),
                shape((LEFT, 1, width), f32),
                token_shape,
            ),
            [VMEM] * 5,
            [],
            [frames, grad_res, vec, weights, *quad_one, *quad_two],
            [VMEM] * 16,
            5,
            made,
        )
        square = shape((part, width), f32)
        q_sum, k_sum, v_sum, m_sum, output_sum, *own = call(
            lower_result_kernel,
            (
                square,
                square,
                square,
                shape((part, 2 * width), f32),
                square,
                *([shape((1, part), f32)] * 8),
                shape((1, inner_part), f32),
            ),
            [VMEM] * 14,
            [],
            [one.total, one.far, two.total, two.far, token],
            [VMEM] * 4 + [ANY],
            1,
            limit=8,
        )
        own_inner = own[8].reshape(inner_part)
        own = [v.reshape(part) for v in own[:8]]
    else:
        grad_frames, grad_bank, grad_ck, grad_cv, token = gated(
            functools.partial(lower_kernel, length),
            (
                row_wide,
                shape((1, MEM, width), f32),
                shape((LEFT, 1, width), f32),
                shape((LEFT, 1, width), f32),
                token_shape,
            ),
            [VMEM] * 5,
            [],
            [frames, grad_res, vec, weights, *quad_one, *quad_two],
            [VMEM] * 16,
            5,
            made,
        )

        def reduce(v):
            total = lax.psum_scatter(v, "fsdp", scatter_dimension=0, tiled=True)
            return lax.psum(total, "rep").astype(f32)

        total = reduce(both_grads[0])
        inner_sum, outer_sum = total[:, :hidden], total[:, hidden:]
        low, high = reduce(one_grads[0]), reduce(two_grads[0])
        output_sum = low[:, :width]
        sums = [v.reshape(part, 5, quad) for v in (low[:, width:], high)]
        q_sum, k_sum, v_sum, m_low, m_high = (
            jnp.concatenate([v[:, i] for v in sums], axis=1) for i in range(5)
        )
        m_sum = jnp.concatenate([m_low, m_high], axis=1)
        vec_sum = lax.psum(vec_grads, ("rep", "fsdp"))
        rank = lax.axis_index("fsdp")
        own = lax.dynamic_slice(vec_sum[:8], (0, rank * part), (8, part))
        own_inner = lax.dynamic_slice(
            vec_sum[8:12].reshape(-1), (rank * inner_part,), (inner_part,)
        )
    return (
        output,
        grad_frames,
        grad_bank,
        jnp.swapaxes(grad_ck, 0, 1),
        jnp.swapaxes(grad_cv, 0, 1),
        own[0],
        own[1],
        q_sum,
        own[2],
        k_sum,
        v_sum,
        own[3],
        m_sum,
        output_sum.T,
        own[4],
        own[5],
        own[6],
        inner_sum,
        own_inner,
        outer_sum.T,
        own[7],
    )


def without_gates(kernel, n_args, n_gates, *refs):
    kernel(*refs[:n_args], *refs[n_args + n_gates :])


def gated(kernel, out_shapes, out_specs, scratch, args, specs, micros, made, carried=()):
    return call(
        functools.partial(without_gates, kernel, len(args), len(made)),
        out_shapes,
        out_specs,
        scratch,
        [*args, *made],
        [*specs, *[ANY] * len(made)],
        micros,
        carried=carried,
    )


def solution(mesh):
    both = ("rep", "fsdp")
    rows, vector = P("fsdp", None), P("fsdp")
    columns = P(None, "fsdp")
    weights = (
        vector,
        vector,
        rows,
        vector,
        rows,
        rows,
        vector,
        rows,
        columns,
        vector,
        vector,
        vector,
        rows,
        vector,
        columns,
        vector,
    )
    blocks = P(both, None, None)
    in_specs = (P(both, None), blocks, blocks, blocks, P(both, None), *weights)
    out_specs = (P(both, None), P(both, None), blocks, blocks, blocks, *weights)
    ring = mesh.shape["fsdp"] == 16 and mesh.shape["rep"] == 2
    return jax.shard_map(
        functools.partial(per_device, ring),
        mesh=mesh,
        in_specs=in_specs,
        out_specs=out_specs,
        check_vma=False,
    )
```

```python
import functools

import jax
import jax.numpy as jnp
from jax import lax
from jax.experimental import pallas as pl
from jax.experimental.pallas import tpu as pltpu
from jax.sharding import PartitionSpec as P

HEADS = 8
SEG = 16
RIGHT = 4
LEFT = 30
MEM = 4

LEAD = 32
GROUP = 64
SPAN = 112
KEYS = 128
QUAD = 4
masked_value = -1e30
epsilon = 1e-05
gelu_a = 0.7978845608028654
gelu_b = gelu_a * 0.044715

bf16 = jnp.bfloat16
f32 = jnp.float32
VMEM = pl.BlockSpec(memory_space=pltpu.VMEM)
ANY = pl.BlockSpec(memory_space=pl.ANY)
HBM = pl.BlockSpec(memory_space=pltpu.HBM)


def dot(a, b):
    return lax.dot_general(a, b, (((1,), (0,)), ((), ())), preferred_element_type=f32)


def dot_nt(a, b):
    return lax.dot_general(a, b, (((1,), (1,)), ((), ())), preferred_element_type=f32)


def dot_tn(a, b):
    return lax.dot_general(a, b, (((0,), (0,)), ((), ())), preferred_element_type=f32)


def row_tiles(rows):
    return [(start, min(256, rows - start)) for start in range(0, rows, 256)]


def centred(v):
    center = v - jnp.mean(v, axis=-1, keepdims=True)
    spread = jnp.mean(center * center, axis=-1, keepdims=True)
    scale = lax.rsqrt(spread + epsilon)
    return center * scale, scale


def norm_back(e, n, scale, gain):
    eg = e * gain
    return scale * (
        eg - jnp.mean(eg, axis=-1, keepdims=True) - n * jnp.mean(eg * n, axis=-1, keepdims=True)
    )


def colsum(v):
    return jnp.sum(v, axis=0, keepdims=True)


RING = (0, 2, 4, 6, 7, 5, 3, 1)


def ring_pairs(step):
    pairs = []
    for k in range(8):
        for core in range(2):
            pairs.append((2 * RING[k] + core, 2 * RING[(k + step) % 8] + core))
    return pairs


TO_RIGHT, TO_LEFT = ring_pairs(1), ring_pairs(-1)
TO_CORE = [(i, i ^ 1) for i in range(16)]


def two_way(cross):
    pairs = []
    for k in range(8):
        pairs.append((2 * RING[k], 2 * RING[(k + 1) % 8] + cross))
        pairs.append((2 * RING[k] + 1, 2 * RING[(k - 1) % 8] + 1 - cross))
    return pairs


ALONG, ACROSS = two_way(0), two_way(1)


def ring_ids():
    rank = lax.axis_index("fsdp")
    core, chip = lax.rem(rank, 2), lax.div(rank, 2)
    z, x = lax.div(chip, 2), lax.rem(chip, 2)
    return jnp.where(x == 0, z, 7 - z), core


def ring_rank(position, core):
    position = lax.rem(position, 8)
    return 2 * jnp.where(position < 4, 2 * position, 15 - 2 * position) + core


def halves(width):
    return width // 2 // 128 * 128


def send(v, pairs):
    return lax.ppermute(v, "fsdp", pairs)


def across(v):
    return lax.ppermute(v, "rep", [(0, 1), (1, 0)])


def shares(width, hidden):
    return 5 * width + 256, (width + 2 * hidden) // 2


def ring_gather(shard, main, common, after):
    third = main.shape[1] - common
    got = [(shard, 0, "all")]
    a = b = main
    for step in (1, 2, 3):
        a, b = send(a, TO_RIGHT), send(b, TO_LEFT)
        pair = call(
            tails_kernel,
            shape((shard.shape[0], 2 * third), bf16),
            VMEM,
            [],
            [a, b],
            [VMEM] * 2,
            0.3,
            limit=4,
        )
        pair = across(pair)
        if step == 1:
            pair = hold(pair, after)
        got += [(a, 8 - step, "main"), (b, step, "main"), (pair, step, "pair")]
    a, b = send(a[:, :common], TO_RIGHT), send(b[:, common:], TO_LEFT)
    return got + [(a, 4, "common"), (b, 4, "own"), (across(b), 4, "other")]


def both_cores(items, after=()):
    items = [(hold(v, after) if after else v, d, k) for v, d, k in items]
    return [(v, d, 0, k) for v, d, k in items] + [(send(v, TO_CORE), d, 1, k) for v, d, k in items]


def tails_kernel(a, b, *refs):
    out = refs[-1]
    third = out.shape[1] // 2
    out[:, :third] = a[:, a.shape[1] - third :]
    out[:, third:] = b[:, b.shape[1] - third :]


def lay_rows(places, common, *refs):
    refs, whole = refs[: len(places)], refs[-1]
    position, core = ring_ids()
    replica = lax.axis_index("rep")
    third = whole.shape[1] // 2
    own = pl.ds(pl.multiple_of(replica * third, 128), third)
    other = pl.ds(pl.multiple_of((1 - replica) * third, 128), third)

    def rows(distance, flip):
        owner = ring_rank(position + distance, core if flip == 0 else 1 - core)
        return pl.ds(pl.multiple_of(owner * 32, 32), 32)

    for ref, (distance, flip, kind) in zip(refs, places):
        at = rows(distance, flip)
        if common:
            whole[at, :] = ref[:, :common]
        elif kind == "all":
            whole[at, :] = ref[:, ref.shape[1] - 2 * third :]
        elif kind == "main":
            whole[at, own] = ref[:, ref.shape[1] - third :]
        elif kind == "pair":
            whole[rows(8 - distance, flip), other] = ref[:, :third]
            whole[at, other] = ref[:, third:]
        else:
            whole[at, own if kind == "own" else other] = ref[...]


def whole_weights(items, kinds, dims, common, after=()):
    items = [v for v in items if v[3] in kinds]
    return call(
        functools.partial(lay_rows, tuple(v[1:] for v in items), common),
        shape(dims, bf16),
        VMEM,
        [],
        [*(v[0] for v in items), *after],
        [VMEM] * len(items) + [ANY] * len(after),
        0.5,
        limit=24,
    )


def spread(ring, grads, outs):
    if not ring:
        outs[0][...] = grads[...]
        return
    position, core = ring_ids()
    mine, mine_far, other, other_far = outs
    half = mine_far.shape[2]
    way = 1 - 2 * core

    def rows(place, k):
        return pl.ds(pl.multiple_of(ring_rank(place, k) * 32, 32), 32)

    def lanes(k):
        return pl.ds(pl.multiple_of(k * half, 128), half)

    for k in range(2):
        for distance in (3, 2, 1):
            at = 2 * (3 - distance) + k
            mine[at] = grads[rows(position + 8 + way * distance, k), :]
            other[at] = grads[rows(position + 8 - way * distance, k), :]
        mine_far[k] = grads[rows(position + 4, k), lanes(core)]
        other_far[k] = grads[rows(position + 4, k), lanes(1 - core)]
    mine[6] = grads[rows(position, core), :]
    other[6] = grads[rows(position, 1 - core), :]


def start_all(pairs, sems, first=0):
    copies = [pltpu.make_async_copy(a, b, sems.at[first + i]) for i, (a, b) in enumerate(pairs)]
    for copy in copies:
        copy.start()
    return copies


def wait_all(copies):
    for copy in copies:
        copy.wait()


def columns(width, hidden):
    return width, width + hidden, width + 2 * hidden


def head_masks():
    lane = lax.broadcasted_iota(jnp.int32, (1, 64 * QUAD), 1)
    return [(lane // 64 == h).astype(f32) for h in range(QUAD)]


def stacked(rows, masks):
    return jnp.concatenate([rows * m for m in masks], axis=0)


def unstacked(wide, masks):
    parts = [wide[GROUP * h : GROUP * (h + 1)] * masks[h] for h in range(QUAD)]
    return parts[0] + parts[1] + parts[2] + parts[3]


def added_mask(limit):
    row = lax.broadcasted_iota(jnp.int32, (KEYS, GROUP * QUAD), 0)
    query = lax.rem(lax.broadcasted_iota(jnp.int32, (KEYS, GROUP * QUAD), 1), GROUP)
    first = query // SEG * SEG + (LEAD - LEFT)
    inside = (row >= first) & (row < first + LEFT + SEG + RIGHT) & (row < limit)
    bank = (row >= SPAN) & (row < SPAN + MEM)
    return jnp.where((inside & (row < SPAN)) | bank, 0.0, masked_value)


def prepare_kernel(length, frames, out_grad, n_out, bias_out, nt_out, gt_out, nt, gt, sems):
    for start, size in row_tiles(length):
        rows = slice(start, start + size)
        n, _ = centred(frames[rows].astype(f32))
        n_out[rows] = n
        nt[:, rows] = n.astype(bf16).T
        gt[:, rows] = out_grad[rows].T
    copies = start_all([(nt, nt_out), (gt, gt_out)], sems)
    bias_out[...] = jnp.zeros(bias_out.shape, f32)
    bias_out[7:8] = colsum(out_grad[...].astype(f32))
    wait_all(copies)


def attention_forward_kernel(ring, length, *refs):
    normal, bank, cache_k, cache_v, vec, w = refs[:6]
    q, kext, vext, kvmem, pt, ctx, vec_out, cols_out, mask = refs[6:]
    width = normal.shape[1]
    groups = q.shape[0] // GROUP
    if not ring:
        vectors = vec[...]
    else:
        blocks = w[:, 5 * width :].astype(f32).reshape(16, 32, 256)
        total = jnp.sum(blocks, axis=0)
        vectors = jnp.concatenate([total[:16], total[16:]], axis=1)
    vec_out[...] = vectors
    cols_out[...] = vectors.T

    def left_rows(cache):
        rows = cache[0].astype(f32)
        return jnp.concatenate([jnp.zeros((LEAD - LEFT, width), f32), rows], axis=0).astype(bf16)

    kext[0:LEAD] = left_rows(cache_k)
    vext[0:LEAD] = left_rows(cache_v)
    tail = kext.shape[0] - LEAD - length
    kext[LEAD + length :] = jnp.zeros((tail, width), bf16)
    vext[LEAD + length :] = jnp.zeros((tail, width), bf16)
    q[length:] = jnp.zeros((q.shape[0] - length, width), bf16)
    bank_rows = jnp.concatenate(
        [bank[0].astype(f32), jnp.zeros((16 - MEM, width), f32)], axis=0
    ).astype(bf16)
    kvmem[...] = dot(bank_rows, w[:, 3 * width : 5 * width]).astype(bf16)

    for start, size in row_tiles(length):
        rows = (normal[start : start + size] * vectors[0:1] + vectors[1:2]).astype(bf16)
        q[start : start + size] = (dot(rows, w[:, :width]) + vectors[2:3]).astype(bf16)
        kext[LEAD + start : LEAD + start + size] = dot(rows, w[:, width : 2 * width]).astype(bf16)
        vext[LEAD + start : LEAD + start + size] = (
            dot(rows, w[:, 2 * width : 3 * width]) + vectors[3:4]
        ).astype(bf16)

    masks = head_masks()
    scale = 64**-0.5
    q_masks = [(m * scale).astype(bf16) for m in masks]
    mask[0] = added_mask(KEYS)
    mask[1] = added_mask(LEAD + length - GROUP * (groups - 1))

    def step(g, carry):
        top = pl.multiple_of(g * GROUP, GROUP)
        hidden = mask[(g == groups - 1).astype(jnp.int32)]
        for j in range(HEADS // QUAD):
            lanes = slice(64 * QUAD * j, 64 * QUAD * (j + 1))
            keys = jnp.concatenate([kext[pl.ds(top, SPAN), lanes], kvmem[:, lanes]], axis=0)
            values = jnp.concatenate(
                [vext[pl.ds(top, SPAN), lanes], kvmem[:, width + lanes.start : width + lanes.stop]],
                axis=0,
            )
            queries = stacked(q[pl.ds(top, GROUP), lanes], q_masks)
            scores = dot_nt(keys, queries) + hidden
            raised = jnp.exp(scores - jnp.max(scores, axis=0, keepdims=True))
            weights = (raised / jnp.sum(raised, axis=0, keepdims=True)).astype(bf16)
            pt[j, g] = weights
            ctx[pl.ds(top, GROUP), lanes] = unstacked(dot_tn(weights, values), masks).astype(bf16)
        return carry

    lax.fori_loop(0, groups, step, 0, unroll=6)


def inner_kernel(length, *refs):
    frames, ctx, vec, w, residual, normed2, active, slope = refs
    width = frames.shape[1]
    hidden = active.shape[1]
    second, _, _ = columns(width, hidden)
    for start, size in row_tiles(length):
        rows = slice(start, start + size)
        res = frames[rows].astype(f32) + dot_nt(ctx[rows], w[:, :second]) + vec[4:5]
        residual[rows] = res
        n, _ = centred(res)
        normed2[rows] = (n * vec[5:6] + vec[6:7]).astype(bf16)

    block = 512
    for b in range(hidden // block):
        cols = slice(b * block, (b + 1) * block)
        for start, size in row_tiles(length):
            rows = slice(start, start + size)
            u = dot(normed2[rows], w[:, second + cols.start : second + cols.stop]) + vec[8 + b : 9 + b]
            uu = u * u
            h = 0.5 + 0.5 * jnp.tanh(u * (gelu_a + gelu_b * uu))
            act = u * h
            active[rows, cols] = act.astype(bf16)
            slope[rows, cols] = (
                h + act * (1.0 - h) * (2 * gelu_a + 6 * gelu_b * uu)
            ).astype(bf16)


def grad_inner_kernel(length, out_grad, slope, vec_before, w, gi, vec_grads):
    width, hidden = out_grad.shape[1], slope.shape[1]
    third = columns(width, hidden)[1]
    block = 512
    vec_grads[...] = vec_before[...]
    for b in range(hidden // block):
        cols = slice(b * block, (b + 1) * block)
        sums = jnp.zeros((1, block), f32)
        for start, size in row_tiles(length):
            rows = slice(start, start + size)
            up = dot(out_grad[rows], w[:, third + cols.start : third + cols.stop])
            part = (up * slope[rows, cols].astype(f32)).astype(bf16)
            gi[rows, cols] = part
            sums += colsum(part.astype(f32))
        vec_grads[8 + b : 9 + b] = sums


def output_kernel(length, active, residual, vec, w, output, token):
    _, third, last = columns(residual.shape[1], active.shape[1])
    token[...] = jnp.zeros(token.shape, f32)
    for start, size in row_tiles(length):
        rows = slice(start, start + size)
        output[rows] = (residual[rows] + dot_nt(active[rows], w[:, third:last]) + vec[7:8]).astype(bf16)


def hidden_weight_kernel(ring, length, *refs):
    normed2, gi, active, gt_in = refs[:4]
    outs, (n2t, gt, grads, sems) = refs[4:-4], refs[-4:]
    hidden = gi.shape[1]
    copies = start_all([(gt_in, gt)], sems)
    for start, size in row_tiles(length):
        rows = slice(start, start + size)
        n2t[:, rows] = normed2[rows].T
    for at in range(0, hidden, 512):
        grads[:, at : at + 512] = dot(n2t[...], gi[:, at : at + 512]).astype(bf16)
    wait_all(copies)
    for at in range(0, hidden, 512):
        cols = slice(hidden + at, hidden + at + 512)
        grads[:, cols] = dot(gt[...], active[:, at : at + 512]).astype(bf16)
    spread(ring, grads, outs)


def grad_residual_kernel(length, *refs):
    gi, residual, out_grad, vec, vec_before, w, nt_in = refs[:7]
    grad_att, grad_ctx, vec_grads, nt, grad_res, sems = refs[7:]
    width = residual.shape[1]
    copies = start_all([(nt_in, nt)], sems)
    second, third, _ = columns(width, gi.shape[1])
    sums = [jnp.zeros((1, width), f32) for _ in range(3)]
    for start, size in row_tiles(length):
        rows = slice(start, start + size)
        e = dot_nt(gi[rows], w[:, second:third])
        n, scale = centred(residual[rows])
        gres = out_grad[rows].astype(f32) + norm_back(e, n, scale, vec[5:6])
        grad_res[rows] = gres
        gat_rows = gres.astype(bf16)
        grad_att[rows] = gat_rows
        grad_ctx[rows] = dot(gat_rows, w[:, :second]).astype(bf16)
        sums = [s + colsum(v) for s, v in zip(sums, (gat_rows.astype(f32), e * n, e))]
    grad_ctx[length:] = jnp.zeros((grad_ctx.shape[0] - length, width), bf16)
    vec_grads[...] = vec_before[...]
    for i in range(3):
        vec_grads[4 + i : 5 + i] = sums[i]
    wait_all(copies)


def attention_backward(j, attended, grad_ctx, gk, gv, gkm, gq):
    q, kext, vext, kvmem, pt = attended
    width = q.shape[1]
    groups = q.shape[0] // GROUP
    size = 64 * QUAD
    lanes = slice(size * j, size * (j + 1))
    value_lanes = slice(width + size * j, width + size * (j + 1))
    gk[...] = jnp.zeros(gk.shape, f32)
    gv[...] = jnp.zeros(gv.shape, f32)
    gkm[...] = jnp.zeros(gkm.shape, f32)
    masks = head_masks()
    scale = 64**-0.5
    q_masks = [(m * scale).astype(bf16) for m in masks]
    c_masks = [m.astype(bf16) for m in masks]
    out_masks = [m * scale for m in masks]

    def step(g, carry):
        top = pl.multiple_of(g * GROUP, GROUP)
        keys = jnp.concatenate([kext[pl.ds(top, SPAN), lanes], kvmem[:, lanes]], axis=0)
        values = jnp.concatenate([vext[pl.ds(top, SPAN), lanes], kvmem[:, value_lanes]], axis=0)
        queries = stacked(q[pl.ds(top, GROUP), lanes], q_masks)
        upstream = stacked(grad_ctx[pl.ds(top, GROUP), lanes], c_masks)
        weights = pt[j, g]
        wide = weights.astype(f32)
        gp = dot_nt(values, upstream)
        gs = (wide * (gp - colsum(gp * wide))).astype(bf16)
        gkeys = dot(gs, queries)
        gvalues = dot(weights, upstream)
        gk[pl.ds(top, SPAN)] += gkeys[:SPAN]
        gv[pl.ds(top, SPAN)] += gvalues[:SPAN]
        gkm[:, :size] += gkeys[SPAN:]
        gkm[:, size:] += gvalues[SPAN:]
        gq[pl.ds(top, GROUP)] = unstacked(dot_tn(gs, keys), out_masks).astype(bf16)
        return carry

    lax.fori_loop(0, groups, step, 0, unroll=6)


def bank_block(bank, width):
    return jnp.concatenate(
        [bank[0].astype(f32), jnp.zeros((16 - MEM, width), f32)], axis=0
    ).astype(bf16)


def pair_of(row):
    high = row.astype(bf16).astype(f32)
    zeros = jnp.zeros((14, row.shape[1]), f32)
    return jnp.concatenate([high, row - high, zeros], axis=0).astype(bf16)


def quad_kernel(j, length, *refs):
    grad_ctx, *attended = refs[:6]
    gq, gk_rows, gv_rows, gk_left, gv_left, gbank, gk, gv, gkm = refs[6:]
    attention_backward(j, attended, grad_ctx, gk, gv, gkm, gq)
    gk_left[...] = gk[0:LEAD]
    gv_left[...] = gv[0:LEAD]
    gk_rows[...] = gk[LEAD : LEAD + length].astype(bf16)
    gv_rows[...] = gv[LEAD : LEAD + length].astype(bf16)
    gbank[...] = gkm[...].astype(bf16)


def quad_weight_kernel(j, ring, length, *refs):
    bank, cols, vec_before, nt, w, gq, gk_rows, gv_rows, gbank = refs[:9]
    width = nt.shape[0]
    size = 64 * QUAD
    first = width * (1 - j)
    refs = refs[9:]
    if j == 0:
        grad_att, ctx = refs[:2]
        refs = refs[2:]
    n_out = 4 if ring else 1
    vec_grads, *outs = refs[: 1 + n_out]
    grads, *rest = refs[1 + n_out :]
    if j == 0:
        gat = rest[0]
        for start, count in row_tiles(length):
            rows = slice(start, start + count)
            gat[:, rows] = grad_att[rows].T
        grads[:, :width] = dot(gat[...], ctx[:length]).astype(bf16)
    gain, shift = cols[:, 0:1], cols[:, 1:2]
    gains, shifts = jnp.zeros((width, 1), f32), jnp.zeros((16, width), f32)
    sums = []
    for i, g in enumerate((gq[:length], gk_rows[...], gv_rows[...])):
        m = dot(nt[...], g)
        sums.append(colsum(g.astype(f32)))
        at = first + i * size
        grads[:, at : at + size] = (gain * m + shift * sums[i]).astype(bf16)
        own = slice(i * width + j * size, i * width + (j + 1) * size)
        gains += jnp.sum(w[:, own].astype(f32) * m, axis=1, keepdims=True)
        shifts += dot_nt(pair_of(sums[i]), w[:, own])
    at = first + 3 * size
    grads[:, at : at + 2 * size] = dot_tn(bank_block(bank, width), gbank[...]).astype(bf16)
    vec_grads[...] = vec_before[...]
    vec_grads[0:1] += jnp.transpose(jnp.broadcast_to(gains, (width, 128)))[0:1]
    vec_grads[1:2] += colsum(shifts)
    vec_grads[2:3, size * j : size * (j + 1)] = sums[0]
    vec_grads[3:4, size * j : size * (j + 1)] = sums[2]
    if j == 1 and ring:
        vectors = vec_grads[...]
        block = jnp.concatenate([vectors[:, :256], vectors[:, 256:]], axis=0).astype(bf16)
        grads[:, at + 2 * size :] = jnp.concatenate([block] * 16, axis=0)
    spread(ring, grads, outs)


def lower_kernel(length, *refs):
    frames, grad_res, vec, w = refs[:4]
    gq, gk, gv, gk_left, gv_left, gbank = ([refs[4 + i], refs[10 + i]] for i in range(6))
    grad_frames, grad_bank, grad_ck, grad_cv, token = refs[16:]
    token[...] = jnp.zeros(token.shape, f32)
    width = frames.shape[1]
    part = gq[0].shape[1]
    for out, parts in ((grad_ck, gk_left), (grad_cv, gv_left)):
        left = jnp.concatenate([v[...] for v in parts], axis=1)
        for row in range(LEFT):
            out[row] = left[LEAD - LEFT + row : LEAD - LEFT + row + 1]
    bank_grads = jnp.concatenate(
        [v[:, at : at + part] for at in (0, part) for v in gbank], axis=1
    )
    grad_bank[0] = dot_nt(bank_grads, w[:, 3 * width : 5 * width])[:MEM]
    for start, size in row_tiles(length):
        rows = slice(start, start + size)
        parts = [jnp.concatenate([v[rows] for v in pair], axis=1) for pair in (gq, gk, gv)]
        e = (
            dot_nt(parts[0], w[:, :width])
            + dot_nt(parts[1], w[:, width : 2 * width])
            + dot_nt(parts[2], w[:, 2 * width : 3 * width])
        )
        n, s = centred(frames[rows].astype(f32))
        grad_frames[rows] = grad_res[rows] + norm_back(e, n, s, vec[0:1])


def pack_first_kernel(*refs):
    weights, vectors, inner_bias, out, main = refs[:7], refs[7:15], refs[15], refs[16], refs[17]
    held, bias_held, sems = refs[18:26], refs[26], refs[27]
    width = weights[0].shape[1]
    column = 0
    copies = []
    for i, ref in enumerate(weights):
        if i == 4:
            column += 256
        copies.append((ref, out.at[:, pl.ds(column, ref.shape[1])]))
        column += ref.shape[1]
    copies += list(zip((*vectors, inner_bias), (*held, bias_held)))
    copies = [pltpu.make_async_copy(a, b, sems.at[i]) for i, (a, b) in enumerate(copies)]
    for copy in copies:
        copy.start()
    wait_all(copies)
    rank = lax.axis_index("fsdp")
    own = jnp.concatenate([ref[...].astype(f32) for ref in held], axis=0)
    part = own.shape[1]
    placed = jnp.where(
        lax.broadcasted_iota(jnp.int32, (8, width), 1) // part == rank,
        jnp.concatenate([own] * (width // part), axis=1),
        0.0,
    )
    bias = bias_held[...].astype(f32)
    count = bias.shape[1]
    row = lax.broadcasted_iota(jnp.int32, (4, width), 0)
    lane = lax.broadcasted_iota(jnp.int32, (4, width), 1)
    inner = jnp.where(
        (row * width + lane) // count == rank,
        jnp.concatenate([jnp.concatenate([bias] * (width // count), axis=1)] * 4, axis=0),
        0.0,
    )
    block = jnp.concatenate([placed, inner, jnp.zeros((4, width), f32)], axis=0)
    block = jnp.concatenate([block[:, : width // 2], block[:, width // 2 :]], axis=0)
    out[:, 5 * width : 5 * width + 256] = block.astype(bf16)
    common, third = 5 * width + 256, main.shape[1] - 5 * width - 256
    main[:, :common] = out[:, :common]
    main[:, common:] = jnp.where(
        lax.axis_index("rep") == 0,
        out[:, common : common + third].astype(f32),
        out[:, common + third :].astype(f32),
    ).astype(bf16)


def first_sum_kernel(mine, other, *refs):
    refs[-1][...] = (mine[...].astype(f32) + other[...].astype(f32)).astype(bf16)


def step_sum_kernel(far, mine_0, other_0, mine_1, other_1, come, *refs):
    out = refs[-1]
    _, core = ring_ids()
    half = come.shape[2]
    for k, (mine, other) in enumerate(((mine_0, other_0), (mine_1, other_1))):
        own = mine[0].astype(f32) + other[0].astype(f32)
        if far:
            here = core == 0
            come_k = come[k].astype(f32)
            out[k, :, :half] = (own[:, :half] + jnp.where(here, come_k, 0.0)).astype(bf16)
            out[k, :, half:] = (own[:, half:] + jnp.where(here, 0.0, come_k)).astype(bf16)
        else:
            out[k] = (own + come[k].astype(f32)).astype(bf16)


def near_sum_kernel(mine_0, other_0, mine_1, other_1, come, *refs):
    same, crossed = refs[-2:]
    _, core = ring_ids()
    first = mine_0[0].astype(f32) + other_0[0].astype(f32) + come[0].astype(f32)
    second = mine_1[0].astype(f32) + other_1[0].astype(f32) + come[1].astype(f32)
    same[...] = jnp.where(core == 0, first, second).astype(bf16)
    crossed[...] = jnp.where(core == 0, second, first).astype(bf16)


def last_sum_kernel(mine, other, a, b, *refs):
    refs[-1][...] = (
        mine[0].astype(f32) + other[0].astype(f32) + a[...].astype(f32) + b[...].astype(f32)
    ).astype(bf16)


def hold_kernel(*refs):
    pass


def hold(v, after):
    return pl.pallas_call(
        hold_kernel,
        out_shape=shape(v.shape, v.dtype),
        in_specs=[ANY] * (1 + len(after)),
        out_specs=ANY,
        input_output_aliases={0: 0},
        compiler_params=pltpu.CompilerParams(vmem_limit_bytes=2**20),
        cost_estimate=pl.CostEstimate(flops=0, bytes_accessed=0, transcendentals=0),
    )(v, *after)


def fence_kernel(*refs):
    refs[-1][...] = jnp.zeros(refs[-1].shape, f32)


def fence(arrays):
    return call(
        fence_kernel, shape((8, 128), f32), VMEM, [], arrays, [ANY] * len(arrays), 20, limit=2
    )


def chunk_spec(width, index):
    return pl.BlockSpec((1, 32, width), lambda i: (index, 0, 0))


class Reduction:
    def __init__(self, mine, mine_far, other, other_far, after=()):
        self.mine, self.mine_far = mine, mine_far
        other_far = hold(other_far, after) if after else other_far
        self.other, self.other_far = other, send(other_far, TO_CORE)
        self.width = mine.shape[2]
        self.distance = 4

    def follow(self, after=()):
        self.other = send(hold(self.other, after) if after else self.other, TO_CORE)
        return self

    def sums(self, kernel, shapes, places, partial, after):
        args, specs = [], []
        for place in places:
            args += [self.mine, self.other]
            specs += [chunk_spec(self.width, place)] * 2
        return call(
            kernel,
            shapes,
            [VMEM] * len(shapes),
            [],
            [*args, *partial, *after],
            [*specs, *[VMEM] * len(partial), *[ANY] * len(after)],
            0.5,
            limit=8,
            grid=(1,),
        )

    def advance(self, after=()):
        s = self.distance
        rows, pair = shape((32, self.width), bf16), shape((2, 32, self.width), bf16)
        places = [2 * (3 - s), 2 * (3 - s) + 1]
        self.distance -= 1
        if s == 0:
            made = self.sums(last_sum_kernel, [rows], [6], self.come, after)
            self.total = made[0]
            self.far = across(self.total)
        elif s == 4:
            made = self.sums(
                first_sum_kernel,
                [shape(self.mine_far.shape, bf16)],
                [],
                [self.mine_far, self.other_far],
                after,
            )
            self.come = [send(made[0], ALONG)]
        elif s > 1:
            kernel = functools.partial(step_sum_kernel, s == 3)
            made = self.sums(kernel, [pair], places, self.come, after)
            self.come = [send(made[0], ALONG)]
        else:
            made = self.sums(near_sum_kernel, [rows, rows], places, self.come, after)
            self.come = [send(made[0], ALONG), send(made[1], ACROSS)]
        return made

    def finish(self):
        while self.distance >= 0:
            self.advance()
        return self


def upper_result_kernel(both, both_far, inner_out, outer_out, token):
    token[...] = jnp.zeros(token.shape, f32)
    total = both[...].astype(f32) + both_far[...].astype(f32)
    hidden = inner_out.shape[1]
    inner_out[...] = total[:, :hidden]
    outer_out[...] = total[:, hidden:]


def lower_result_kernel(one, one_far, two, two_far, _, *refs):
    q_out, k_out, v_out, m_out, output_out = refs[:5]
    vector_outs, inner_out = refs[5:13], refs[13]
    width = output_out.shape[1]
    part = 64 * QUAD
    total = one[...].astype(f32) + one_far[...].astype(f32)
    output_out[...] = total[:, :width]
    pair = [total[:, width:], two[...].astype(f32) + two_far[...].astype(f32)]
    for i, out in enumerate((q_out, k_out, v_out)):
        for j in range(2):
            out[:, j * part : (j + 1) * part] = pair[j][:, i * part : (i + 1) * part]
    for i in range(2):
        for j in range(2):
            at = (2 * i + j) * part
            m_out[:, at : at + part] = pair[j][:, (3 + i) * part : (4 + i) * part]
    block = pair[1][:, 5 * part :]
    vectors = jnp.concatenate([block[:16], block[16:]], axis=1)
    rank = lax.axis_index("fsdp")
    quarter = lax.rem(rank, 4)

    def pick(v, index, size):
        found = jnp.zeros((v.shape[0], size), f32)
        for k in range(v.shape[1] // size):
            found += jnp.where(index == k, v[:, k * size : (k + 1) * size], 0.0)
        return found

    own = pick(pick(vectors[:8], lax.div(rank, 4), 128), quarter, 32)
    for i, out in enumerate(vector_outs):
        out[...] = own[i : i + 1]
    inner = pick(vectors[8:12], quarter, 128)
    found = jnp.zeros((1, 128), f32)
    for k in range(4):
        found += jnp.where(lax.div(rank, 4) == k, inner[k : k + 1], 0.0)
    inner_out[...] = found


def without_carried(kernel, n_in, n_carried, n_out, *refs):
    outs = refs[n_in + n_carried : n_in + n_carried + n_out]
    kernel(*refs[:n_in], *outs, *refs[n_in + n_out + 2 * n_carried :])


def call(
    kernel, out_shapes, out_specs, scratch, args, specs, micros, limit=20, grid=(), carried=()
):
    specs = list(specs)
    args = [
        pltpu.with_memory_space_constraint(v, pltpu.HBM) if spec is HBM else v
        for v, spec in zip(args, specs)
    ]
    single = not isinstance(out_specs, (list, tuple))
    shapes = [out_shapes] if single else list(out_shapes)
    spaces = [out_specs] if single else list(out_specs)
    shapes = [
        pltpu.HBM(v.shape, v.dtype) if spec is HBM else v for v, spec in zip(shapes, spaces)
    ]
    aliases = {}
    if carried:
        kernel = functools.partial(without_carried, kernel, len(args), len(carried), len(shapes))
        aliases = {len(args) + i: len(shapes) + i for i in range(len(carried))}
        args, specs = [*args, *carried], [*specs, *[ANY] * len(carried)]
        shapes += [shape(v.shape, v.dtype) for v in carried]
        spaces += [ANY] * len(carried)
        single = False
    return pl.pallas_call(
        kernel,
        grid=grid,
        out_shape=shapes[0] if single else tuple(shapes),
        in_specs=specs,
        out_specs=spaces[0] if single else tuple(spaces),
        input_output_aliases=aliases,
        scratch_shapes=scratch,
        compiler_params=pltpu.CompilerParams(vmem_limit_bytes=limit * 1024 * 1024),
        cost_estimate=pl.CostEstimate(
            flops=int(micros * 1e6), bytes_accessed=int(micros * 1e3), transcendentals=0
        ),
    )(*args)


def shape(dims, dtype):
    return jax.ShapeDtypeStruct(dims, dtype)


def per_device(ring, *args):
    (
        frames,
        memory_bank,
        cache_keys,
        cache_values,
        out_grad,
        first_gain,
        first_shift,
        query_weight,
        query_bias,
        key_weight,
        value_weight,
        value_bias,
        memory_weight,
        output_weight,
        output_bias,
        second_gain,
        second_shift,
        inner_weight,
        inner_bias,
        outer_weight,
        outer_bias,
    ) = args
    length, width = frames.shape
    ranks = width // first_gain.shape[0]
    part = width // ranks
    inner_part = inner_bias.shape[0]
    hidden = inner_part * ranks
    groups = -(-length // GROUP)
    padded = groups * GROUP
    extended = (groups - 1) * GROUP + SPAN
    quad = 64 * QUAD
    vectors = [
        first_gain,
        first_shift,
        query_bias,
        value_bias,
        output_bias,
        second_gain,
        second_shift,
        outer_bias,
    ]
    first = [query_weight, key_weight, value_weight, memory_weight]
    second = [output_weight.T, inner_weight, outer_weight.T]
    dma = pltpu.SemaphoreType.DMA
    row, wide_row = shape((length, width), bf16), shape((length, hidden), bf16)
    row_wide, vec_shape = shape((length, width), f32), shape((16, width), f32)
    turned = shape((width, length), bf16)

    def scratch_of(*shapes):
        return [pltpu.VMEM(v.shape, v.dtype) for v in shapes]

    if ring:
        common, third = shares(width, hidden)
        total = common + 2 * third
        weights, main = call(
            pack_first_kernel,
            (shape((part, total), bf16), shape((part, common + third), bf16)),
            [VMEM] * 2,
            [
                *([pltpu.VMEM((1, part), bf16)] * 8),
                pltpu.VMEM((1, inner_part), bf16),
                pltpu.SemaphoreType.DMA((16,)),
            ],
            [
                *first,
                *second,
                *(v.reshape(1, part) for v in vectors),
                inner_bias.reshape(1, inner_part),
            ],
            [HBM] * 16,
            1,
            limit=8,
        )
        vec = jnp.zeros((16, width), f32)
    else:
        weights = query_weight
        vec = jnp.concatenate(
            [
                jnp.stack([lax.all_gather(v, "fsdp", axis=0, tiled=True) for v in vectors]),
                lax.all_gather(inner_bias, "fsdp", axis=0, tiled=True).reshape(-1, width),
                jnp.zeros((4, width), bf16),
            ],
            axis=0,
        ).astype(f32)
    normal, bias_grad, nt, gt = gated(
        functools.partial(prepare_kernel, length),
        (row_wide, vec_shape, turned, turned),
        [VMEM, VMEM, HBM, HBM],
        [*scratch_of(turned, turned), dma((2,))],
        [frames, out_grad],
        [VMEM] * 2,
        3,
        [weights],
    )
    if ring:
        got = ring_gather(weights, main, common, [bias_grad])
        others = [v for v in got if v[2] in ("pair", "own")]
        items = both_cores([v for v in got if v[2] in ("all", "main", "common")])
        weights = whole_weights(
            items, ("all", "main", "common"), (width, common), common, [v[0] for v in others]
        )
    else:
        weights, second = (
            lax.all_gather(jnp.concatenate(v, axis=1), "fsdp", axis=0, tiled=True)
            for v in (first, second)
        )

    attended_shapes = (
        shape((padded, width), bf16),
        shape((extended, width), bf16),
        shape((extended, width), bf16),
        shape((16, 2 * width), bf16),
        shape((HEADS // QUAD, groups, KEYS, GROUP * QUAD), bf16),
    )
    *attended, ctx, vec, cols = call(
        functools.partial(attention_forward_kernel, ring, length),
        (
            *attended_shapes,
            shape((padded, width), bf16),
            vec_shape,
            shape((width, 16), f32),
        ),
        [VMEM] * 8,
        [pltpu.VMEM((2, KEYS, GROUP * QUAD), f32)],
        [normal, memory_bank, cache_keys, cache_values, vec, weights],
        [VMEM] * 6,
        6,
    )

    def grad_shapes(w):
        if ring:
            dims = [(7, 32, w), (2, 32, w // 2)]
            return tuple(shape(v, bf16) for v in dims + dims)
        return (shape((width, w), bf16),)

    grad_specs = [VMEM] * (4 if ring else 1)
    token_shape = shape((8, 128), f32)
    if ring:
        items += both_cores(others + got[-1:], [vec])
        second = whole_weights(
            items, ("all", "main", "pair", "own", "other"), (width, 2 * third), 0
        )
    residual, normed2, active, slope, *attended = call(
        functools.partial(inner_kernel, length),
        (row_wide, row, wide_row, wide_row),
        [VMEM] * 4,
        [],
        [frames, ctx, vec, second],
        [VMEM] * 4,
        5,
        carried=attended,
    )

    gi, vec_grads, active, residual, *attended = call(
        functools.partial(grad_inner_kernel, length),
        (wide_row, vec_shape),
        [VMEM] * 2,
        [],
        [out_grad, slope, bias_grad, second],
        [VMEM] * 4,
        2,
        carried=[active, residual, *attended],
    )
    results = call(
        functools.partial(hidden_weight_kernel, ring, length),
        grad_shapes(2 * hidden),
        grad_specs,
        [
            *scratch_of(turned, turned),
            pltpu.VMEM((width, 2 * hidden), bf16),
            dma((1,)),
        ],
        [normed2, gi, active, gt],
        [VMEM] * 3 + [HBM],
        5,
        carried=[residual, *attended],
    )
    both_grads, (residual, *attended) = results[:-6], results[-6:]
    both = Reduction(*both_grads).follow() if ring else None

    def steps(after, *reductions):
        made = []
        if ring:
            for reduction in reductions:
                made += reduction.advance([after])
        return made

    grad_att, grad_ctx, vec_grads, nt, grad_res, active, *attended = gated(
        functools.partial(grad_residual_kernel, length),
        (row, shape((padded, width), bf16), vec_shape, turned, row_wide),
        [VMEM] * 5,
        [dma((1,))],
        [gi, residual, out_grad, vec, vec_grads, second, nt],
        [VMEM] * 6 + [HBM],
        4,
        both_grads[:1],
        carried=[active, *attended],
    )
    made = steps(vec_grads, both)
    part_row = shape((length, quad), bf16)
    left_row = shape((LEAD, quad), f32)
    quad_shapes = (
        shape((padded, quad), bf16),
        part_row,
        part_row,
        left_row,
        left_row,
        shape((16, 2 * quad), bf16),
    )
    quad_scratch = [
        pltpu.VMEM((extended, quad), f32),
        pltpu.VMEM((extended, quad), f32),
        pltpu.VMEM((16, 2 * quad), f32),
    ]
    def quad_attention(j, made, carried):
        return gated(
            functools.partial(quad_kernel, j, length),
            quad_shapes,
            [VMEM] * 6,
            quad_scratch,
            [grad_ctx, *attended],
            [VMEM] * 6,
            4,
            made,
            carried=carried,
        )

    def quad_weights(j, grads, vec_grads, extra, w, made, carried):
        return gated(
            functools.partial(quad_weight_kernel, j, ring, length),
            (vec_shape, *grad_shapes(w)),
            [VMEM] + grad_specs,
            [pltpu.VMEM((width, w), bf16), *(scratch_of(turned) if extra else [])],
            [memory_bank, cols, vec_grads, nt, weights, *grads[:3], grads[5], *extra],
            [VMEM] * (9 + len(extra)),
            3,
            made,
            carried=carried,
        )

    results = quad_attention(0, made, [active, residual, grad_res])
    quad_one, carried = results[:6], results[6:]
    made = steps(quad_one[5], both)
    results = quad_weights(
        0, quad_one, vec_grads, [grad_att, ctx], width + 5 * quad, made, [*carried, *attended]
    )
    vec_grads, one_grads = results[0], results[1:-8]
    carried, attended = results[-8:-5], results[-5:]
    results = quad_attention(1, [vec_grads], carried)
    quad_two, carried = results[:6], results[6:]
    two_width = 5 * quad + (256 if ring else 0)
    results = quad_weights(1, quad_two, vec_grads, [], two_width, [], carried)
    vec_grads, two_grads = results[0], results[1:-3]
    active, residual, grad_res = results[-3:]
    made = [vec_grads]
    if ring:
        one = Reduction(*one_grads, after=[quad_two[5]]).follow([quad_two[5]])
        two = Reduction(*two_grads)
        made = both.advance(made) + one.advance(made)
        two.follow(made[:1])
        made = two.advance(made[-1:])
    output, token, grad_res = gated(
        functools.partial(output_kernel, length),
        (row, token_shape),
        [VMEM] * 2,
        [],
        [active, residual, vec, second],
        [VMEM] * 4,
        3,
        made,
        carried=[grad_res],
    )
    if ring:
        made = one.advance([token]) + two.advance([token])
        both.advance([fence(made)])
        made = one.advance() + two.advance()
        made = both.advance([fence(made)])
        inner_sum, outer_sum, token = call(
            upper_result_kernel,
            (shape((part, hidden), f32), shape((part, hidden), f32), token_shape),
            [VMEM] * 3,
            [],
            [both.total, both.far],
            [VMEM] * 2,
            1,
            limit=8,
        )
        made = one.advance(made) + two.advance(made)
        token = fence(made)
        made = one.advance([token]) + two.advance([token])
        grad_frames, grad_bank, grad_ck, grad_cv, token = gated(
            functools.partial(lower_kernel, length),
            (
                row_wide,
                shape((1, MEM, width), f32),
                shape((LEFT, 1, width), f32),
                shape((LEFT, 1, width), f32),
                token_shape,
            ),
            [VMEM] * 5,
            [],
            [frames, grad_res, vec, weights, *quad_one, *quad_two],
            [VMEM] * 16,
            5,
            made,
        )
        square = shape((part, width), f32)
        q_sum, k_sum, v_sum, m_sum, output_sum, *own = call(
            lower_result_kernel,
            (
                square,
                square,
                square,
                shape((part, 2 * width), f32),
                square,
                *([shape((1, part), f32)] * 8),
                shape((1, inner_part), f32),
            ),
            [VMEM] * 14,
            [],
            [one.total, one.far, two.total, two.far, token],
            [VMEM] * 4 + [ANY],
            1,
            limit=8,
        )
        own_inner = own[8].reshape(inner_part)
        own = [v.reshape(part) for v in own[:8]]
    else:
        grad_frames, grad_bank, grad_ck, grad_cv, token = gated(
            functools.partial(lower_kernel, length),
            (
                row_wide,
                shape((1, MEM, width), f32),
                shape((LEFT, 1, width), f32),
                shape((LEFT, 1, width), f32),
                token_shape,
            ),
            [VMEM] * 5,
            [],
            [frames, grad_res, vec, weights, *quad_one, *quad_two],
            [VMEM] * 16,
            5,
            made,
        )

        def reduce(v):
            total = lax.psum_scatter(v, "fsdp", scatter_dimension=0, tiled=True)
            return lax.psum(total, "rep").astype(f32)

        total = reduce(both_grads[0])
        inner_sum, outer_sum = total[:, :hidden], total[:, hidden:]
        low, high = reduce(one_grads[0]), reduce(two_grads[0])
        output_sum = low[:, :width]
        sums = [v.reshape(part, 5, quad) for v in (low[:, width:], high)]
        q_sum, k_sum, v_sum, m_low, m_high = (
            jnp.concatenate([v[:, i] for v in sums], axis=1) for i in range(5)
        )
        m_sum = jnp.concatenate([m_low, m_high], axis=1)
        vec_sum = lax.psum(vec_grads, ("rep", "fsdp"))
        rank = lax.axis_index("fsdp")
        own = lax.dynamic_slice(vec_sum[:8], (0, rank * part), (8, part))
        own_inner = lax.dynamic_slice(
            vec_sum[8:12].reshape(-1), (rank * inner_part,), (inner_part,)
        )
    return (
        output,
        grad_frames,
        grad_bank,
        jnp.swapaxes(grad_ck, 0, 1),
        jnp.swapaxes(grad_cv, 0, 1),
        own[0],
        own[1],
        q_sum,
        own[2],
        k_sum,
        v_sum,
        own[3],
        m_sum,
        output_sum.T,
        own[4],
        own[5],
        own[6],
        inner_sum,
        own_inner,
        outer_sum.T,
        own[7],
    )


def without_gates(kernel, n_args, n_gates, *refs):
    kernel(*refs[:n_args], *refs[n_args + n_gates :])


def gated(kernel, out_shapes, out_specs, scratch, args, specs, micros, made, carried=()):
    return call(
        functools.partial(without_gates, kernel, len(args), len(made)),
        out_shapes,
        out_specs,
        scratch,
        [*args, *made],
        [*specs, *[ANY] * len(made)],
        micros,
        carried=carried,
    )


def solution(mesh):
    both = ("rep", "fsdp")
    rows, vector = P("fsdp", None), P("fsdp")
    columns = P(None, "fsdp")
    weights = (
        vector,
        vector,
        rows,
        vector,
        rows,
        rows,
        vector,
        rows,
        columns,
        vector,
        vector,
        vector,
        rows,
        vector,
        columns,
        vector,
    )
    blocks = P(both, None, None)
    in_specs = (P(both, None), blocks, blocks, blocks, P(both, None), *weights)
    out_specs = (P(both, None), P(both, None), blocks, blocks, blocks, *weights)
    ring = mesh.shape["fsdp"] == 16 and mesh.shape["rep"] == 2
    return jax.shard_map(
        functools.partial(per_device, ring),
        mesh=mesh,
        in_specs=in_specs,
        out_specs=out_specs,
        check_vma=False,
    )
```
